32 devices in a mesh: dp: 4 (over x, core), seq: 8 (over z, y).
Axes of the slice: x: 2, y: 2, z: 4, core: 2. Of those that a mesh axis runs over, the one named last changes fastest.
Arguments:
- tokens: bfloat16 [4, 1024, 2048], P('dp', 'seq'), may hold values from -6 to 6
- segment_ids: int32 [4, 1024], P('dp', 'seq'), may hold values from 0 to 4, as said below
- gain_attn: bfloat16 [2048], P(('dp', 'seq')), may hold values from 0.25 to 1.75
- w_query: bfloat16 [2048, 2048], P(('dp', 'seq')), may hold values from -0.125 to 0.125
- w_key: bfloat16 [2048, 256], P(('dp', 'seq')), may hold values from -0.125 to 0.125
- w_value: bfloat16 [2048, 256], P(('dp', 'seq')), may hold values from -0.125 to 0.125
- w_output: bfloat16 [2048, 2048], P(('dp', 'seq')), may hold values from -2 to 2
- gain_mlp: bfloat16 [2048], P(('dp', 'seq')), may hold values from 0.25 to 1.75
- w_gate: bfloat16 [2048, 5632], P(('dp', 'seq')), may hold values from -0.125 to 0.125
- w_up: bfloat16 [2048, 5632], P(('dp', 'seq')), may hold values from -0.125 to 0.125
- w_down: bfloat16 [5632, 2048], P(('dp', 'seq')), may hold values from -0.078125 to 0.078125
- cotangent: bfloat16 [4, 1024, 2048], P('dp', 'seq'), may hold values from -6 to 6
Outputs:
- out_tokens: bfloat16 [4, 1024, 2048], P('dp', 'seq')
- grad_tokens: float32 [4, 1024, 2048], P('dp', 'seq')
- grad_gain_attn: float32 [2048], P(('dp', 'seq'))
- grad_query: float32 [2048, 2048], P(('dp', 'seq'))
- grad_key: float32 [2048, 256], P(('dp', 'seq'))
- grad_value: float32 [2048, 256], P(('dp', 'seq'))
- grad_output: float32 [2048, 2048], P(('dp', 'seq'))
- grad_gain_mlp: float32 [2048], P(('dp', 'seq'))
- grad_gate: float32 [2048, 5632], P(('dp', 'seq'))
- grad_up: float32 [2048, 5632], P(('dp', 'seq'))
- grad_down: float32 [5632, 2048], P(('dp', 'seq'))
The draws below stay inside these ranges and needn't reach their ends.
Inputs may be any that keep to these rules, and one draw needn't show every extreme that they name: `segment_ids`: ids never fall along a row; in each row one document starts within the first 128 positions and ends within the last 128.
All inputs are finite; a program needn't handle non-finite values.
Results may differ from the reference program's by a relative error of at most 0.015.
Values may be sent and summed in bfloat16 or wider, within the bound.
A program may use at most 384 MiB of HBM per device.

```python
import math
import jax
import jax.numpy as jnp
from jax import lax

D = 2048
HEADS = 32
HEAD_DIM = 64
KV_HEADS = 4
FF = 5632
TOK_DEV = 128
KVD = 256
LEN = 1024
ROWS = 4


def draw_segment_ids(key, part):
    key = jax.random.fold_in(key, 11)
    keys = jax.random.split(key, 4)
    begin = jax.random.randint(keys[0], (ROWS, 1), 1, TOK_DEV)
    finish = LEN - jax.random.randint(keys[1], (ROWS, 1), 1, TOK_DEV)
    early = jax.random.randint(keys[2], (ROWS, 1), 1, begin + 1)
    late = jax.random.randint(keys[3], (ROWS, 1), finish, LEN)
    places = jnp.arange(LEN, dtype=jnp.int32)[None, :]
    total = (places >= early).astype(jnp.int32) + (places >= begin).astype(jnp.int32)
    total = total + (places >= finish).astype(jnp.int32) + (places >= late).astype(jnp.int32)
    return total


def block_scale(rng, extent, cuts, smallest, high):
    level, own = 1.0, jax.random.fold_in(rng, 6)
    for axis_at, parts in cuts:
        steps = jnp.exp(jax.random.uniform(jax.random.fold_in(own, axis_at), (parts,), jnp.float32, smallest / len(cuts), high / len(cuts)))
        level = level * jnp.repeat(steps, extent[axis_at] // parts).reshape([-1 if axis == axis_at else 1 for axis in range(len(extent))])
    return level


def centred(own_key, dims, scale, bound, cuts=(), kind=jnp.bfloat16):
    loudness = block_scale(own_key, dims, cuts, -0.22, 0.18) if cuts else 1.0
    values = jax.random.normal(own_key, dims, jnp.float32) * scale * loudness
    return jnp.minimum(jnp.maximum(values, -bound), bound).astype(kind)


def setup_inputs(seed: int = 0) -> dict:
    splits = jax.random.split(jax.random.key(seed), 13)
    return {
        "tokens": centred(splits[0], (ROWS, LEN, D), 1.0, 6.0, ((0, 4), (1, 8))),
        "segment_ids": draw_segment_ids(jax.random.fold_in(splits[12], 71), 0),
        "gain_attn": jnp.clip(1.0 + 0.15 * jax.random.normal(splits[2], (D,), jnp.float32), 0.25, 1.75).astype(jnp.bfloat16),
        "w_query": centred(splits[3], (D, D), D ** -0.5, 0.125, ((0, 32),)),
        "w_key": centred(splits[4], (D, KVD), D ** -0.5, 0.125, ((0, 32),)),
        "w_value": centred(splits[5], (D, KVD), D ** -0.5, 0.125, ((0, 32),)),
        "w_output": centred(splits[6], (D, D), (max(D // 256, 1)) ** -0.5, 2.0, ((0, 32),)),
        "gain_mlp": jnp.clip(1.0 + 0.15 * jax.random.normal(splits[7], (D,), jnp.float32), 0.25, 1.75).astype(jnp.bfloat16),
        "w_gate": centred(splits[8], (D, FF), D ** -0.5, 0.125, ((0, 32),)),
        "w_up": centred(splits[9], (D, FF), D ** -0.5, 0.125, ((0, 32),)),
        "w_down": centred(splits[10], (FF, D), FF ** -0.5, 0.078125, ((0, 32),)),
        "cotangent": centred(splits[11], (ROWS, LEN, D), 1.0, 6.0, ((0, 4), (1, 8))),
    }


EPS = 1e-05
ROPE_BASE = 10000.0
MASK_VALUE = -1e+30

@jax.custom_vjp
def low(v):
    return lax.optimization_barrier(v.astype(jnp.bfloat16)).astype(jnp.float32)

@jax.custom_vjp
def low_back(v):
    return v

def low_keep(v):
    return (low(v), None)

def low_pass(kept, grad):
    return (grad,)

def back_keep(v):
    return (v, None)

def back_low(kept, grad):
    return (low(grad),)
low.defvjp(low_keep, low_pass)
low_back.defvjp(back_keep, back_low)

def product(left, right):
    return jnp.dot(left, right, precision=lax.Precision.HIGHEST)

def angles(positions):
    freqs = ROPE_BASE ** (-jnp.arange(0, HEAD_DIM, 2).astype(jnp.float32) / HEAD_DIM)
    turned = positions.astype(jnp.float32)[:, None] * freqs[None, :]
    return (jnp.cos(turned)[:, None, :], jnp.sin(turned)[:, None, :])

def rotate(values, cosines, sines):
    half = values.shape[-1] // 2
    first = values[..., :half]
    second = values[..., half:]
    return jnp.concatenate([first * cosines - second * sines, second * cosines + first * sines], -1)

def row_positions(segments):
    index = jnp.arange(segments.shape[0], dtype=jnp.int32)
    fresh = jnp.concatenate([jnp.ones((1,), dtype=jnp.bool_), segments[1:] != segments[:-1]])
    starts = lax.cummax(jnp.where(fresh, index, jnp.zeros_like(index)), axis=0)
    return index - starts

def row_forward(weights, items):
    inputs, segments, places = items
    attn_gain, query_w, key_w, value_w, output_w, mlp_gain, gate_w, up_w, down_w = weights
    group = HEADS // KV_HEADS
    factor = HEAD_DIM ** (-0.5)
    norm_one = inputs * lax.rsqrt(lax.optimization_barrier(jnp.mean(inputs * inputs, -1, keepdims=True)) + EPS)
    normed = low(norm_one * attn_gain)
    cosines, sines = angles(places)
    query_pre = low_back(product(normed, query_w))
    key_pre = low_back(product(normed, key_w))
    values = low(low_back(product(normed, value_w))).reshape(LEN, KV_HEADS, HEAD_DIM)
    queries = low(rotate(query_pre.reshape(LEN, HEADS, HEAD_DIM), cosines, sines) * factor)
    queries = queries.reshape(LEN, KV_HEADS, group, HEAD_DIM)
    keys = low(rotate(key_pre.reshape(LEN, KV_HEADS, HEAD_DIM), cosines, sines))
    block = math.gcd(LEN, 512)
    count = LEN // block
    index = jnp.arange(LEN, dtype=jnp.int32)

    def attend(pieces):
        query_block, query_segs, query_index = pieces
        raw = low_back(jnp.einsum('qgrd,kgd->grqk', query_block, keys, precision=lax.Precision.HIGHEST))
        allowed = (segments[None, :] == query_segs[:, None]) & (index[None, :] <= query_index[:, None])
        masked = jnp.where(allowed, raw, MASK_VALUE)
        total = jax.nn.logsumexp(masked, -1, keepdims=True)
        probs = low(jnp.where(allowed, jnp.exp(raw - total), 0.0))
        return jnp.einsum('grqk,kgd->qgrd', probs, values, precision=lax.Precision.HIGHEST)
    attended = lax.map(jax.checkpoint(attend), (queries.reshape(count, block, KV_HEADS, group, HEAD_DIM), segments.reshape(count, block), index.reshape(count, block)))
    attended = low(low_back(attended.reshape(LEN, D)))
    middle = inputs + low_back(product(attended, output_w))
    norm_two = middle * lax.rsqrt(lax.optimization_barrier(jnp.mean(middle * middle, -1, keepdims=True)) + EPS)
    second = low(norm_two * mlp_gain)
    gate = low_back(product(second, gate_w))
    upward = low_back(product(second, up_w))
    hidden = low(jax.nn.silu(gate) * upward)
    return middle + product(hidden, down_w)

def reference(tokens, segment_ids, gain_attn, w_query, w_key, w_value, w_output, gain_mlp, w_gate, w_up, w_down, cotangent):
    positions = jax.vmap(row_positions)(segment_ids)
    params = tuple((weight.astype(jnp.float32) for weight in (gain_attn, w_query, w_key, w_value, w_output, gain_mlp, w_gate, w_up, w_down)))

    def forward(inputs, *weights):

        def one_row(items):
            return row_forward(weights, items)
        return lax.map(jax.checkpoint(one_row), (inputs, segment_ids, positions))
    output, pull = jax.vjp(forward, tokens.astype(jnp.float32), *params)
    grads = pull(cotangent.astype(jnp.float32))
    return (output.astype(jnp.bfloat16), grads[0], grads[1], grads[2], grads[3], grads[4], grads[5], grads[6], grads[7], grads[8], grads[9])
```

```python
import functools

import jax
import jax.numpy as jnp
from jax import lax
from jax.experimental import pallas as pl
from jax.experimental.pallas import tpu as pltpu
from jax.sharding import PartitionSpec as P

HEADS = 32
HEAD_DIM = 64
KV_HEADS = 4
GROUP = HEADS // KV_HEADS

EPS = 1e-05
ROPE_BASE = 10000.0
MASK_VALUE = -1e30
MESH = pl.DeviceIdType.MESH
LOW = jnp.bfloat16
FULL = jnp.float32
VMEM_BYTES = 56 * 1024 * 1024


def matmul(left, right):
    return jnp.dot(left, right, preferred_element_type=FULL)


def matmul_nt(left, right):
    return lax.dot_general(left, right, (((1,), (1,)), ((), ())), preferred_element_type=FULL)


def matmul_tn(left, right):
    return lax.dot_general(left, right, (((0,), (0,)), ((), ())), preferred_element_type=FULL)


def ring_at(place, n):
    upper = lax.div(place, n // 2)
    return (1 - upper) * 2 * place + upper * (2 * (n - place) - 1)


def ring_place(index, n):
    odd = lax.rem(index, 2)
    return (1 - odd) * lax.div(index, 2) + odd * (n - lax.div(index + 1, 2))


class Where:
    def __init__(self, n_dp, n_seq):
        self.n_dp, self.n_seq = n_dp, n_seq
        self.chips = n_dp // 2
        self.dp = lax.axis_index("dp")
        self.seq = lax.axis_index("seq")
        self.core = lax.rem(self.dp, 2)
        self.chip = lax.div(self.dp, 2)
        self.place = ring_place(self.seq, n_seq)

    def ring(self, step):
        return ring_at(lax.rem(self.place + step + self.n_seq, self.n_seq), self.n_seq)

    def ring_ids(self):
        return [(self.dp, self.ring(1)), (self.dp, self.ring(-1))]

    def seq_ids(self):
        return [
            (self.dp, lax.rem(self.seq + k, self.n_seq)) for k in range(1, self.n_seq)
        ]

    def core_id(self):
        return (self.dp + 1 - 2 * self.core, self.seq)

    def chip_ids(self):
        return [
            (2 * lax.rem(self.chip + k, self.chips) + self.core, self.seq)
            for k in range(1, self.chips)
        ]


def greet(ids):
    barrier = pltpu.get_barrier_semaphore()
    for one in ids:
        pl.semaphore_signal(barrier, inc=1, device_id=one, device_id_type=MESH)
    pl.semaphore_wait(barrier, len(ids))


def remote(src, dst, send, recv, target):
    return pltpu.make_async_remote_copy(
        src_ref=src,
        dst_ref=dst,
        send_sem=send,
        recv_sem=recv,
        device_id=target,
        device_id_type=MESH,
    )


class RingGather:
    def __init__(self, at, own, everything, send, recv, local):
        self.at, self.own, self.everything = at, own, everything
        self.send, self.recv = send, recv
        self.steps = at.n_seq // 2
        self.half = own.shape[0] // 2
        self.copies = {}
        self.kept = pltpu.make_async_copy(own, everything.at[at.seq], local)

    @staticmethod
    def scratch(n_seq):
        shape = (2, n_seq // 2, 2)
        return [pltpu.SemaphoreType.DMA(shape), pltpu.SemaphoreType.DMA(shape)]

    def step(self, t):
        at = self.at
        if t == 0:
            self.kept.start()
        for h in (0, 1):
            for d in (0, 1):
                if t == self.steps - 1 and h != d:
                    continue
                if t > 0:
                    self.copies[(d, t - 1, h)].wait_recv()
                origin = at.ring(-t if d == 0 else t)
                rows = pl.ds(h * self.half, self.half)
                dst = self.everything.at[origin, rows]
                src = self.own.at[rows] if t == 0 else dst
                copy = remote(
                    src, dst, self.send.at[d, t, h], self.recv.at[d, t, h], at.ring_ids()[d]
                )
                copy.start()
                self.copies[(d, t, h)] = copy

    def finish(self):
        last = self.steps - 1
        for (d, t, h), copy in self.copies.items():
            if t == last or (t == last - 1 and h != d):
                copy.wait_recv()
        for copy in self.copies.values():
            copy.wait_send()
        self.kept.wait()


class RingScatter:
    def __init__(self, at, parts, slots, send, recv):
        self.at, self.parts, self.slots = at, parts, slots
        self.send, self.recv = send, recv
        self.steps = at.n_seq // 2
        self.half = parts.shape[1] // 2
        self.copies = {}

    @staticmethod
    def scratch(n_seq, rows, columns):
        shape = (2, n_seq // 2, 2)
        return [
            pltpu.VMEM((2, n_seq // 2, rows, columns), LOW),
            pltpu.SemaphoreType.DMA(shape),
            pltpu.SemaphoreType.DMA(shape),
        ]

    def step(self, t):
        at = self.at
        for h in (0, 1):
            for d in (0, 1):
                if t == 0 and h != d:
                    continue
                there = at.ring(self.steps - t if d == 0 else t - self.steps)
                rows = pl.ds(h * self.half, self.half)
                src = self.parts.at[there, rows]
                if t > 1 or (t == 1 and h == d):
                    self.copies[(d, t - 1, h)].wait_recv()
                    held = self.slots.at[d, t - 1, rows]
                    held[...] = (held[...].astype(FULL) + src[...].astype(FULL)).astype(LOW)
                    src = held
                copy = remote(
                    src,
                    self.slots.at[d, t, rows],
                    self.send.at[d, t, h],
                    self.recv.at[d, t, h],
                    at.ring_ids()[d],
                )
                copy.start()
                self.copies[(d, t, h)] = copy

    def finish(self, out):
        last = self.steps - 1
        for h in (0, 1):
            rows = pl.ds(h * self.half, self.half)
            total = self.parts[self.at.seq, rows].astype(FULL)
            for d in (0, 1):
                if last == 0 and h != d:
                    continue
                self.copies[(d, last, h)].wait_recv()
                total = total + self.slots[d, last, rows].astype(FULL)
            out[rows] = total
        for copy in self.copies.values():
            copy.wait_send()


class SeqExchange:
    def __init__(self, at, packed, landing, send, recv, local):
        self.kept = pltpu.make_async_copy(packed.at[at.seq], landing.at[at.seq], local)
        self.copies = [
            remote(packed.at[one[1]], landing.at[at.seq], send.at[k], recv.at[k], one)
            for k, one in enumerate(at.seq_ids())
        ]

    @staticmethod
    def scratch(n_seq):
        return [pltpu.SemaphoreType.DMA((n_seq - 1,)), pltpu.SemaphoreType.DMA((n_seq - 1,))]

    def start(self):
        self.kept.start()
        for copy in self.copies:
            copy.start()

    def arrived(self):
        self.kept.wait()
        for copy in self.copies:
            copy.wait_recv()

    def finish(self):
        for copy in self.copies:
            copy.wait_send()


class DpGather:
    def __init__(self, at, everything, send, recv):
        self.at, self.everything, self.send, self.recv = at, everything, send, recv
        own = everything.at[at.dp]
        self.out = [
            remote(own, own, send.at[k], recv.at[k], one) for k, one in enumerate(at.chip_ids())
        ]
        base = at.chips - 1
        self.mate = remote(own, own, send.at[base], recv.at[base], at.core_id())
        self.handed = []
        for k in range(1, at.chips):
            origin = 2 * lax.rem(at.chip + at.chips - k, at.chips) + at.core
            there = everything.at[origin]
            self.handed.append(
                remote(there, there, send.at[base + k], recv.at[base + k], at.core_id())
            )

    @staticmethod
    def scratch(n_dp):
        return [pltpu.SemaphoreType.DMA((n_dp - 1,)), pltpu.SemaphoreType.DMA((n_dp - 1,))]

    def start(self):
        for copy in self.out:
            copy.start()
        self.mate.start()

    def hand(self):
        for copy, onward in zip(self.out, self.handed):
            copy.wait_recv()
            onward.start()

    def finish(self):
        self.mate.wait_recv()
        for copy in self.handed:
            copy.wait_recv()
        for copy in self.out + [self.mate] + self.handed:
            copy.wait_send()


def add_rows(rows, chunk, one):
    def step(r, carry):
        one(pl.ds(pl.multiple_of(r * chunk, chunk), chunk))
        return carry

    lax.fori_loop(0, rows // chunk, step, 0)


def chunk_of(rows, columns):
    chunk = rows
    while chunk % 32 == 0 and chunk * columns > 65536:
        chunk //= 2
    return chunk


class DpScatter:
    def __init__(self, at, parts, core, other, send, recv):
        self.at, self.parts, self.core, self.other = at, parts, core, other
        self.send, self.recv = send, recv
        self.rows, self.columns = parts.shape[1], parts.shape[2]

    @staticmethod
    def scratch(n_dp, rows, columns):
        chips = n_dp // 2
        return [
            pltpu.VMEM((chips, rows, columns), LOW),
            pltpu.VMEM((max(chips - 1, 1), rows, columns), LOW),
            pltpu.SemaphoreType.DMA((2 * chips - 1,)),
            pltpu.SemaphoreType.DMA((2 * chips - 1,)),
        ]

    def to_core(self, k):
        at = self.at
        return remote(
            self.parts.at[2 * k + 1 - at.core],
            self.core.at[k],
            self.send.at[k],
            self.recv.at[k],
            at.core_id(),
        )

    def to_chip(self, k):
        at = self.at
        sem = at.chips + k - 1
        return remote(
            self.core.at[lax.rem(at.chip + k, at.chips)],
            self.other.at[k - 1],
            self.send.at[sem],
            self.recv.at[sem],
            at.chip_ids()[k - 1],
        )

    def start(self):
        for k in range(self.at.chips):
            self.to_core(k).start()

    def add_core(self, k):
        held = self.core.at[k]
        mine = self.parts.at[2 * k + self.at.core]

        def one(rows):
            held[rows] = (held[rows].astype(FULL) + mine[rows].astype(FULL)).astype(LOW)

        add_rows(self.rows, chunk_of(self.rows, self.columns), one)

    def across(self):
        at = self.at
        for k in range(1, at.chips):
            there = lax.rem(at.chip + k, at.chips)
            self.to_core(there).wait_recv()
            self.add_core(there)
            self.to_chip(k).start()

    def finish(self, out):
        at = self.at
        self.to_core(at.chip).wait_recv()
        for k in range(1, at.chips):
            self.to_chip(k).wait_recv()
        held = self.core.at[at.chip]
        mine = self.parts.at[2 * at.chip + at.core]

        def one(rows):
            total = held[rows].astype(FULL) + mine[rows].astype(FULL)
            for k in range(1, at.chips):
                total = total + self.other[k - 1, rows].astype(FULL)
            out[rows] = total.astype(out.dtype)

        add_rows(self.rows, chunk_of(self.rows, self.columns), one)
        for k in range(at.chips):
            self.to_core(k).wait_send()
        for k in range(1, at.chips):
            self.to_chip(k).wait_send()


def comm_params(number):
    return pltpu.CompilerParams(
        collective_id=number, has_side_effects=True, vmem_limit_bytes=VMEM_BYTES
    )


ANY = pl.BlockSpec(memory_space=pl.ANY)
VMEM = pl.BlockSpec(memory_space=pltpu.VMEM)


def shape_of(dims, kind):
    return jax.ShapeDtypeStruct(dims, kind)


def spread_kernel(
    n_dp, n_seq, x, dy, seg, pq, pgu, wd, wo,
    x_all, dy_all, seg_all, q_all, gu_all, wd_all, wo_all,
    local, seg_s, seg_r, pq_s, pq_r, pgu_s, pgu_r, x_s, x_r, dy_s, dy_r,
    gq_s, gq_r, ggu_s, ggu_r, gd_s, gd_r, go_s, go_r,
):
    at = Where(n_dp, n_seq)
    greet(at.seq_ids() + [at.core_id()] + at.chip_ids())
    put_d = pltpu.make_async_copy(wd, wd_all.at[at.dp], local.at[0])
    put_o = pltpu.make_async_copy(wo, wo_all.at[at.dp], local.at[1])
    put_d.start()
    put_o.start()
    swap_q = SeqExchange(at, pq, q_all.at[at.dp], pq_s, pq_r, local.at[2])
    swap_seg = SeqExchange(at, seg, seg_all, seg_s, seg_r, local.at[3])
    swap_gu = SeqExchange(at, pgu, gu_all.at[at.dp], pgu_s, pgu_r, local.at[4])
    ring_x = RingGather(at, x, x_all, x_s, x_r, local.at[5])
    ring_dy = RingGather(at, dy, dy_all, dy_s, dy_r, local.at[6])
    dp_q = DpGather(at, q_all, gq_s, gq_r)
    dp_gu = DpGather(at, gu_all, ggu_s, ggu_r)
    dp_d = DpGather(at, wd_all, gd_s, gd_r)
    dp_o = DpGather(at, wo_all, go_s, go_r)
    swap_q.start()
    swap_seg.start()
    ring_x.step(0)
    put_o.wait()
    dp_o.start()
    put_d.wait()
    dp_d.start()
    swap_gu.start()
    swap_q.arrived()
    dp_q.start()
    for t in range(1, ring_x.steps):
        ring_x.step(t)
    dp_o.hand()
    dp_q.hand()
    dp_d.hand()
    ring_dy.step(0)
    swap_gu.arrived()
    dp_gu.start()
    for t in range(1, ring_dy.steps):
        ring_dy.step(t)
    dp_gu.hand()
    for one in (ring_x, swap_q, swap_seg, dp_o, dp_d, dp_q, swap_gu, ring_dy, dp_gu):
        if one is swap_seg:
            one.arrived()
        one.finish()


def spread(n_dp, n_seq, x, dy, seg, pq, pgu, wd, wo):
    scratch = [pltpu.SemaphoreType.DMA((7,))]
    for _ in range(3):
        scratch += SeqExchange.scratch(n_seq)
    for _ in range(2):
        scratch += RingGather.scratch(n_seq)
    for _ in range(4):
        scratch += DpGather.scratch(n_dp)
    return pl.pallas_call(
        functools.partial(spread_kernel, n_dp, n_seq),
        name="spread_inputs",
        out_shape=[
            shape_of((n_seq,) + x.shape, x.dtype),
            shape_of((n_seq,) + dy.shape, dy.dtype),
            shape_of(seg.shape, seg.dtype),
            shape_of((n_dp,) + pq.shape, LOW),
            shape_of((n_dp,) + pgu.shape, LOW),
            shape_of((n_dp,) + wd.shape, LOW),
            shape_of((n_dp,) + wo.shape, LOW),
        ],
        in_specs=[ANY] * 7,
        out_specs=[ANY] * 7,
        scratch_shapes=scratch,
        compiler_params=comm_params(1),
    )(x, dy, seg, pq, pgu, wd, wo)


def gather_kernel(n_dp, n_seq, own, everything, local, send, recv):
    at = Where(n_dp, n_seq)
    greet(at.ring_ids())
    ring = RingGather(at, own, everything, send, recv, local.at[0])
    for t in range(ring.steps):
        ring.step(t)
    ring.finish()


def gather(n_dp, n_seq, number, own):
    return pl.pallas_call(
        functools.partial(gather_kernel, n_dp, n_seq),
        name="ring_gather",
        out_shape=shape_of((n_seq,) + own.shape, own.dtype),
        in_specs=[ANY],
        out_specs=ANY,
        scratch_shapes=[pltpu.SemaphoreType.DMA((1,))] + RingGather.scratch(n_seq),
        compiler_params=comm_params(number),
    )(own)


def scatter_kernel(n_dp, n_seq, parts, out, slots, send, recv):
    at = Where(n_dp, n_seq)
    greet(at.ring_ids())
    ring = RingScatter(at, parts, slots, send, recv)
    for t in range(ring.steps):
        ring.step(t)
    ring.finish(out)


def scatter(n_dp, n_seq, number, parts):
    return pl.pallas_call(
        functools.partial(scatter_kernel, n_dp, n_seq),
        name="ring_scatter",
        out_shape=shape_of(parts.shape[1:], FULL),
        in_specs=[VMEM],
        out_specs=VMEM,
        scratch_shapes=RingScatter.scratch(n_seq, *parts.shape[1:]),
        compiler_params=comm_params(number),
    )(parts)


def reduce_kernel(
    n_dp, n_seq, cols, rows, got, total, total_v,
    c_core, c_other, c_s, c_r, r_core, r_other, r_s, r_r, fin, a_s, a_r, local,
):
    at = Where(n_dp, n_seq)
    greet(at.seq_ids() + [at.core_id()] + at.chip_ids())
    down = DpScatter(at, rows, r_core, r_other, r_s, r_r)
    side = DpScatter(at, cols, c_core, c_other, c_s, c_r)
    side.start()
    down.start()
    side.across()
    down.across()
    side.finish(fin)
    n, width = got.shape[1], got.shape[2]
    copies = []
    kept = pltpu.make_async_copy(
        fin.at[pl.ds(pl.multiple_of(at.seq * n, n), n)], got.at[at.seq], local.at[0]
    )
    kept.start()
    for k, one in enumerate(at.seq_ids()):
        src = fin.at[pl.ds(pl.multiple_of(one[1] * n, n), n)]
        copy = remote(src, got.at[at.seq], a_s.at[k], a_r.at[k], one)
        copy.start()
        copies.append(copy)
    down.finish(total_v)
    store = pltpu.make_async_copy(total_v, total, local.at[1])
    store.start()
    for copy in copies:
        copy.wait()
    kept.wait()
    store.wait()


def reduce(n_dp, n_seq, number, cols, rows, kind):
    _, deep, wide = cols.shape
    return pl.pallas_call(
        functools.partial(reduce_kernel, n_dp, n_seq),
        name="reduce_grads",
        out_shape=[
            shape_of((n_seq, deep // n_seq, wide), LOW),
            shape_of(rows.shape[1:], kind),
        ],
        in_specs=[VMEM, VMEM],
        out_specs=[ANY, ANY],
        scratch_shapes=[pltpu.VMEM(rows.shape[1:], kind)]
        + DpScatter.scratch(n_dp, deep, wide)
        + DpScatter.scratch(n_dp, *rows.shape[1:])
        + [pltpu.VMEM((deep, wide), LOW)]
        + SeqExchange.scratch(n_seq)
        + [pltpu.SemaphoreType.DMA((2,))],
        compiler_params=comm_params(number),
    )(cols, rows)


def allowed_at(start_ref, begin, count, stop):
    query = lax.broadcasted_iota(jnp.int32, (count, stop), 0) + begin
    key = lax.broadcasted_iota(jnp.int32, (count, stop), 1)
    return (key <= query) & (key >= start_ref[begin : begin + count])


def attend_kernel(block, start_ref, q_ref, k_ref, v_ref, o_ref, lse_ref):
    for begin in range(0, q_ref.shape[1], block):
        stop = begin + block
        allowed = allowed_at(start_ref, begin, block, stop)
        raw = matmul_nt(q_ref[0, begin:stop], k_ref[0, :stop])
        raw = jnp.where(allowed, raw, MASK_VALUE)
        top = jnp.max(raw, -1, keepdims=True)
        probs = jnp.where(allowed, jnp.exp(raw - top), 0.0)
        total = jnp.sum(probs, -1, keepdims=True)
        probs = (probs * (1.0 / total)).astype(LOW)
        o_ref[0, begin:stop] = matmul(probs, v_ref[0, :stop]).astype(LOW)
        lse_ref[0, begin:stop] = top + jnp.log(total)


def attend(starts, queries, keys, values):
    heads, length, dim = queries.shape
    block = min(256, length)
    per_kv = heads // keys.shape[0]
    one = pl.BlockSpec((1, length, dim), lambda h: (h, 0, 0))
    shared = pl.BlockSpec((1, length, dim), lambda h: (h // per_kv, 0, 0))
    stat = pl.BlockSpec((1, length, 1), lambda h: (h, 0, 0))
    return pl.pallas_call(
        functools.partial(attend_kernel, block),
        name="attend",
        grid=(heads,),
        out_shape=[
            shape_of((heads, length, dim), LOW),
            shape_of((heads, length, 1), FULL),
        ],
        in_specs=[pl.BlockSpec((length, 1), lambda h: (0, 0)), one, shared, shared],
        out_specs=[one, stat],
        compiler_params=pltpu.CompilerParams(vmem_limit_bytes=VMEM_BYTES),
    )(starts, queries, keys, values)


def attend_back_kernel(
    block, per_kv, start_ref, q_ref, k_ref, v_ref, do_ref, lse_ref, dq_ref, dk_ref, dv_ref
):
    @pl.when(lax.rem(pl.program_id(0), per_kv) == 0)
    def _():
        dk_ref[...] = jnp.zeros_like(dk_ref)
        dv_ref[...] = jnp.zeros_like(dv_ref)

    for begin in range(0, q_ref.shape[1], block):
        stop = begin + block
        allowed = allowed_at(start_ref, begin, block, stop)
        q = q_ref[0, begin:stop]
        do = do_ref[0, begin:stop]
        k = k_ref[0, :stop]
        raw = matmul_nt(q, k)
        probs = jnp.where(allowed, jnp.exp(raw - lse_ref[0, begin:stop]), 0.0)
        grad_probs = matmul_nt(do, v_ref[0, :stop])
        delta = jnp.sum(probs * grad_probs, -1, keepdims=True)
        grad_raw = (probs * (grad_probs - delta)).astype(LOW)
        dq_ref[0, begin:stop] = matmul(grad_raw, k)
        dk_ref[0, :stop] += matmul_tn(grad_raw, q)
        dv_ref[0, :stop] += matmul_tn(probs.astype(LOW), do)


def attend_back(starts, queries, keys, values, grads, lse):
    heads, length, dim = queries.shape
    block = min(256, length)
    per_kv = heads // keys.shape[0]
    one = pl.BlockSpec((1, length, dim), lambda h: (h, 0, 0))
    shared = pl.BlockSpec((1, length, dim), lambda h: (h // per_kv, 0, 0))
    stat = pl.BlockSpec((1, length, 1), lambda h: (h, 0, 0))
    return pl.pallas_call(
        functools.partial(attend_back_kernel, block, per_kv),
        name="attend_back",
        grid=(heads,),
        out_shape=[
            shape_of((heads, length, dim), FULL),
            shape_of(keys.shape, FULL),
            shape_of(keys.shape, FULL),
        ],
        in_specs=[pl.BlockSpec((length, 1), lambda h: (0, 0)), one, shared, shared, one, stat],
        out_specs=[one, shared, shared],
        compiler_params=pltpu.CompilerParams(vmem_limit_bytes=VMEM_BYTES),
    )(starts, queries, keys, values, grads, lse)


def rotate(values, cosines, sines):
    half = values.shape[-1] // 2
    first = values[..., :half]
    second = values[..., half:]
    return jnp.concatenate([first * cosines - second * sines, second * cosines + first * sines], -1)


def norm_back(grad_normed, normed, scale):
    return scale * (grad_normed - normed * jnp.mean(grad_normed * normed, -1, keepdims=True))


def body(
    n_dp,
    n_seq,
    tokens,
    segment_ids,
    gain_attn,
    w_query,
    w_key,
    w_value,
    w_output,
    gain_mlp,
    w_gate,
    w_up,
    w_down,
    cotangent,
):
    local, width = tokens.shape[1], tokens.shape[2]
    length = n_seq * local
    own_rows = w_query.shape[0]
    own_ff = w_down.shape[0]
    part_ff = n_dp * own_ff
    heads = HEADS // n_seq
    q_width = heads * HEAD_DIM
    kv_heads = max(heads // GROUP, 1)
    kv_width = kv_heads * HEAD_DIM
    factor = HEAD_DIM ** (-0.5)
    dtype = tokens.dtype
    x_own = tokens.reshape(local, width)
    dy_own = cotangent.reshape(local, width)

    gain_one = gain_attn.astype(FULL)[:, None]
    gain_two = gain_mlp.astype(FULL)[:, None]

    def gained(gain, weight):
        return (gain * weight.astype(FULL)).astype(LOW)

    def for_kv(weight):
        return jnp.stack(
            [
                weight[:, first * HEAD_DIM : first * HEAD_DIM + kv_width]
                for first in [s * heads // GROUP for s in range(n_seq)]
            ]
        )

    pack_q = jnp.concatenate(
        [
            gained(gain_one, w_query).reshape(own_rows, n_seq, q_width).transpose(1, 0, 2),
            for_kv(gained(gain_one, w_key)),
            for_kv(gained(gain_one, w_value)),
        ],
        -1,
    )

    def ff_split(weight):
        return (
            weight.reshape(own_rows, n_dp, n_seq, own_ff)
            .transpose(2, 0, 1, 3)
            .reshape(n_seq, own_rows, part_ff)
        )

    pack_gu = jnp.concatenate(
        [ff_split(gained(gain_two, w_gate)), ff_split(gained(gain_two, w_up))], -1
    )
    there = [(l, (l % n_dp) * n_seq + l // n_dp) for l in range(n_dp * n_seq)]
    back = [(b, a) for a, b in there]
    wo_block = lax.ppermute(w_output, ("dp", "seq"), there)
    seg_block = jnp.broadcast_to(
        segment_ids.reshape(1, 1, local), (n_seq, 8, local)
    )
    down_block = w_down if own_ff % 16 == 0 else w_down.reshape(16, own_ff * width // 16)

    x_all, dy_all, seg_all, q_all, gu_all, wd_all, wo_all = spread(
        n_dp, n_seq, x_own, dy_own, seg_block, pack_q, pack_gu, down_block, wo_block
    )
    inputs = x_all.reshape(length, width).astype(FULL)
    dy = dy_all.reshape(length, width)
    weight_q = q_all.reshape(width, q_width + 2 * kv_width)
    weight_gu = gu_all.reshape(width, 2 * part_ff)
    weight_d = wd_all.reshape(part_ff, width)
    weight_o = wo_all.reshape(q_width, width)
    segs = seg_all[:, 0, :].reshape(length)

    starts = jnp.sum((segs[None, :] < segs[:, None]).astype(jnp.int32), 1)
    places = (jnp.arange(length, dtype=jnp.int32) - starts).astype(FULL)
    freqs = ROPE_BASE ** (-jnp.arange(0, HEAD_DIM, 2).astype(FULL) / HEAD_DIM)
    turned = places[:, None] * freqs[None, :]
    cosines, sines = jnp.cos(turned)[:, None, :], jnp.sin(turned)[:, None, :]
    starts = starts[:, None]

    scale_one = lax.rsqrt(jnp.mean(inputs * inputs, -1, keepdims=True) + EPS)
    norm_one = (inputs * scale_one).astype(LOW)
    qkv = matmul(norm_one, weight_q)

    def to_heads(values):
        return values.astype(LOW).transpose(1, 0, 2)

    queries = to_heads(
        rotate(qkv[:, :q_width].reshape(length, heads, HEAD_DIM), cosines, sines) * factor
    )
    keys = to_heads(
        rotate(
            qkv[:, q_width : q_width + kv_width].reshape(length, kv_heads, HEAD_DIM),
            cosines,
            sines,
        )
    )
    values = to_heads(qkv[:, q_width + kv_width :].reshape(length, kv_heads, HEAD_DIM))
    attended, lse = attend(starts, queries, keys, values)
    attended = attended.transpose(1, 0, 2).reshape(length, q_width)
    part = matmul(attended, weight_o).astype(LOW).reshape(n_seq, local, width)
    middle = x_own.astype(FULL) + scatter(n_dp, n_seq, 2, part)

    scale_two = lax.rsqrt(jnp.mean(middle * middle, -1, keepdims=True) + EPS)
    norm_two = middle * scale_two
    second = gather(n_dp, n_seq, 3, norm_two.astype(LOW)).reshape(length, width)
    both = matmul(second, weight_gu)
    gate, upward = both[:, :part_ff], both[:, part_ff:]
    sigma = jax.nn.sigmoid(gate)
    hidden = (gate * sigma * upward).astype(LOW)
    part = matmul(hidden, weight_d).astype(LOW).reshape(n_seq, local, width)
    result = (middle + scatter(n_dp, n_seq, 4, part)).astype(dtype)

    grad_hidden = matmul_nt(dy, weight_d)
    grad_gate = (grad_hidden * upward * sigma * (1.0 + gate * (1.0 - sigma))).astype(LOW)
    grad_up = (grad_hidden * gate * sigma).astype(LOW)
    grad_both = jnp.concatenate([grad_gate, grad_up], 1)
    part = matmul_nt(grad_both, weight_gu).astype(LOW).reshape(n_seq, local, width)
    grad_second = scatter(n_dp, n_seq, 5, part)
    grad_middle = dy_own.astype(FULL) + norm_back(grad_second, norm_two, scale_two)
    grad_gu = matmul_tn(second, grad_both).astype(LOW)
    grad_d = matmul_tn(hidden, dy).astype(LOW)

    middle_low = gather(n_dp, n_seq, 6, grad_middle.astype(LOW)).reshape(length, width)
    grad_o = matmul_tn(attended, middle_low).astype(LOW)
    grad_attended = (
        matmul_nt(middle_low, weight_o).astype(LOW).reshape(length, heads, HEAD_DIM)
    ).transpose(1, 0, 2)
    dq, dk, dv = attend_back(starts, queries, keys, values, grad_attended, lse)

    def from_heads(grads):
        return grads.transpose(1, 0, 2)

    def flat(grads):
        return grads.reshape(length, grads.shape[1] * HEAD_DIM).astype(LOW)

    grad_qkv = jnp.concatenate(
        [
            flat(rotate(from_heads(dq) * factor, cosines, -sines)),
            flat(rotate(from_heads(dk), cosines, -sines)),
            flat(from_heads(dv)),
        ],
        1,
    )
    part = matmul_nt(grad_qkv, weight_q).astype(LOW).reshape(n_seq, local, width)
    grad_normed = scatter(n_dp, n_seq, 7, part)
    own_inputs = x_own.astype(FULL)
    own_scale = lax.rsqrt(jnp.mean(own_inputs * own_inputs, -1, keepdims=True) + EPS)
    grad_inputs = grad_middle + norm_back(grad_normed, own_inputs * own_scale, own_scale)
    grad_q = matmul_tn(norm_one, grad_qkv).astype(LOW)

    got_gu, got_d = reduce(
        n_dp,
        n_seq,
        8,
        grad_gu.reshape(n_dp, n_seq * own_rows, 2 * part_ff),
        grad_d.reshape((n_dp,) + down_block.shape),
        FULL,
    )
    got_q, got_o = reduce(
        n_dp,
        n_seq,
        9,
        grad_q.reshape(n_dp, n_seq * own_rows, q_width + 2 * kv_width),
        grad_o.reshape((n_dp,) + w_output.shape),
        LOW,
    )
    grad_output_w = lax.ppermute(got_o, ("dp", "seq"), back).astype(FULL)
    grad_down_w = got_d.reshape(own_ff, width)

    def ff_join(grads):
        return (
            grads.astype(FULL)
            .reshape(n_seq, own_rows, n_dp, own_ff)
            .transpose(1, 2, 0, 3)
            .reshape(own_rows, n_dp * n_seq * own_ff)
        )

    raw_gate = ff_join(got_gu[:, :, :part_ff])
    raw_up = ff_join(got_gu[:, :, part_ff:])
    raw_query = (
        got_q[:, :, :q_width].astype(FULL).transpose(1, 0, 2).reshape(own_rows, width)
    )

    def kv_join(grads):
        firsts = [s * heads // GROUP for s in range(n_seq)]
        columns = []
        for head in range(KV_HEADS):
            terms = [
                grads[s, :, (head - first) * HEAD_DIM : (head - first + 1) * HEAD_DIM].astype(FULL)
                for s, first in enumerate(firsts)
                if first <= head < first + kv_heads
            ]
            columns.append(functools.reduce(jnp.add, terms))
        return jnp.concatenate(columns, 1)

    raw_key = kv_join(got_q[:, :, q_width : q_width + kv_width])
    raw_value = kv_join(got_q[:, :, q_width + kv_width :])

    def gain_grad(*pairs):
        return sum(jnp.sum(weight.astype(FULL) * raw, 1) for weight, raw in pairs)

    grad_attn_gain = gain_grad((w_query, raw_query), (w_key, raw_key), (w_value, raw_value))
    grad_mlp_gain = gain_grad((w_gate, raw_gate), (w_up, raw_up))
    return (
        result.reshape(tokens.shape),
        grad_inputs.reshape(tokens.shape),
        grad_attn_gain,
        gain_one * raw_query,
        gain_one * raw_key,
        gain_one * raw_value,
        grad_output_w,
        grad_mlp_gain,
        gain_two * raw_gate,
        gain_two * raw_up,
        grad_down_w,
    )


def solution(mesh):
    rows = P(("dp", "seq"), None)
    vector = P(("dp", "seq"))
    row = P("dp", "seq", None)
    return jax.shard_map(
        functools.partial(body, mesh.shape["dp"], mesh.shape["seq"]),
        mesh=mesh,
        in_specs=(row, P("dp", "seq"), vector, rows, rows, rows, rows, vector, rows, rows, rows, row),
        out_specs=(row, row, vector, rows, rows, rows, rows, vector, rows, rows, rows),
        check_vma=False,
    )
```

```python
import functools

import jax
import jax.numpy as jnp
from jax import lax
from jax.experimental import pallas as pl
from jax.experimental.pallas import tpu as pltpu
from jax.sharding import PartitionSpec as P

HEADS = 32
HEAD_DIM = 64
KV_HEADS = 4
GROUP = HEADS // KV_HEADS

EPS = 1e-05
ROPE_BASE = 10000.0
MASK_VALUE = -1e30
MESH = pl.DeviceIdType.MESH
LOW = jnp.bfloat16
FULL = jnp.float32
VMEM_BYTES = 60 * 1024 * 1024


def matmul(left, right):
    return jnp.dot(left, right, preferred_element_type=FULL)


def matmul_nt(left, right):
    return lax.dot_general(left, right, (((1,), (1,)), ((), ())), preferred_element_type=FULL)


def matmul_tn(left, right):
    return lax.dot_general(left, right, (((0,), (0,)), ((), ())), preferred_element_type=FULL)


def ring_at(place, n):
    upper = lax.div(place, n // 2)
    return (1 - upper) * 2 * place + upper * (2 * (n - place) - 1)


def ring_place(index, n):
    odd = lax.rem(index, 2)
    return (1 - odd) * lax.div(index, 2) + odd * (n - lax.div(index + 1, 2))


class Where:
    def __init__(self, n_dp, n_seq):
        self.n_dp, self.n_seq = n_dp, n_seq
        self.chips = n_dp // 2
        self.dp = lax.axis_index("dp")
        self.seq = lax.axis_index("seq")
        self.core = lax.rem(self.dp, 2)
        self.chip = lax.div(self.dp, 2)
        self.place = ring_place(self.seq, n_seq)

    def ring(self, step):
        return ring_at(lax.rem(self.place + step + self.n_seq, self.n_seq), self.n_seq)

    def ring_ids(self):
        return [(self.dp, self.ring(1)), (self.dp, self.ring(-1))]

    def seq_ids(self):
        return [
            (self.dp, lax.rem(self.seq + k, self.n_seq)) for k in range(1, self.n_seq)
        ]

    def dp_ids(self):
        return [(lax.rem(self.dp + k, self.n_dp), self.seq) for k in range(1, self.n_dp)]

    def core_id(self):
        return (self.dp + 1 - 2 * self.core, self.seq)

    def chip_ids(self):
        return [
            (2 * lax.rem(self.chip + k, self.chips) + self.core, self.seq)
            for k in range(1, self.chips)
        ]


def greet(ids):
    barrier = pltpu.get_barrier_semaphore()
    for one in ids:
        pl.semaphore_signal(barrier, inc=1, device_id=one, device_id_type=MESH)
    pl.semaphore_wait(barrier, len(ids))


def remote(src, dst, send, recv, target):
    return pltpu.make_async_remote_copy(
        src_ref=src,
        dst_ref=dst,
        send_sem=send,
        recv_sem=recv,
        device_id=target,
        device_id_type=MESH,
    )


class Ring:
    def __init__(self, at, shape, send, recv):
        self.at, self.send, self.recv = at, send, recv
        self.steps = at.n_seq // 2
        self.halves = 2 if len(shape) > 2 or shape[0] % 32 == 0 else 1
        self.half = shape[0] // self.halves
        self.copies = {}

    @staticmethod
    def semaphores(n_seq):
        shape = (2, n_seq // 2, 2)
        return [pltpu.SemaphoreType.DMA(shape), pltpu.SemaphoreType.DMA(shape)]

    def opposite(self, h, d):
        return d == h if self.halves == 2 else d == 0

    def rows(self, h):
        return pl.ds(h * self.half, self.half)

    def go(self, src, dst, d, t, h):
        target = self.at.ring_ids()[d]
        copy = remote(src, dst, self.send.at[d, t, h], self.recv.at[d, t, h], target)
        copy.start()
        self.copies[(d, t, h)] = copy

    def pieces(self):
        return [(h, d) for h in range(self.halves) for d in (0, 1)]


class RingGather(Ring):
    def __init__(self, at, own, everything, send, recv, local):
        super().__init__(at, own.shape, send, recv)
        self.own, self.everything = own, everything
        self.kept = pltpu.make_async_copy(own, everything.at[at.seq], local)
        self.waited = set()

    @staticmethod
    def scratch(n_seq):
        return Ring.semaphores(n_seq)

    def wait(self, key):
        self.copies[key].wait_recv()
        self.waited.add(key)

    def step(self, t):
        if t == 0:
            self.kept.start()
        for h, d in self.pieces():
            if t == self.steps - 1 and not self.opposite(h, d):
                continue
            if t > 0:
                self.wait((d, t - 1, h))
            origin = self.at.ring(-t if d == 0 else t)
            dst = self.everything.at[origin, self.rows(h)]
            self.go(self.own.at[self.rows(h)] if t == 0 else dst, dst, d, t, h)

    def finish(self):
        for key in self.copies:
            if key not in self.waited:
                self.wait(key)
        for copy in self.copies.values():
            copy.wait_send()
        self.kept.wait()


class RingScatter(Ring):
    def __init__(self, at, parts, slots, send, recv, staged=None, loads=None):
        super().__init__(at, parts.shape[1:], send, recv)
        self.parts, self.slots, self.staged, self.loads = parts, slots, staged, loads

    @staticmethod
    def scratch(n_seq, *block):
        return [pltpu.VMEM((2, n_seq // 2) + block, LOW)] + Ring.semaphores(n_seq)

    @staticmethod
    def staging(*block):
        return [pltpu.VMEM((2,) + block, LOW), pltpu.SemaphoreType.DMA((2, 2))]

    def there(self, t, d):
        return self.at.ring(self.steps - t if d == 0 else t - self.steps)

    def adds(self, t, h, d):
        return t > 1 or (t == 1 and self.opposite(h, d))

    def load(self, t, h, d):
        rows = self.rows(h)
        block = self.parts.at[self.there(t, d), rows]
        return pltpu.make_async_copy(block, self.staged.at[d, rows], self.loads.at[d, h])

    def load_all(self, t):
        if self.staged is not None:
            for h, d in self.pieces():
                if t < self.steps and self.adds(t, h, d):
                    self.load(t, h, d).start()
                elif t == self.steps and d == 0:
                    self.load(t, h, d).start()

    def step(self, t):
        if t == 0:
            self.load_all(1)
        for h, d in self.pieces():
            if t == 0 and not self.opposite(h, d):
                continue
            rows = self.rows(h)
            src = self.parts.at[self.there(t, d), rows]
            if self.adds(t, h, d):
                if self.staged is not None:
                    self.load(t, h, d).wait()
                    src = self.staged.at[d, rows]
                self.copies[(d, t - 1, h)].wait_recv()
                held = self.slots.at[d, t - 1, rows]
                held[...] = (held[...].astype(FULL) + src[...].astype(FULL)).astype(LOW)
                src = held
            self.go(src, self.slots.at[d, t, rows], d, t, h)
        if t > 0:
            self.load_all(t + 1)

    def finish(self, out):
        last = self.steps - 1
        if last == 0:
            self.load_all(1)
        for h in range(self.halves):
            rows = self.rows(h)
            if self.staged is None:
                total = self.parts[self.at.seq, rows].astype(FULL)
            else:
                self.load(self.steps, h, 0).wait()
                total = self.staged[0, rows].astype(FULL)
            for d in (0, 1):
                if last == 0 and not self.opposite(h, d):
                    continue
                self.copies[(d, last, h)].wait_recv()
                total = total + self.slots[d, last, rows].astype(FULL)
            out[rows] = total.astype(out.dtype)
        for copy in self.copies.values():
            copy.wait_send()


class Exchange:
    def __init__(self, me, ids, axis, packed, landing, send, recv, local):
        self.kept = pltpu.make_async_copy(packed.at[me], landing.at[me], local)
        self.copies = [
            remote(packed.at[one[axis]], landing.at[me], send.at[k], recv.at[k], one)
            for k, one in enumerate(ids)
        ]

    @staticmethod
    def scratch(n):
        return [pltpu.SemaphoreType.DMA((n - 1,)), pltpu.SemaphoreType.DMA((n - 1,))]

    def start(self):
        self.kept.start()
        for copy in self.copies:
            copy.start()

    def arrived(self):
        self.kept.wait()
        for copy in self.copies:
            copy.wait_recv()

    def finish(self):
        for copy in self.copies:
            copy.wait_send()


def seq_exchange(at, *refs):
    return Exchange(at.seq, at.seq_ids(), 1, *refs)


def dp_exchange(at, *refs):
    return Exchange(at.dp, at.dp_ids(), 0, *refs)


class DpGather:
    def __init__(self, at, own, everything, send, recv, local):
        self.kept = pltpu.make_async_copy(own, everything.at[at.dp], local)
        slot = everything.at[at.dp]
        self.out = [
            remote(own, slot, send.at[k], recv.at[k], one) for k, one in enumerate(at.chip_ids())
        ]
        base = at.chips - 1
        self.mate = remote(own, slot, send.at[base], recv.at[base], at.core_id())
        self.handed = []
        for k in range(1, at.chips):
            origin = 2 * lax.rem(at.chip + at.chips - k, at.chips) + at.core
            there = everything.at[origin]
            self.handed.append(
                remote(there, there, send.at[base + k], recv.at[base + k], at.core_id())
            )

    @staticmethod
    def scratch(n_dp):
        return [pltpu.SemaphoreType.DMA((n_dp - 1,)), pltpu.SemaphoreType.DMA((n_dp - 1,))]

    def start(self):
        for copy in self.out:
            copy.start()
        self.mate.start()
        self.kept.start()

    def hand(self):
        for copy, onward in zip(self.out, self.handed):
            copy.wait_recv()
            onward.start()

    def arrived(self):
        self.kept.wait()
        self.mate.wait_recv()
        for copy in self.handed:
            copy.wait_recv()

    def finish(self):
        for copy in self.out + [self.mate] + self.handed:
            copy.wait_send()


def add_rows(rows, chunk, one):
    def step(r, carry):
        one(pl.ds(pl.multiple_of(r * chunk, chunk), chunk))
        return carry

    lax.fori_loop(0, rows // chunk, step, 0)


def chunk_of(rows, columns):
    chunk = rows
    while chunk % 32 == 0 and chunk * columns > 65536:
        chunk //= 2
    return chunk


class DpScatter:
    def __init__(self, at, parts, core, other, send, recv):
        self.at, self.parts, self.core, self.other = at, parts, core, other
        self.send, self.recv = send, recv
        self.rows, self.columns = parts.shape[1], parts.shape[2]

    @staticmethod
    def scratch(n_dp, rows, columns):
        chips = n_dp // 2
        return [
            pltpu.VMEM((chips, rows, columns), LOW),
            pltpu.VMEM((max(chips - 1, 1), rows, columns), LOW),
            pltpu.SemaphoreType.DMA((2 * chips - 1,)),
            pltpu.SemaphoreType.DMA((2 * chips - 1,)),
        ]

    def to_core(self, k):
        at = self.at
        return remote(
            self.parts.at[2 * k + 1 - at.core],
            self.core.at[k],
            self.send.at[k],
            self.recv.at[k],
            at.core_id(),
        )

    def to_chip(self, k):
        at = self.at
        sem = at.chips + k - 1
        return remote(
            self.core.at[lax.rem(at.chip + k, at.chips)],
            self.other.at[k - 1],
            self.send.at[sem],
            self.recv.at[sem],
            at.chip_ids()[k - 1],
        )

    def start(self):
        for k in range(self.at.chips):
            self.to_core(k).start()

    def add_core(self, k):
        held = self.core.at[k]
        mine = self.parts.at[2 * k + self.at.core]

        def one(rows):
            held[rows] = (held[rows].astype(FULL) + mine[rows].astype(FULL)).astype(LOW)

        add_rows(self.rows, chunk_of(self.rows, self.columns), one)

    def across(self):
        at = self.at
        for k in range(1, at.chips):
            there = lax.rem(at.chip + k, at.chips)
            self.to_core(there).wait_recv()
            self.add_core(there)
            self.to_chip(k).start()

    def finish(self, out):
        at = self.at
        self.to_core(at.chip).wait_recv()
        for k in range(1, at.chips):
            self.to_chip(k).wait_recv()
        held = self.core.at[at.chip]
        mine = self.parts.at[2 * at.chip + at.core]

        def one(rows):
            total = held[rows].astype(FULL) + mine[rows].astype(FULL)
            for k in range(1, at.chips):
                total = total + self.other[k - 1, rows].astype(FULL)
            out[rows] = total.astype(out.dtype)

        add_rows(self.rows, chunk_of(self.rows, self.columns), one)
        for k in range(at.chips):
            self.to_core(k).wait_send()
        for k in range(1, at.chips):
            self.to_chip(k).wait_send()


def comm_params(number):
    return pltpu.CompilerParams(
        collective_id=number, has_side_effects=True, vmem_limit_bytes=VMEM_BYTES
    )


ANY = pl.BlockSpec(memory_space=pl.ANY)
VMEM = pl.BlockSpec(memory_space=pltpu.VMEM)


def shape_of(dims, kind):
    return jax.ShapeDtypeStruct(dims, kind)


class Refs:
    def __init__(self, names, refs):
        refs = list(refs)
        for name, count in names:
            taken, refs = refs[: max(count, 1)], refs[max(count, 1) :]
            setattr(self, name, taken if count else taken[0])


def run(kernel, name, number, ins, outs, scratch):
    names = [(key, 0) for key in ins] + [(key, 0) for key in outs]
    shapes = []
    for key, value in scratch.items():
        if isinstance(value, list):
            names.append((key, len(value)))
            shapes += value
        else:
            names.append((key, 0))
            shapes.append(value)
    found = pl.pallas_call(
        lambda *refs: kernel(Refs(names, refs)),
        name=name,
        out_shape=[shape for shape, _ in outs.values()],
        in_specs=[spec for _, spec in ins.values()],
        out_specs=[spec for _, spec in outs.values()],
        scratch_shapes=shapes,
        compiler_params=comm_params(number),
    )(*[array for array, _ in ins.values()])
    return dict(zip(outs, found))


def dma(*dims):
    return pltpu.SemaphoreType.DMA(dims)


def vm(kind, *dims):
    return pltpu.VMEM(dims, kind)


def lanes(rows):
    return lax.broadcasted_iota(jnp.int32, (rows, 2 * HEAD_DIM), 1)


def low_head(rows):
    return lanes(rows) < HEAD_DIM


def swapped(pair):
    half = HEAD_DIM // 2
    first = lax.rem(lanes(pair.shape[0]), HEAD_DIM) < half
    return jnp.where(
        first, pltpu.roll(pair, 2 * HEAD_DIM - half, 1), pltpu.roll(pair, half, 1)
    )


def split_heads(pair):
    wide = pair.astype(FULL)
    low = low_head(pair.shape[0])
    return jnp.concatenate(
        [jnp.where(low, wide, 0.0), jnp.where(low, 0.0, wide)], 0
    ).astype(LOW)


def join_heads(both):
    rows = both.shape[0] // 2
    return jnp.where(low_head(rows), both[:rows], both[rows:])


def spread_kv(kv):
    wide = kv.astype(FULL)
    turned = pltpu.roll(wide, HEAD_DIM, 1)
    low = low_head(kv.shape[0])
    return jnp.where(low, wide, turned).astype(LOW), jnp.where(low, turned, wide).astype(LOW)


def mask_of(position, start, length):
    key = lax.broadcasted_iota(jnp.int32, (start.shape[0], length), 1)
    return jnp.where((key <= position) & (key >= start), 0.0, MASK_VALUE)


def own_positions(at, tok):
    return at.seq * tok + lax.broadcasted_iota(jnp.int32, (tok, 1), 0)


def rows_of(r, count):
    return pl.ds(pl.multiple_of(r * count, count), count)


def interleave(ring, jobs):
    jobs = list(jobs)
    for t in range(1, ring.steps):
        if jobs:
            jobs.pop(0)()
        ring.step(t)
    for job in jobs:
        job()


def front_kernel(n_dp, n_seq, own_ff, m):
    at = Where(n_dp, n_seq)
    tok, width = m.x.shape
    q_width = m.q.shape[1]
    groups = q_width // (2 * HEAD_DIM)
    rank = n_seq * m.pq.shape[1]
    length = n_seq * tok
    greet(at.seq_ids() + at.dp_ids())
    swap_q = dp_exchange(at, m.pq, m.landed, *m.swap_q_sem, m.local.at[0])
    x_g = DpGather(at, m.x, m.xs, *m.x_sem, m.local.at[1])
    row_x = seq_exchange(at, m.seg_rows, m.seg_row, *m.row_x_sem, m.local.at[2])
    row_g = DpGather(at, m.seg_row, m.segs, *m.row_g_sem, m.local.at[3])
    col_g = DpGather(at, m.seg_col, m.seg_cols, *m.col_g_sem, m.local.at[4])
    ring_q = RingGather(at, m.landed, m.wq_all, *m.ring_q_sem, m.local.at[5])
    ring_o = RingGather(at, m.wo, m.wo_all, *m.ring_o_sem, m.local.at[6])
    ring_kv = RingGather(at, m.kv_own, m.kv_all, *m.ring_kv_sem, m.local.at[7])
    swap_gu = seq_exchange(at, m.pgu, m.gu, *m.swap_gu_sem, m.local.at[8])
    stores = []

    def store(src, dst):
        copy = pltpu.make_async_copy(src, dst, m.local.at[9 + len(stores)])
        copy.start()
        stores.append(copy)

    swap_q.start()
    x_g.start()
    row_x.start()
    col_g.start()

    def pack(weight, first):
        for s in range(n_seq):
            for i in range(n_dp):
                piece = weight[:, (i * n_seq + s) * own_ff : (i * n_seq + s + 1) * own_ff]
                m.pgu[s, :, first + i * own_ff : first + (i + 1) * own_ff] = (
                    m.gain[:, :1] * piece.astype(FULL)
                ).astype(LOW)

    swap_q.arrived()
    ring_q.step(0)
    row_x.arrived()
    row_g.start()

    def hand():
        x_g.hand()
        row_g.hand()
        col_g.hand()

    def norm():
        x_g.arrived()
        for r in range(n_dp):
            x = m.xs[r].astype(FULL)
            scale = lax.rsqrt(jnp.mean(x * x, -1, keepdims=True) + EPS)
            m.n1[r] = (x * scale).astype(LOW)
        store(m.n1, m.n1_out)

    def place():
        row_g.arrived()
        col_g.arrived()
        position = own_positions(at, tok)
        first = lax.rem(lanes(tok), HEAD_DIM) < HEAD_DIM // 2
        for r in range(n_dp):
            segs = jnp.concatenate([m.segs[r, s, :1] for s in range(n_seq)], 1)
            own = m.seg_cols[r][:, :1]
            start = jnp.sum((segs < own).astype(jnp.int32), 1, keepdims=True)
            turned = (position - start).astype(FULL) * m.freqs[:1]
            rows = slice(r * tok, (r + 1) * tok)
            m.cos[rows] = jnp.cos(turned)
            sines = jnp.sin(turned)
            m.sin[rows] = jnp.where(first, -sines, sines)
            m.starts[rows] = jnp.broadcast_to(start, (tok, 2 * HEAD_DIM))
        store(m.cos, m.cos_out)
        store(m.sin, m.sin_out)
        store(m.starts, m.starts_out)

    interleave(
        ring_q,
        [lambda: pack(m.wg, 0), hand, norm, place, lambda: pack(m.wu, n_dp * own_ff)],
    )
    ring_q.finish()
    ring_o.step(0)
    store(m.wq_all, m.wq_out)

    m.qkv[...] = sum(
        matmul(
            m.n1[:, :, i * rank : (i + 1) * rank].reshape(n_dp * tok, rank),
            m.wq_all[:, i].reshape(rank, q_width + 2 * HEAD_DIM),
        )
        for i in range(n_dp)
    )
    factor = HEAD_DIM ** (-0.5)
    for g in range(groups + 1):
        cols = slice(g * 2 * HEAD_DIM, (g + 1) * 2 * HEAD_DIM)
        pair = m.qkv[:, cols]
        turned = pair * m.cos[...] + swapped(pair) * m.sin[...]
        if g < groups:
            m.q[:, cols] = (turned * factor).astype(LOW)
        else:
            m.kv_own[...] = jnp.where(low_head(pair.shape[0]), turned, pair).astype(LOW)
    ring_kv.step(0)
    store(m.q, m.q_out)
    ring_o.step(1)
    for t in range(1, ring_kv.steps):
        ring_kv.step(t)
    ring_kv.finish()
    store(m.kv_all, m.kv_out)
    swap_gu.start()

    later = list(range(2, ring_o.steps))
    for r in range(n_dp):
        rows = slice(r * tok, (r + 1) * tok)
        k, v = spread_kv(m.kv_all[:, rows].reshape(length, 2 * HEAD_DIM))
        m.k2[...] = k
        m.v2[...] = v
        m.mask[...] = mask_of(own_positions(at, tok), m.starts[rows, :1], length)

        def group(g, carry):
            cols = rows_of(g, 2 * HEAD_DIM)
            raw = matmul_nt(split_heads(m.q[rows, cols]), m.k2[...])
            raw = raw + jnp.concatenate([m.mask[...]] * 2, 0)
            top = jnp.max(raw, -1, keepdims=True)
            probs = jnp.exp(raw - top)
            total = jnp.sum(probs, -1, keepdims=True)
            probs = (probs * (1.0 / total)).astype(LOW)
            m.o[rows, cols] = join_heads(matmul(probs, m.v2[...])).astype(LOW)
            m.lse[r * groups + g] = top + jnp.log(total)
            return carry

        lax.fori_loop(0, groups, group, 0)
        if later:
            ring_o.step(later.pop(0))
    for t in later:
        ring_o.step(t)
    store(m.o, m.o_out)
    store(m.lse, m.lse_out)
    ring_o.finish()
    store(m.wo_all, m.wo_out)
    full = m.wo_all[...].reshape(q_width, width)
    for r in range(n_dp):
        m.parts[r] = matmul(m.o[r * tok : (r + 1) * tok], full).astype(LOW)
    back = DpScatter(at, m.parts, *m.back)
    back.start()
    back.across()
    back.finish(m.middle)
    middle = m.x[...].astype(FULL) + m.middle[...]
    m.middle[...] = middle
    scale = lax.rsqrt(jnp.mean(middle * middle, -1, keepdims=True) + EPS)
    m.second[...] = (middle * scale).astype(LOW)
    swap_gu.arrived()
    for one in (swap_q, x_g, row_x, row_g, col_g, swap_gu):
        one.finish()
    for copy in stores:
        copy.wait()


def front(n_dp, n_seq, own_ff, x, seg_rows, seg_col, freqs, pq, wg, wu, gain, wo):
    tok, width = x.shape
    rank, columns = pq.shape[1:]
    q_width = columns - 2 * HEAD_DIM
    groups = q_width // (2 * HEAD_DIM)
    pair = 2 * HEAD_DIM
    length = n_seq * tok
    every = n_dp * tok
    gu_width = 2 * n_dp * own_ff
    ins = {
        "x": x, "seg_rows": seg_rows, "seg_col": seg_col, "freqs": freqs, "pq": pq, "wg": wg, "wu": wu, "gain": gain, "wo": wo,
    }
    ins = {key: (value, VMEM) for key, value in ins.items()}
    kept = {
        "n1": (LOW, n_dp, tok, width),
        "q": (LOW, every, q_width),
        "kv_all": (LOW, n_seq, every, pair),
        "o": (LOW, every, q_width),
        "lse": (FULL, n_dp * groups, 2 * tok, 1),
        "cos": (FULL, every, pair),
        "sin": (FULL, every, pair),
        "starts": (jnp.int32, every, pair),
        "wq_all": (LOW, n_seq, n_dp, rank, columns),
        "wo_all": (LOW, n_seq, rank, width),
    }
    outs = {
        key.replace("_all", "") + "_out": (shape_of(dims[1:], dims[0]), ANY)
        for key, dims in kept.items()
    }
    outs["gu"] = (shape_of((n_seq, rank, gu_width), LOW), ANY)
    outs["middle"] = (shape_of((tok, width), FULL), VMEM)
    outs["second"] = (shape_of((tok, width), LOW), VMEM)
    scratch = {key: vm(*dims) for key, dims in kept.items()}
    scratch |= {
        "landed": vm(LOW, n_dp, rank, columns),
        "xs": vm(LOW, n_dp, tok, width),
        "seg_row": vm(jnp.int32, n_seq, 8, tok),
        "segs": vm(jnp.int32, n_dp, n_seq, 8, tok),
        "seg_cols": vm(jnp.int32, n_dp, tok, pair),
        "kv_own": vm(LOW, every, pair),
        "mask": vm(FULL, tok, length),
        "pgu": vm(LOW, n_seq, rank, gu_width),
        "qkv": vm(FULL, every, columns),
        "k2": vm(LOW, length, pair),
        "v2": vm(LOW, length, pair),
        "parts": vm(LOW, n_dp, tok, width),
        "back": DpScatter.scratch(n_dp, tok, width),
        "local": dma(9 + len(kept)),
        "swap_q_sem": Exchange.scratch(n_dp),
        "x_sem": DpGather.scratch(n_dp),
        "row_x_sem": Exchange.scratch(n_seq),
        "row_g_sem": DpGather.scratch(n_dp),
        "col_g_sem": DpGather.scratch(n_dp),
        "ring_q_sem": Ring.semaphores(n_seq),
        "ring_o_sem": Ring.semaphores(n_seq),
        "ring_kv_sem": Ring.semaphores(n_seq),
        "swap_gu_sem": Exchange.scratch(n_seq),
    }
    return run(
        functools.partial(front_kernel, n_dp, n_seq, own_ff), "attention_forward", 1, ins, outs, scratch
    )


def feed_kernel(n_dp, n_seq, m):
    at = Where(n_dp, n_seq)
    greet(at.ring_ids() + at.dp_ids())
    ring_n = RingGather(at, m.second, m.second_all, *m.ring_n, m.local.at[0])
    ring_dy = RingGather(at, m.dy, m.dy_all, *m.ring_dy, m.local.at[1])
    gu = DpGather(at, m.gu, m.gu_all, *m.gu_sem, m.local.at[2])
    down = DpGather(at, m.wd, m.wd_all, *m.wd_sem, m.local.at[3])
    ring_n.step(0)
    gu.start()
    down.start()
    for t in range(1, ring_n.steps):
        ring_n.step(t)
    ring_dy.step(0)
    gu.hand()
    down.hand()
    for t in range(1, ring_dy.steps):
        ring_dy.step(t)
    for one in (gu, down):
        one.arrived()
    for one in (ring_n, ring_dy, gu, down):
        one.finish()


def feed(n_dp, n_seq, second, dy, gu, wd):
    ins = {"second": second, "dy": dy, "gu": gu, "wd": wd}
    outs = {
        "second_all": (shape_of((n_seq,) + second.shape, LOW), ANY),
        "dy_all": (shape_of((n_seq,) + dy.shape, LOW), ANY),
        "gu_all": (shape_of((n_dp,) + gu.shape, LOW), ANY),
        "wd_all": (shape_of((n_dp,) + wd.shape, LOW), ANY),
    }
    scratch = {
        "local": dma(4),
        "ring_n": Ring.semaphores(n_seq),
        "ring_dy": Ring.semaphores(n_seq),
        "gu_sem": DpGather.scratch(n_dp),
        "wd_sem": DpGather.scratch(n_dp),
    }
    return run(
        functools.partial(feed_kernel, n_dp, n_seq),
        "gather_feed_forward",
        2,
        {key: (value, ANY) for key, value in ins.items()},
        outs,
        scratch,
    )


def back_kernel(n_dp, n_seq, m):
    at = Where(n_dp, n_seq)
    tok, width = m.x.shape
    q_width = m.q.shape[1]
    groups = q_width // (2 * HEAD_DIM)
    rank = n_seq * m.wq.shape[2]
    length = n_seq * tok
    pair = 2 * HEAD_DIM
    greet(at.ring_ids() + at.dp_ids())
    ring_h = RingScatter(at, m.part_h, *m.ring_h, *m.staged)
    ring_y = RingScatter(at, m.part_y, m.ring_h[0], *m.ring_y, *m.staged)
    d_g = DpGather(at, m.d_own, m.d_all, *m.d_sem, m.local.at[0])
    ring_kv = RingScatter(at, m.part_kv, *m.ring_kv)
    ring_q = RingScatter(at, m.part_q, *m.ring_q)
    ring_o = RingScatter(at, m.part_o, *m.ring_o)
    back = DpScatter(at, m.d_all, *m.back)
    swap_q = dp_exchange(at, m.sum_q, m.got_q, *m.swap_q, m.local.at[1])
    for t in range(ring_h.steps):
        ring_h.step(t)
    ring_h.finish(m.dmid)
    for one in at.ring_ids():
        pl.semaphore_signal(m.free, inc=1, device_id=one, device_id_type=MESH)

    def norm_back(grad, value):
        scale = lax.rsqrt(jnp.mean(value * value, -1, keepdims=True) + EPS)
        normed = value * scale
        return scale * (grad - normed * jnp.mean(grad * normed, -1, keepdims=True))

    m.dmid[...] = m.dy[...].astype(FULL) + norm_back(m.dmid[...], m.middle[...])
    m.d_own[...] = m.dmid[...].astype(LOW)
    d_g.start()
    pl.semaphore_wait(m.free, 2)
    ring_y.step(0)
    d_g.hand()
    d_g.arrived()
    m.do[...] = matmul_nt(
        m.d_all[...].reshape(n_dp * tok, width), m.wo[...].reshape(q_width, width)
    ).astype(LOW)
    later = list(range(1, ring_y.steps))
    for r in range(n_dp):
        rows = slice(r * tok, (r + 1) * tok)
        k, v = spread_kv(m.kv[:, rows].reshape(length, pair))
        m.k2[...] = k
        m.v2[...] = v
        m.mask[...] = mask_of(own_positions(at, tok), m.starts[rows, :1], length)
        m.dk2[...] = jnp.zeros_like(m.dk2)
        m.dv2[...] = jnp.zeros_like(m.dv2)

        def group(g, carry):
            cols = rows_of(g, pair)
            q2 = split_heads(m.q[rows, cols])
            do2 = split_heads(m.do[rows, cols])
            raw = matmul_nt(q2, m.k2[...])
            raw = raw + jnp.concatenate([m.mask[...]] * 2, 0)
            probs = jnp.exp(raw - m.lse[r * groups + g])
            grad_probs = matmul_nt(do2, m.v2[...])
            delta = jnp.sum(probs * grad_probs, -1, keepdims=True)
            grad_raw = (probs * (grad_probs - delta)).astype(LOW)
            m.dq[rows, cols] = join_heads(matmul(grad_raw, m.k2[...]))
            m.dk2[...] += matmul_tn(grad_raw, q2)
            m.dv2[...] += matmul_tn(probs.astype(LOW), do2)
            return carry

        lax.fori_loop(0, groups, group, 0)
        dk = m.dk2[...]
        dv = m.dv2[...]
        dkv = jnp.where(
            low_head(length), dk + pltpu.roll(dk, HEAD_DIM, 1), dv + pltpu.roll(dv, HEAD_DIM, 1)
        )
        m.part_kv[:, rows] = dkv.astype(LOW).reshape(n_seq, tok, pair)
        if later:
            ring_y.step(later.pop(0))
    for t in later:
        ring_y.step(t)
    ring_kv.step(0)
    m.part_o[...] = (
        matmul_tn(m.o[...], m.d_all[...].reshape(n_dp * tok, width))
        .astype(LOW)
        .reshape(m.part_o.shape)
    )
    d_g.finish()
    for t in range(1, ring_kv.steps):
        ring_kv.step(t)
    ring_kv.finish(m.dkv)
    ring_y.finish(m.sum_y)
    n1 = m.ring_h[0].at[0, pl.ds(0, n_dp)]
    fetch = pltpu.make_async_copy(m.n1, n1, m.local.at[2])
    fetch.start()
    ring_o.step(0)
    m.out[...] = (m.middle[...] + m.sum_y[...]).astype(m.out.dtype)
    factor = HEAD_DIM ** (-0.5)
    for g in range(groups + 1):
        cols = slice(g * pair, (g + 1) * pair)
        grad = m.dq[:, cols] * factor if g < groups else m.dkv[...]
        turned = grad * m.cos[...] - swapped(grad) * m.sin[...]
        if g == groups:
            turned = jnp.where(low_head(grad.shape[0]), turned, grad)
        m.dqkv[:, cols] = turned.astype(LOW)
    for i in range(n_dp):
        cols = slice(i * rank, (i + 1) * rank)
        weight = m.wq[:, i].reshape(rank, q_width + pair)
        m.d_all[:, :, cols] = (
            matmul_nt(m.dqkv[...], weight).astype(LOW).reshape(n_dp, tok, rank)
        )
    back.start()
    fetch.wait()
    for i in range(n_dp):
        cols = slice(i * rank, (i + 1) * rank)
        m.part_q[:, i] = (
            matmul_tn(n1[:, :, cols].reshape(n_dp * tok, rank), m.dqkv[...]).astype(LOW).reshape(n_seq, rank // n_seq, q_width + pair)
        )
    ring_q.step(0)
    back.across()
    for t in range(1, ring_q.steps):
        ring_q.step(t)
        ring_o.step(t)
    back.finish(m.dn1)
    m.grad_x[...] = m.dmid[...] + norm_back(m.dn1[...], m.x[...].astype(FULL))
    ring_q.finish(m.sum_q)
    swap_q.start()
    ring_o.finish(m.grad_o)
    swap_q.arrived()
    swap_q.finish()


def back(n_dp, n_seq, dtype, ins):
    tok, width = ins["x"].shape
    every = n_dp * tok
    q_width = ins["q"].shape[1]
    pair = 2 * HEAD_DIM
    length = n_seq * tok
    rank, columns = ins["wq"].shape[2:]
    outs = {
        "out": (shape_of((tok, width), dtype), VMEM),
        "grad_x": (shape_of((tok, width), FULL), VMEM),
        "grad_o": (shape_of((rank, width), FULL), VMEM),
        "got_q": (shape_of((n_dp, rank, columns), LOW), ANY),
    }
    scratch = {
        "local": dma(3),
        "free": pltpu.SemaphoreType.REGULAR,
        "dmid": vm(FULL, tok, width),
        "d_own": vm(LOW, tok, width),
        "d_all": vm(LOW, n_dp, tok, width),
        "d_sem": DpGather.scratch(n_dp),
        "do": vm(LOW, every, q_width),
        "k2": vm(LOW, length, pair),
        "v2": vm(LOW, length, pair),
        "mask": vm(FULL, tok, length),
        "dk2": vm(FULL, length, pair),
        "dv2": vm(FULL, length, pair),
        "dq": vm(FULL, every, q_width),
        "dkv": vm(FULL, every, pair),
        "dqkv": vm(LOW, every, columns),
        "dn1": vm(FULL, tok, width),
        "sum_y": vm(FULL, tok, width),
        "sum_q": vm(LOW, n_dp, rank, columns),
        "part_kv": vm(LOW, n_seq, every, pair),
        "part_q": vm(LOW, n_seq, n_dp, rank, columns),
        "part_o": vm(LOW, n_seq, rank, width),
        "back": DpScatter.scratch(n_dp, tok, width),
        "ring_h": RingScatter.scratch(n_seq, tok, width),
        "ring_y": Ring.semaphores(n_seq),
        "staged": RingScatter.staging(tok, width),
        "ring_kv": RingScatter.scratch(n_seq, every, pair),
        "ring_q": RingScatter.scratch(n_seq, n_dp, rank, columns),
        "ring_o": RingScatter.scratch(n_seq, rank, width),
        "swap_q": Exchange.scratch(n_dp),
    }
    return run(
        functools.partial(back_kernel, n_dp, n_seq),
        "attention_backward",
        3,
        {key: (value, ANY if key in ("part_h", "part_y", "n1") else VMEM) for key, value in ins.items()},
        outs,
        scratch,
    )


def reduce_kernel(n_dp, n_seq, m):
    at = Where(n_dp, n_seq)
    greet(at.seq_ids() + at.dp_ids())
    down = DpScatter(at, m.rows, *m.down)
    side = DpScatter(at, m.cols, *m.side)
    side.start()
    down.start()
    side.across()
    down.across()
    side.finish(m.fin)
    n = m.got.shape[1]
    copies = []
    kept = pltpu.make_async_copy(m.fin.at[rows_of(at.seq, n)], m.got.at[at.seq], m.local.at[0])
    kept.start()
    for k, one in enumerate(at.seq_ids()):
        src = m.fin.at[rows_of(one[1], n)]
        copy = remote(src, m.got.at[at.seq], m.swap[0].at[k], m.swap[1].at[k], one)
        copy.start()
        copies.append(copy)
    down.finish(m.total)
    for copy in copies:
        copy.wait()
    kept.wait()


def reduce(n_dp, n_seq, cols, rows):
    _, deep, wide = cols.shape
    return run(
        functools.partial(reduce_kernel, n_dp, n_seq),
        "reduce_feed_forward_grads",
        4,
        {"cols": (cols, VMEM), "rows": (rows, VMEM)},
        {
            "got": (shape_of((n_seq, deep // n_seq, wide), LOW), ANY),
            "total": (shape_of(rows.shape[1:], FULL), VMEM),
        },
        {
            "local": dma(1),
            "side": DpScatter.scratch(n_dp, deep, wide),
            "down": DpScatter.scratch(n_dp, *rows.shape[1:]),
            "fin": vm(LOW, deep, wide),
            "swap": Exchange.scratch(n_seq),
        },
    )


def body(
    n_dp,
    n_seq,
    tokens,
    segment_ids,
    gain_attn,
    w_query,
    w_key,
    w_value,
    w_output,
    gain_mlp,
    w_gate,
    w_up,
    w_down,
    cotangent,
):
    local, width = tokens.shape[1], tokens.shape[2]
    length = n_seq * local
    own_rows = w_query.shape[0]
    own_ff = w_down.shape[0]
    part_ff = n_dp * own_ff
    heads = HEADS // n_dp
    q_width = heads * HEAD_DIM
    x_own = tokens.reshape(local, width)
    dy_own = cotangent.reshape(local, width)

    gain_one = gain_attn.astype(FULL)[:, None]
    gain_two = gain_mlp.astype(FULL)[:, None]
    kv_of = [i * heads // GROUP for i in range(n_dp)]

    def gained(weight):
        return (gain_one * weight.astype(FULL)).astype(LOW)

    pack_q = jnp.stack(
        [
            jnp.concatenate(
                [
                    gained(w_query[:, i * q_width : (i + 1) * q_width]),
                    gained(w_key[:, kv * HEAD_DIM : (kv + 1) * HEAD_DIM]),
                    gained(w_value[:, kv * HEAD_DIM : (kv + 1) * HEAD_DIM]),
                ],
                1,
            )
            for i, kv in enumerate(kv_of)
        ]
    )
    freqs = ROPE_BASE ** (-jnp.arange(0, HEAD_DIM, 2).astype(FULL) / HEAD_DIM)
    ids = segment_ids.reshape(local)
    pair = 2 * HEAD_DIM
    got = front(
        n_dp,
        n_seq,
        own_ff,
        x_own,
        jnp.broadcast_to(ids, (n_seq, 8, local)),
        jnp.broadcast_to(ids[:, None], (local, pair)),
        jnp.broadcast_to(jnp.tile(freqs, 4), (8, pair)),
        pack_q,
        w_gate,
        w_up,
        jnp.broadcast_to(gain_two, (own_rows, pair)),
        w_output,
    )
    down_block = w_down if own_ff % 16 == 0 else w_down.reshape(16, own_ff * width // 16)
    fed = feed(n_dp, n_seq, got["second"], dy_own, got["gu"], down_block)
    second = fed["second_all"].reshape(length, width)
    dy = fed["dy_all"].reshape(length, width)
    weight_gu = fed["gu_all"].reshape(width, 2 * part_ff)
    weight_d = fed["wd_all"].reshape(part_ff, width)

    both = matmul(second, weight_gu)
    gate, upward = both[:, :part_ff], both[:, part_ff:]
    sigma = jax.nn.sigmoid(gate)
    hidden = (gate * sigma * upward).astype(LOW)
    part_y = matmul(hidden, weight_d).astype(LOW).reshape(n_seq, local, width)
    grad_hidden = matmul_nt(dy, weight_d)
    grad_gate = (grad_hidden * upward * sigma * (1.0 + gate * (1.0 - sigma))).astype(LOW)
    grad_up = (grad_hidden * gate * sigma).astype(LOW)
    grad_both = jnp.concatenate([grad_gate, grad_up], 1)
    part_h = matmul_nt(grad_both, weight_gu).astype(LOW).reshape(n_seq, local, width)
    grad_gu = matmul_tn(second, grad_both).astype(LOW)
    grad_d = matmul_tn(hidden, dy).astype(LOW)

    ins = {
        "part_h": part_h,
        "part_y": part_y,
        "x": x_own,
        "dy": dy_own,
        "middle": got["middle"],
    }
    for name in ("n1", "q", "kv", "o", "lse", "cos", "sin", "starts", "wq", "wo"):
        ins[name] = got[name + "_out"]
    done = back(n_dp, n_seq, tokens.dtype, ins)
    reduced = reduce(
        n_dp,
        n_seq,
        grad_gu.reshape(n_dp, n_seq * own_rows, 2 * part_ff),
        grad_d.reshape((n_dp,) + down_block.shape),
    )
    got_q, got_gu = done["got_q"], reduced["got"]

    def ff_join(grads):
        return (
            grads.astype(FULL)
            .reshape(n_seq, own_rows, n_dp, own_ff)
            .transpose(1, 2, 0, 3)
            .reshape(own_rows, n_dp * n_seq * own_ff)
        )

    raw_gate = ff_join(got_gu[:, :, :part_ff])
    raw_up = ff_join(got_gu[:, :, part_ff:])
    raw_query = jnp.concatenate([got_q[i, :, :q_width] for i in range(n_dp)], 1).astype(FULL)

    def kv_join(first):
        terms = [got_q[i, :, first : first + HEAD_DIM].astype(FULL) for i in range(n_dp)]
        return jnp.concatenate(
            [
                sum(term for term, kv in zip(terms, kv_of) if kv == head)
                for head in range(KV_HEADS)
            ],
            1,
        )

    raw_key = kv_join(q_width)
    raw_value = kv_join(q_width + HEAD_DIM)

    def gain_grad(*pairs):
        return sum(jnp.sum(weight.astype(FULL) * raw, 1) for weight, raw in pairs)

    return (
        done["out"].reshape(tokens.shape),
        done["grad_x"].reshape(tokens.shape),
        gain_grad((w_query, raw_query), (w_key, raw_key), (w_value, raw_value)),
        gain_one * raw_query,
        gain_one * raw_key,
        gain_one * raw_value,
        done["grad_o"],
        gain_grad((w_gate, raw_gate), (w_up, raw_up)),
        gain_two * raw_gate,
        gain_two * raw_up,
        reduced["total"].reshape(own_ff, width),
    )


def solution(mesh):
    rows = P(("dp", "seq"), None)
    vector = P(("dp", "seq"))
    row = P("dp", "seq", None)
    return jax.shard_map(
        functools.partial(body, mesh.shape["dp"], mesh.shape["seq"]),
        mesh=mesh,
        in_specs=(row, P("dp", "seq"), vector, rows, rows, rows, rows, vector, rows, rows, rows, row),
        out_specs=(row, row, vector, rows, rows, rows, rows, vector, rows, rows, rows),
        check_vma=False,
    )
```

```python
import functools

import jax
import jax.numpy as jnp
from jax import lax
from jax.experimental import pallas as pl
from jax.experimental.pallas import tpu as pltpu
from jax.sharding import PartitionSpec as P

HEADS = 32
HEAD_DIM = 64
KV_HEADS = 4
GROUP = HEADS // KV_HEADS

EPS = 1e-05
ROPE_BASE = 10000.0
MASK_VALUE = -1e30
MESH = pl.DeviceIdType.MESH
LOW = jnp.bfloat16
FULL = jnp.float32
VMEM_BYTES = 60 * 1024 * 1024


def matmul(left, right):
    return jnp.dot(left, right, preferred_element_type=FULL)


def matmul_nt(left, right):
    return lax.dot_general(left, right, (((1,), (1,)), ((), ())), preferred_element_type=FULL)


def matmul_tn(left, right):
    return lax.dot_general(left, right, (((0,), (0,)), ((), ())), preferred_element_type=FULL)


def ring_at(place, n):
    upper = lax.div(place, n // 2)
    return (1 - upper) * 2 * place + upper * (2 * (n - place) - 1)


def ring_place(index, n):
    odd = lax.rem(index, 2)
    return (1 - odd) * lax.div(index, 2) + odd * (n - lax.div(index + 1, 2))


class Where:
    def __init__(self, n_dp, n_seq):
        self.n_dp, self.n_seq = n_dp, n_seq
        self.chips = n_dp // 2
        self.dp = lax.axis_index("dp")
        self.seq = lax.axis_index("seq")
        self.core = lax.rem(self.dp, 2)
        self.chip = lax.div(self.dp, 2)
        self.place = ring_place(self.seq, n_seq)

    def ring(self, step):
        return ring_at(lax.rem(self.place + step + self.n_seq, self.n_seq), self.n_seq)

    def ring_ids(self):
        return [(self.dp, self.ring(1)), (self.dp, self.ring(-1))]

    def seq_ids(self):
        return [
            (self.dp, lax.rem(self.seq + k, self.n_seq)) for k in range(1, self.n_seq)
        ]

    def dp_ids(self):
        return [(lax.rem(self.dp + k, self.n_dp), self.seq) for k in range(1, self.n_dp)]

    def core_id(self):
        return (self.dp + 1 - 2 * self.core, self.seq)

    def chip_ids(self):
        return [
            (2 * lax.rem(self.chip + k, self.chips) + self.core, self.seq)
            for k in range(1, self.chips)
        ]


def greet(ids):
    barrier = pltpu.get_barrier_semaphore()
    for one in ids:
        pl.semaphore_signal(barrier, inc=1, device_id=one, device_id_type=MESH)
    pl.semaphore_wait(barrier, len(ids))


def remote(src, dst, send, recv, target):
    return pltpu.make_async_remote_copy(
        src_ref=src,
        dst_ref=dst,
        send_sem=send,
        recv_sem=recv,
        device_id=target,
        device_id_type=MESH,
    )


class Ring:
    def __init__(self, at, shape, send, recv):
        self.at, self.send, self.recv = at, send, recv
        self.steps = at.n_seq // 2
        self.halves = 2 if len(shape) > 2 or shape[0] % 32 == 0 else 1
        self.half = shape[0] // self.halves
        self.copies = {}

    @staticmethod
    def semaphores(n_seq):
        shape = (2, n_seq // 2, 2)
        return [pltpu.SemaphoreType.DMA(shape), pltpu.SemaphoreType.DMA(shape)]

    def opposite(self, h, d):
        return d == h if self.halves == 2 else d == 0

    def rows(self, h):
        return pl.ds(h * self.half, self.half)

    def go(self, src, dst, d, t, h):
        target = self.at.ring_ids()[d]
        copy = remote(src, dst, self.send.at[d, t, h], self.recv.at[d, t, h], target)
        copy.start()
        self.copies[(d, t, h)] = copy

    def pieces(self):
        return [(h, d) for h in range(self.halves) for d in (0, 1)]


class RingGather(Ring):
    def __init__(self, at, own, everything, send, recv, local):
        super().__init__(at, own.shape, send, recv)
        self.own, self.everything = own, everything
        self.kept = pltpu.make_async_copy(own, everything.at[at.seq], local)
        self.waited = set()

    @staticmethod
    def scratch(n_seq):
        return Ring.semaphores(n_seq)

    def wait(self, key):
        self.copies[key].wait_recv()
        self.waited.add(key)

    def step(self, t):
        if t == 0:
            self.kept.start()
        if t == 1:
            self.kept.wait()
        for h, d in self.pieces():
            if t == self.steps - 1 and not self.opposite(h, d):
                continue
            if t > 0:
                self.wait((d, t - 1, h))
            origin = self.at.ring(-t if d == 0 else t)
            dst = self.everything.at[origin, self.rows(h)]
            self.go(self.own.at[self.rows(h)] if t == 0 else dst, dst, d, t, h)

    def rest(self, t):
        for key in self.copies:
            if key not in self.waited and key[1] <= t:
                self.wait(key)

    def finish(self):
        self.rest(self.steps)
        for copy in self.copies.values():
            copy.wait_send()
        if self.steps == 1:
            self.kept.wait()


class RingScatter(Ring):
    def __init__(self, at, parts, slots, send, recv, staged=None, loads=None):
        super().__init__(at, parts.shape[1:], send, recv)
        self.parts, self.slots, self.staged, self.loads = parts, slots, staged, loads

    @staticmethod
    def scratch(n_seq, *block):
        return [pltpu.VMEM((2, n_seq // 2) + block, LOW)] + Ring.semaphores(n_seq)

    @staticmethod
    def staging(*block):
        return [pltpu.VMEM((2,) + block, LOW), pltpu.SemaphoreType.DMA((2, 2))]

    def there(self, t, d):
        return self.at.ring(self.steps - t if d == 0 else t - self.steps)

    def adds(self, t, h, d):
        return t > 1 or (t == 1 and self.opposite(h, d))

    def load(self, t, h, d):
        rows = self.rows(h)
        block = self.parts.at[self.there(t, d), rows]
        return pltpu.make_async_copy(block, self.staged.at[d, rows], self.loads.at[d, h])

    def load_all(self, t):
        if self.staged is not None:
            for h, d in self.pieces():
                if t < self.steps and self.adds(t, h, d):
                    self.load(t, h, d).start()
                elif t == self.steps and d == 0:
                    self.load(t, h, d).start()

    def step(self, t):
        if t == 0:
            self.load_all(1)
        for h, d in self.pieces():
            if t == 0 and not self.opposite(h, d):
                continue
            rows = self.rows(h)
            src = self.parts.at[self.there(t, d), rows]
            if self.adds(t, h, d):
                if self.staged is not None:
                    self.load(t, h, d).wait()
                    src = self.staged.at[d, rows]
                self.copies[(d, t - 1, h)].wait_recv()
                held = self.slots.at[d, t - 1, rows]
                held[...] = (held[...].astype(FULL) + src[...].astype(FULL)).astype(LOW)
                src = held
            self.go(src, self.slots.at[d, t, rows], d, t, h)
        if t > 0:
            self.load_all(t + 1)

    def finish(self, out):
        last = self.steps - 1
        if last == 0:
            self.load_all(1)
        for h in range(self.halves):
            rows = self.rows(h)
            if self.staged is None:
                total = self.parts[self.at.seq, rows].astype(FULL)
            else:
                self.load(self.steps, h, 0).wait()
                total = self.staged[0, rows].astype(FULL)
            for d in (0, 1):
                if last == 0 and not self.opposite(h, d):
                    continue
                self.copies[(d, last, h)].wait_recv()
                total = total + self.slots[d, last, rows].astype(FULL)
            out[rows] = total.astype(out.dtype)
        for copy in self.copies.values():
            copy.wait_send()


class Exchange:
    def __init__(self, me, ids, axis, packed, landing, send, recv, local):
        self.kept = pltpu.make_async_copy(packed.at[me], landing.at[me], local)
        self.copies = [
            remote(packed.at[one[axis]], landing.at[me], send.at[k], recv.at[k], one)
            for k, one in enumerate(ids)
        ]

    @staticmethod
    def scratch(n):
        return [pltpu.SemaphoreType.DMA((n - 1,)), pltpu.SemaphoreType.DMA((n - 1,))]

    def start(self):
        self.kept.start()
        for copy in self.copies:
            copy.start()

    def arrived(self):
        self.kept.wait()
        for copy in self.copies:
            copy.wait_recv()

    def finish(self):
        for copy in self.copies:
            copy.wait_send()


def seq_exchange(at, *refs):
    return Exchange(at.seq, at.seq_ids(), 1, *refs)


def dp_exchange(at, *refs):
    return Exchange(at.dp, at.dp_ids(), 0, *refs)


class DpGather:
    def __init__(self, at, own, everything, send, recv, local):
        self.kept = pltpu.make_async_copy(own, everything.at[at.dp], local)
        slot = everything.at[at.dp]
        self.out = [
            remote(own, slot, send.at[k], recv.at[k], one) for k, one in enumerate(at.chip_ids())
        ]
        base = at.chips - 1
        self.mate = remote(own, slot, send.at[base], recv.at[base], at.core_id())
        self.handed = []
        for k in range(1, at.chips):
            origin = 2 * lax.rem(at.chip + at.chips - k, at.chips) + at.core
            there = everything.at[origin]
            self.handed.append(
                remote(there, there, send.at[base + k], recv.at[base + k], at.core_id())
            )

    @staticmethod
    def scratch(n_dp):
        return [pltpu.SemaphoreType.DMA((n_dp - 1,)), pltpu.SemaphoreType.DMA((n_dp - 1,))]

    def start(self):
        for copy in self.out:
            copy.start()
        self.mate.start()
        self.kept.start()

    def hand(self):
        for copy, onward in zip(self.out, self.handed):
            copy.wait_recv()
            onward.start()

    def arrived(self):
        self.kept.wait()
        self.mate.wait_recv()
        for copy in self.handed:
            copy.wait_recv()

    def finish(self):
        for copy in self.out + [self.mate] + self.handed:
            copy.wait_send()


def add_rows(rows, chunk, one):
    def step(r, carry):
        one(pl.ds(pl.multiple_of(r * chunk, chunk), chunk))
        return carry

    lax.fori_loop(0, rows // chunk, step, 0)


def chunk_of(rows, columns):
    chunk = rows
    while chunk % 32 == 0 and chunk * columns > 65536:
        chunk //= 2
    return chunk


class DpScatter:
    def __init__(self, at, parts, core, other, send, recv):
        self.at, self.parts, self.core, self.other = at, parts, core, other
        self.send, self.recv = send, recv
        self.rows, self.columns = parts.shape[1], parts.shape[2]

    @staticmethod
    def scratch(n_dp, rows, columns):
        chips = n_dp // 2
        return [
            pltpu.VMEM((chips, rows, columns), LOW),
            pltpu.VMEM((max(chips - 1, 1), rows, columns), LOW),
            pltpu.SemaphoreType.DMA((2 * chips - 1,)),
            pltpu.SemaphoreType.DMA((2 * chips - 1,)),
        ]

    def to_core(self, k):
        at = self.at
        return remote(
            self.parts.at[2 * k + 1 - at.core],
            self.core.at[k],
            self.send.at[k],
            self.recv.at[k],
            at.core_id(),
        )

    def to_chip(self, k):
        at = self.at
        sem = at.chips + k - 1
        return remote(
            self.core.at[lax.rem(at.chip + k, at.chips)],
            self.other.at[k - 1],
            self.send.at[sem],
            self.recv.at[sem],
            at.chip_ids()[k - 1],
        )

    def start(self):
        for k in range(self.at.chips):
            self.to_core(k).start()

    def add_core(self, k):
        held = self.core.at[k]
        mine = self.parts.at[2 * k + self.at.core]

        def one(rows):
            held[rows] = (held[rows].astype(FULL) + mine[rows].astype(FULL)).astype(LOW)

        add_rows(self.rows, chunk_of(self.rows, self.columns), one)

    def across(self):
        at = self.at
        for k in range(1, at.chips):
            there = lax.rem(at.chip + k, at.chips)
            self.to_core(there).wait_recv()
            self.add_core(there)
            self.to_chip(k).start()

    def finish(self, out):
        at = self.at
        self.to_core(at.chip).wait_recv()
        for k in range(1, at.chips):
            self.to_chip(k).wait_recv()
        held = self.core.at[at.chip]
        mine = self.parts.at[2 * at.chip + at.core]

        def one(rows):
            total = held[rows].astype(FULL) + mine[rows].astype(FULL)
            for k in range(1, at.chips):
                total = total + self.other[k - 1, rows].astype(FULL)
            out[rows] = total.astype(out.dtype)

        add_rows(self.rows, chunk_of(self.rows, self.columns), one)
        for k in range(at.chips):
            self.to_core(k).wait_send()
        for k in range(1, at.chips):
            self.to_chip(k).wait_send()


def comm_params(number):
    return pltpu.CompilerParams(
        collective_id=number, has_side_effects=True, vmem_limit_bytes=VMEM_BYTES
    )


ANY = pl.BlockSpec(memory_space=pl.ANY)
VMEM = pl.BlockSpec(memory_space=pltpu.VMEM)


def shape_of(dims, kind):
    return jax.ShapeDtypeStruct(dims, kind)


class Refs:
    def __init__(self, names, refs):
        refs = list(refs)
        for name, count in names:
            taken, refs = refs[: max(count, 1)], refs[max(count, 1) :]
            setattr(self, name, taken if count else taken[0])


def run(kernel, name, number, ins, outs, scratch):
    names = [(key, 0) for key in ins] + [(key, 0) for key in outs]
    shapes = []
    for key, value in scratch.items():
        if isinstance(value, list):
            names.append((key, len(value)))
            shapes += value
        else:
            names.append((key, 0))
            shapes.append(value)
    found = pl.pallas_call(
        lambda *refs: kernel(Refs(names, refs)),
        name=name,
        out_shape=[shape for shape, _ in outs.values()],
        in_specs=[spec for _, spec in ins.values()],
        out_specs=[spec for _, spec in outs.values()],
        scratch_shapes=shapes,
        compiler_params=comm_params(number),
    )(*[array for array, _ in ins.values()])
    return dict(zip(outs, found))


def dma(*dims):
    return pltpu.SemaphoreType.DMA(dims)


def vm(kind, *dims):
    return pltpu.VMEM(dims, kind)


def lanes(rows):
    return lax.broadcasted_iota(jnp.int32, (rows, 2 * HEAD_DIM), 1)


def low_head(rows):
    return lanes(rows) < HEAD_DIM


def swapped(pair):
    half = HEAD_DIM // 2
    first = lax.rem(lanes(pair.shape[0]), HEAD_DIM) < half
    return jnp.where(
        first, pltpu.roll(pair, 2 * HEAD_DIM - half, 1), pltpu.roll(pair, half, 1)
    )


def split_heads(pair):
    wide = pair.astype(FULL)
    low = low_head(pair.shape[0])
    return jnp.concatenate(
        [jnp.where(low, wide, 0.0), jnp.where(low, 0.0, wide)], 0
    ).astype(LOW)


def join_heads(both):
    rows = both.shape[0] // 2
    return jnp.where(low_head(rows), both[:rows], both[rows:])


def spread_kv(kv):
    wide = kv.astype(FULL)
    turned = pltpu.roll(wide, HEAD_DIM, 1)
    low = low_head(kv.shape[0])
    return jnp.where(low, wide, turned).astype(LOW), jnp.where(low, turned, wide).astype(LOW)


def mask_of(position, start, length):
    key = lax.broadcasted_iota(jnp.int32, (start.shape[0], length), 1)
    return jnp.where((key <= position) & (key >= start), 0.0, MASK_VALUE)


def own_positions(at, tok):
    return at.seq * tok + lax.broadcasted_iota(jnp.int32, (tok, 1), 0)


def rows_of(r, count):
    return pl.ds(pl.multiple_of(r * count, count), count)


def interleave(ring, jobs):
    jobs = list(jobs)
    for t in range(1, ring.steps):
        if jobs:
            jobs.pop(0)()
        ring.step(t)
    for job in jobs:
        job()


def front_kernel(n_dp, n_seq, own_ff, ff, m):
    at = Where(n_dp, n_seq)
    tok, width = m.x.shape
    q_width = m.q.shape[1]
    groups = q_width // (2 * HEAD_DIM)
    rank = n_seq * m.pq.shape[1]
    length = n_seq * tok
    greet(at.seq_ids() + at.dp_ids())
    swap_q = dp_exchange(at, m.pq, m.landed, *m.swap_q_sem, m.local.at[0])
    x_g = DpGather(at, m.x, m.xs, *m.x_sem, m.local.at[1])
    row_x = seq_exchange(at, m.seg_rows, m.seg_row, *m.row_x_sem, m.local.at[2])
    row_g = DpGather(at, m.seg_row, m.segs, *m.row_g_sem, m.local.at[3])
    col_g = DpGather(at, m.seg_col, m.seg_cols, *m.col_g_sem, m.local.at[4])
    ring_q = RingGather(at, m.landed, m.wq_all, *m.ring_q_sem, m.local.at[5])
    ring_o = RingGather(at, m.wo, m.wo_all, *m.ring_o_sem, m.local.at[6])
    ring_kv = RingGather(at, m.kv_own, m.kv_all, *m.ring_kv_sem, m.local.at[7])
    swap_gu = seq_exchange(at, m.pgu, m.gu, *m.swap_gu_sem, m.local.at[8])
    down = DpGather(at, m.wd, m.wd_all, *m.down_sem, m.local.at[9])
    stores = []

    def store(src, dst):
        copy = pltpu.make_async_copy(src, dst, m.local.at[10 + len(stores)])
        copy.start()
        stores.append(copy)

    swap_q.start()
    x_g.start()
    row_x.start()
    col_g.start()

    def pack(weight, first):
        if ff > own_ff:
            m.pgu[:, :, first : first + n_dp * ff] = jnp.zeros(
                m.pgu.shape[:2] + (n_dp * ff,), LOW
            )
        for s in range(n_seq):
            for i in range(n_dp):
                piece = weight[:, (i * n_seq + s) * own_ff : (i * n_seq + s + 1) * own_ff]
                m.pgu[s, :, first + i * ff : first + i * ff + own_ff] = (
                    m.gain[:, :1] * piece.astype(FULL)
                ).astype(LOW)

    swap_q.arrived()
    ring_q.step(0)
    down.start()
    row_x.arrived()
    row_g.start()

    def hand():
        x_g.hand()
        row_g.hand()
        col_g.hand()

    def norm():
        x_g.arrived()
        for r in range(n_dp):
            x = m.xs[r].astype(FULL)
            scale = lax.rsqrt(jnp.mean(x * x, -1, keepdims=True) + EPS)
            m.n1[r] = (x * scale).astype(LOW)
        store(m.n1, m.n1_out)

    def place():
        row_g.arrived()
        col_g.arrived()
        position = own_positions(at, tok)
        first = lax.rem(lanes(tok), HEAD_DIM) < HEAD_DIM // 2
        for r in range(n_dp):
            segs = jnp.concatenate([m.segs[r, s, :1] for s in range(n_seq)], 1)
            own = m.seg_cols[r][:, :1]
            start = jnp.sum((segs < own).astype(jnp.int32), 1, keepdims=True)
            turned = (position - start).astype(FULL) * m.freqs[:1]
            rows = slice(r * tok, (r + 1) * tok)
            m.cos[rows] = jnp.cos(turned)
            sines = jnp.sin(turned)
            m.sin[rows] = jnp.where(first, -sines, sines)
            m.starts[rows] = jnp.broadcast_to(start, (tok, 2 * HEAD_DIM))
        store(m.cos, m.cos_out)
        store(m.sin, m.sin_out)
        store(m.starts, m.starts_out)

    interleave(
        ring_q,
        [lambda: pack(m.wg, 0), hand, norm, place, lambda: pack(m.wu, n_dp * ff)],
    )
    ring_q.finish()
    ring_o.step(0)
    store(m.wq_all, m.wq_out)

    m.qkv[...] = sum(
        matmul(
            m.n1[:, :, i * rank : (i + 1) * rank].reshape(n_dp * tok, rank),
            m.wq_all[:, i].reshape(rank, q_width + 2 * HEAD_DIM),
        )
        for i in range(n_dp)
    )
    factor = HEAD_DIM ** (-0.5)
    for g in range(groups + 1):
        cols = slice(g * 2 * HEAD_DIM, (g + 1) * 2 * HEAD_DIM)
        pair = m.qkv[:, cols]
        turned = pair * m.cos[...] + swapped(pair) * m.sin[...]
        if g < groups:
            m.q[:, cols] = (turned * factor).astype(LOW)
        else:
            m.kv_own[...] = jnp.where(low_head(pair.shape[0]), turned, pair).astype(LOW)
    ring_kv.step(0)
    store(m.q, m.q_out)
    ring_o.step(1)
    for t in range(1, ring_kv.steps):
        ring_kv.step(t)
    down.hand()
    ring_kv.finish()
    store(m.kv_all, m.kv_out)
    swap_gu.start()

    later = list(range(2, ring_o.steps))
    for r in range(n_dp):
        rows = slice(r * tok, (r + 1) * tok)
        k, v = spread_kv(m.kv_all[:, rows].reshape(length, 2 * HEAD_DIM))
        m.k2[...] = k
        m.v2[...] = v
        m.mask[...] = mask_of(own_positions(at, tok), m.starts[rows, :1], length)

        def group(g, carry):
            cols = rows_of(g, 2 * HEAD_DIM)
            raw = matmul_nt(split_heads(m.q[rows, cols]), m.k2[...])
            raw = raw + jnp.concatenate([m.mask[...]] * 2, 0)
            top = jnp.max(raw, -1, keepdims=True)
            probs = jnp.exp(raw - top)
            total = jnp.sum(probs, -1, keepdims=True)
            probs = (probs * (1.0 / total)).astype(LOW)
            m.o[rows, cols] = join_heads(matmul(probs, m.v2[...])).astype(LOW)
            m.lse[r * groups + g] = top + jnp.log(total)
            return carry

        lax.fori_loop(0, groups, group, 0)
        if later:
            ring_o.step(later.pop(0))
    for t in later:
        ring_o.step(t)
    store(m.o, m.o_out)
    store(m.lse, m.lse_out)
    ring_o.finish()
    store(m.wo_all, m.wo_out)
    full = m.wo_all[...].reshape(q_width, width)
    for r in range(n_dp):
        m.parts[r] = matmul(m.o[r * tok : (r + 1) * tok], full).astype(LOW)
    back = DpScatter(at, m.parts, *m.back)
    back.start()
    back.across()
    back.finish(m.middle)
    middle = m.x[...].astype(FULL) + m.middle[...]
    m.middle[...] = middle
    scale = lax.rsqrt(jnp.mean(middle * middle, -1, keepdims=True) + EPS)
    m.second[...] = (middle * scale).astype(LOW)
    swap_gu.arrived()
    down.arrived()
    for one in (swap_q, x_g, row_x, row_g, col_g, swap_gu, down):
        one.finish()
    for copy in stores:
        copy.wait()


def front(n_dp, n_seq, own_ff, x, seg_rows, seg_col, freqs, pq, wg, wu, gain, wo, wd):
    tok, width = x.shape
    rank, columns = pq.shape[1:]
    q_width = columns - 2 * HEAD_DIM
    groups = q_width // (2 * HEAD_DIM)
    pair = 2 * HEAD_DIM
    length = n_seq * tok
    every = n_dp * tok
    ff = wd.shape[0]
    gu_width = 2 * n_dp * ff
    ins = {
        "x": x, "seg_rows": seg_rows, "seg_col": seg_col, "freqs": freqs, "pq": pq, "wg": wg, "wu": wu, "gain": gain, "wo": wo,
    }
    ins = {key: (value, VMEM) for key, value in ins.items()}
    ins["wd"] = (wd, ANY)
    kept = {
        "n1": (LOW, n_dp, tok, width),
        "q": (LOW, every, q_width),
        "kv_all": (LOW, n_seq, every, pair),
        "o": (LOW, every, q_width),
        "lse": (FULL, n_dp * groups, 2 * tok, 1),
        "cos": (FULL, every, pair),
        "sin": (FULL, every, pair),
        "starts": (jnp.int32, every, pair),
        "wq_all": (LOW, n_seq, n_dp, rank, columns),
        "wo_all": (LOW, n_seq, rank, width),
    }
    outs = {
        key.replace("_all", "") + "_out": (shape_of(dims[1:], dims[0]), ANY)
        for key, dims in kept.items()
    }
    outs["gu"] = (shape_of((n_seq, rank, gu_width), LOW), ANY)
    outs["wd_all"] = (shape_of((n_dp,) + wd.shape, LOW), ANY)
    outs["middle"] = (shape_of((tok, width), FULL), VMEM)
    outs["second"] = (shape_of((tok, width), LOW), VMEM)
    scratch = {key: vm(*dims) for key, dims in kept.items()}
    scratch |= {
        "landed": vm(LOW, n_dp, rank, columns),
        "xs": vm(LOW, n_dp, tok, width),
        "seg_row": vm(jnp.int32, n_seq, 8, tok),
        "segs": vm(jnp.int32, n_dp, n_seq, 8, tok),
        "seg_cols": vm(jnp.int32, n_dp, tok, pair),
        "kv_own": vm(LOW, every, pair),
        "mask": vm(FULL, tok, length),
        "pgu": vm(LOW, n_seq, rank, gu_width),
        "qkv": vm(FULL, every, columns),
        "k2": vm(LOW, length, pair),
        "v2": vm(LOW, length, pair),
        "parts": vm(LOW, n_dp, tok, width),
        "back": DpScatter.scratch(n_dp, tok, width),
        "local": dma(10 + len(kept)),
        "swap_q_sem": Exchange.scratch(n_dp),
        "x_sem": DpGather.scratch(n_dp),
        "row_x_sem": Exchange.scratch(n_seq),
        "row_g_sem": DpGather.scratch(n_dp),
        "col_g_sem": DpGather.scratch(n_dp),
        "ring_q_sem": Ring.semaphores(n_seq),
        "ring_o_sem": Ring.semaphores(n_seq),
        "ring_kv_sem": Ring.semaphores(n_seq),
        "swap_gu_sem": Exchange.scratch(n_seq),
        "down_sem": DpGather.scratch(n_dp),
    }
    return run(
        functools.partial(front_kernel, n_dp, n_seq, own_ff, ff), "attention_forward", 1, ins, outs, scratch
    )


def feed_kernel(n_dp, n_seq, m):
    at = Where(n_dp, n_seq)
    tok, width = m.second.shape
    wide = m.wgu.shape[2]
    part = wide // 2
    rank = width // n_dp
    length = n_seq * tok
    greet(at.ring_ids() + at.dp_ids())
    gu = DpGather(at, m.gu, m.wgu, *m.gu_sem, m.local.at[0])
    ring_n = RingGather(at, m.second, m.second_all, *m.ring_n, m.local.at[1])
    ring_dy = RingGather(at, m.dy, m.dy_all, *m.ring_dy, m.local.at[2])
    ring_h = RingScatter(at, m.part, *m.ring_h)
    side = DpScatter(at, m.wgu, *m.side)
    down = DpScatter(at, m.wd, *m.down)
    gu.start()
    held = pltpu.make_async_copy(m.wd_all, m.wd, m.local.at[3])
    held.start()
    ring_n.step(0)
    for t in range(1, ring_n.steps):
        ring_n.step(t)
    ring_dy.step(0)
    gu.hand()
    ring_n.finish()
    gu.arrived()
    held.wait()
    stores = []

    def forward(c):
        blocks = slice(2 * c, 2 * c + 2)
        normed = m.second_all[blocks].reshape(2 * tok, width)
        both = matmul(normed, m.wgu[...].reshape(width, wide))
        gate, upward = both[:, :part], both[:, part:]
        sigma = jax.nn.sigmoid(gate)
        silu = gate * sigma
        hidden = (silu * upward).astype(LOW)
        m.by_up[blocks] = silu.reshape(2, tok, part)
        m.by_gate[blocks] = (upward * sigma * (1.0 + gate * (1.0 - sigma))).reshape(2, tok, part)
        m.hidden[blocks] = hidden.reshape(2, tok, part)
        out = matmul(hidden, m.wd[...].reshape(part, width))
        m.part[blocks] = out.astype(LOW).reshape(2, tok, width)
        copy = pltpu.make_async_copy(m.part.at[blocks], m.part_y.at[blocks], m.store.at[c])
        copy.start()
        stores.append(copy)

    def backward(blocks):
        rows = len(blocks) * tok
        dy = jnp.concatenate([m.dy_all[b] for b in blocks], 0)
        grad = matmul_nt(dy, m.wd[...].reshape(part, width))
        for k, b in enumerate(blocks):
            one = grad[k * tok : (k + 1) * tok]
            m.grads[b, :, :part] = (one * m.by_gate[b]).astype(LOW)
            m.grads[b, :, part:] = (one * m.by_up[b]).astype(LOW)
        both = jnp.concatenate([m.grads[b] for b in blocks], 0)
        for i in range(n_dp):
            cols = slice(i * rank, (i + 1) * rank)
            out = matmul_nt(both, m.wgu[i]).astype(LOW)
            for k, b in enumerate(blocks):
                m.part[b, :, cols] = out[k * tok : (k + 1) * tok]

    jobs = [functools.partial(forward, c) for c in range(n_seq // 2)]

    def stored():
        for copy in stores:
            copy.wait()

    jobs.append(stored)
    jobs.append(lambda: backward([at.seq]))
    for t in range(1, ring_dy.steps):
        for _ in range(2):
            if jobs:
                jobs.pop(0)()
        ring_dy.step(t)
        if t < ring_dy.steps - 1:
            jobs.append(functools.partial(backward, [at.ring(-t), at.ring(t)]))
    for job in jobs:
        job()
    if ring_dy.steps > 1:
        ring_dy.rest(ring_dy.steps - 2)
        backward([at.ring(1 - ring_dy.steps), at.ring(ring_dy.steps - 1)])
    ring_dy.finish()
    backward([at.ring(ring_dy.steps)])
    gu.finish()

    ring_h.step(0)
    grads = m.grads[...].reshape(length, wide)

    def grad_gu(k):
        chip = lax.rem(at.chip + 1 + k, at.chips)
        for c in (0, 1):
            normed = m.second_all[:, :, rows_of(2 * chip + c, rank)].reshape(length, rank)
            m.wgu[2 * chip + c] = matmul_tn(normed, m.grads[...].reshape(length, wide)).astype(LOW)
        side.to_core(chip).start()

    def grad_down():
        step = width // n_dp
        for i in range(n_dp):
            cols = slice(i * step, (i + 1) * step)
            dy = m.dy_all[:, :, cols].reshape(length, step)
            m.wd[:, :, cols] = (
                matmul_tn(m.hidden[...].reshape(length, part), dy)
                .astype(LOW)
                .reshape(m.wd.shape[:2] + (step,))
            )
        down.start()

    jobs = [functools.partial(grad_gu, 0)]
    jobs += [functools.partial(grad_gu, k) for k in range(1, at.chips)]
    jobs.insert(max(len(jobs) - 1, 1), side.across)
    jobs.append(grad_down)
    jobs.append(down.across)
    per = -(-len(jobs) // (ring_h.steps))
    for t in range(1, ring_h.steps):
        for _ in range(per):
            if jobs:
                jobs.pop(0)()
        ring_h.step(t)
    for job in jobs:
        job()
    ring_h.finish(m.grad_h)
    side.finish(m.fin)
    down.finish(m.grad_d)


def feed(n_dp, n_seq, second, dy, gu, wd):
    tok, width = second.shape
    deep, wide = gu.shape
    ff = wd.shape[1]
    part = wide // 2
    ins = {"second": (second, ANY), "dy": (dy, ANY), "gu": (gu, ANY), "wd_all": (wd, ANY)}
    outs = {
        "part_y": (shape_of((n_seq, tok, width), LOW), ANY),
        "grad_h": (shape_of((tok, width), FULL), VMEM),
        "fin": (shape_of((deep, wide), LOW), VMEM),
        "grad_d": (shape_of((ff, width), FULL), VMEM),
    }
    scratch = {
        "local": dma(4),
        "wd": vm(LOW, *wd.shape),
        "store": dma(n_seq // 2),
        "second_all": vm(LOW, n_seq, tok, width),
        "dy_all": vm(LOW, n_seq, tok, width),
        "wgu": vm(LOW, n_dp, deep, wide),
        "by_gate": vm(FULL, n_seq, tok, part),
        "by_up": vm(FULL, n_seq, tok, part),
        "hidden": vm(LOW, n_seq, tok, part),
        "grads": vm(LOW, n_seq, tok, wide),
        "part": vm(LOW, n_seq, tok, width),
        "gu_sem": DpGather.scratch(n_dp),
        "ring_n": Ring.semaphores(n_seq),
        "ring_dy": Ring.semaphores(n_seq),
        "ring_h": RingScatter.scratch(n_seq, tok, width),
        "side": DpScatter.scratch(n_dp, deep, wide),
        "down": DpScatter.scratch(n_dp, ff, width),
    }
    return run(functools.partial(feed_kernel, n_dp, n_seq), "feed_forward", 2, ins, outs, scratch)


def back_kernel(n_dp, n_seq, own_ff, ff, m):
    at = Where(n_dp, n_seq)
    tok, width = m.x.shape
    q_width = m.q.shape[1]
    groups = q_width // (2 * HEAD_DIM)
    rank = n_seq * m.wq.shape[2]
    length = n_seq * tok
    pair = 2 * HEAD_DIM
    greet(at.seq_ids() + at.dp_ids())
    swap_gu = [
        remote(m.fin.at[one[1]], m.got_gu.at[at.seq], m.swap_gu[0].at[k], m.swap_gu[1].at[k], one)
        for k, one in enumerate(at.seq_ids())
    ]
    ring_y = RingScatter(at, m.part_y, *m.ring_y, *m.staged)
    d_g = DpGather(at, m.d_own, m.d_all, *m.d_sem, m.local.at[0])
    ring_kv = RingScatter(at, m.part_kv, *m.ring_kv)
    ring_q = RingScatter(at, m.part_q, *m.ring_q)
    ring_o = RingScatter(at, m.part_o, *m.ring_o)
    back = DpScatter(at, m.d_all, *m.back)
    swap_q = dp_exchange(at, m.sum_q, m.got_q, *m.swap_q, m.local.at[1])
    def norm_back(grad, value):
        scale = lax.rsqrt(jnp.mean(value * value, -1, keepdims=True) + EPS)
        normed = value * scale
        return scale * (grad - normed * jnp.mean(grad * normed, -1, keepdims=True))

    m.dmid[...] = m.dy[...].astype(FULL) + norm_back(m.grad_h[...], m.middle[...])
    m.d_own[...] = m.dmid[...].astype(LOW)
    d_g.start()
    ring_y.step(0)
    d_g.hand()
    d_g.arrived()
    m.do[...] = matmul_nt(
        m.d_all[...].reshape(n_dp * tok, width), m.wo[...].reshape(q_width, width)
    ).astype(LOW)
    later = list(range(1, ring_y.steps))

    def load_kv(r):
        block = m.kv.at[:, pl.ds(r * tok, tok)]
        return pltpu.make_async_copy(block, m.kv_row.at[r % 2], m.load.at[r % 2])

    load_kv(0).start()
    for r in range(n_dp):
        rows = slice(r * tok, (r + 1) * tok)
        load_kv(r).wait()
        if r + 1 < n_dp:
            load_kv(r + 1).start()
        k, v = spread_kv(m.kv_row[r % 2].reshape(length, pair))
        m.k2[...] = k
        m.v2[...] = v
        m.mask[...] = mask_of(own_positions(at, tok), m.starts[rows, :1], length)
        m.dk2[...] = jnp.zeros_like(m.dk2)
        m.dv2[...] = jnp.zeros_like(m.dv2)

        def group(g, carry):
            cols = rows_of(g, pair)
            q2 = split_heads(m.q[rows, cols])
            do2 = split_heads(m.do[rows, cols])
            raw = matmul_nt(q2, m.k2[...])
            raw = raw + jnp.concatenate([m.mask[...]] * 2, 0)
            probs = jnp.exp(raw - m.lse[r * groups + g])
            grad_probs = matmul_nt(do2, m.v2[...])
            delta = jnp.sum(probs * grad_probs, -1, keepdims=True)
            grad_raw = (probs * (grad_probs - delta)).astype(LOW)
            m.dq[rows, cols] = join_heads(matmul(grad_raw, m.k2[...]))
            m.dk2[...] += matmul_tn(grad_raw, q2)
            m.dv2[...] += matmul_tn(probs.astype(LOW), do2)
            return carry

        lax.fori_loop(0, groups, group, 0)
        dk = m.dk2[...]
        dv = m.dv2[...]
        dkv = jnp.where(
            low_head(length), dk + pltpu.roll(dk, HEAD_DIM, 1), dv + pltpu.roll(dv, HEAD_DIM, 1)
        )
        m.part_kv[:, rows] = dkv.astype(LOW).reshape(n_seq, tok, pair)
        if later:
            ring_y.step(later.pop(0))
    for t in later:
        ring_y.step(t)
    ring_kv.step(0)
    m.part_o[...] = (
        matmul_tn(m.o[...], m.d_all[...].reshape(n_dp * tok, width))
        .astype(LOW)
        .reshape(m.part_o.shape)
    )
    d_g.finish()
    for t in range(1, ring_kv.steps):
        ring_kv.step(t)
    ring_kv.finish(m.dkv)
    ring_y.finish(m.wide)
    for copy in swap_gu:
        copy.start()
    n1 = m.ring_y[0].at[0, pl.ds(0, n_dp)]
    fetch = pltpu.make_async_copy(m.n1, n1, m.local.at[2])
    fetch.start()
    ring_o.step(0)
    m.out[...] = (m.middle[...] + m.wide[...]).astype(m.out.dtype)
    factor = HEAD_DIM ** (-0.5)
    for g in range(groups + 1):
        cols = slice(g * pair, (g + 1) * pair)
        grad = m.dq[:, cols] * factor if g < groups else m.dkv[...]
        turned = grad * m.cos[...] - swapped(grad) * m.sin[...]
        if g == groups:
            turned = jnp.where(low_head(grad.shape[0]), turned, grad)
        m.dqkv[:, cols] = turned.astype(LOW)
    for i in range(n_dp):
        cols = slice(i * rank, (i + 1) * rank)
        weight = m.wq[:, i].reshape(rank, q_width + pair)
        m.d_all[:, :, cols] = (
            matmul_nt(m.dqkv[...], weight).astype(LOW).reshape(n_dp, tok, rank)
        )
    back.start()
    fetch.wait()
    for i in range(n_dp):
        cols = slice(i * rank, (i + 1) * rank)
        m.part_q[:, i] = (
            matmul_tn(n1[:, :, cols].reshape(n_dp * tok, rank), m.dqkv[...]).astype(LOW).reshape(n_seq, rank // n_seq, q_width + pair)
        )
    ring_q.step(0)
    back.across()
    for t in range(1, ring_q.steps):
        ring_q.step(t)
        ring_o.step(t)
    back.finish(m.wide)
    m.grad_x[...] = m.dmid[...] + norm_back(m.wide[...], m.x[...].astype(FULL))
    ring_q.finish(m.sum_q)
    swap_q.start()
    ring_o.finish(m.grad_o)
    for copy in swap_gu:
        copy.wait()
    m.got_gu[at.seq] = m.fin[at.seq]
    gain = m.gain[:, :1]
    gain_grad = jnp.zeros(gain.shape, FULL)
    for weight, grad, first in ((m.wg, m.grad_g, 0), (m.wu, m.grad_u, n_dp * ff)):
        for s in range(n_seq):
            for i in range(n_dp):
                raw = m.got_gu[s, :, first + i * ff : first + i * ff + own_ff].astype(FULL)
                cols = slice((i * n_seq + s) * own_ff, (i * n_seq + s + 1) * own_ff)
                gain_grad += jnp.sum(weight[:, cols].astype(FULL) * raw, 1, keepdims=True)
                grad[:, cols] = gain * raw
    m.grad_gain[...] = jnp.broadcast_to(gain_grad, m.grad_gain.shape)
    swap_q.arrived()
    swap_q.finish()


def back(n_dp, n_seq, own_ff, ff, dtype, ins):
    tok, width = ins["x"].shape
    every = n_dp * tok
    q_width = ins["q"].shape[1]
    pair = 2 * HEAD_DIM
    length = n_seq * tok
    rank, columns = ins["wq"].shape[2:]
    outs = {
        "out": (shape_of((tok, width), dtype), VMEM),
        "grad_x": (shape_of((tok, width), FULL), VMEM),
        "grad_o": (shape_of((rank, width), FULL), VMEM),
        "got_q": (shape_of((n_dp, rank, columns), LOW), ANY),
        "grad_g": (shape_of(ins["wg"].shape, FULL), VMEM),
        "grad_u": (shape_of(ins["wg"].shape, FULL), VMEM),
        "grad_gain": (shape_of((rank, pair), FULL), VMEM),
    }
    scratch = {
        "local": dma(3),
        "load": dma(2),
        "kv_row": vm(LOW, 2, n_seq, tok, pair),
        "dmid": vm(FULL, tok, width),
        "d_own": vm(LOW, tok, width),
        "d_all": vm(LOW, n_dp, tok, width),
        "d_sem": DpGather.scratch(n_dp),
        "do": vm(LOW, every, q_width),
        "k2": vm(LOW, length, pair),
        "v2": vm(LOW, length, pair),
        "mask": vm(FULL, tok, length),
        "dk2": vm(FULL, length, pair),
        "dv2": vm(FULL, length, pair),
        "dq": vm(FULL, every, q_width),
        "dkv": vm(FULL, every, pair),
        "dqkv": vm(LOW, every, columns),
        "wide": vm(FULL, tok, width),
        "sum_q": vm(LOW, n_dp, rank, columns),
        "part_kv": vm(LOW, n_seq, every, pair),
        "part_q": vm(LOW, n_seq, n_dp, rank, columns),
        "part_o": vm(LOW, n_seq, rank, width),
        "back": DpScatter.scratch(n_dp, tok, width),
        "ring_y": RingScatter.scratch(n_seq, tok, width),
        "staged": RingScatter.staging(tok, width),
        "ring_kv": RingScatter.scratch(n_seq, every, pair),
        "ring_q": RingScatter.scratch(n_seq, n_dp, rank, columns),
        "ring_o": RingScatter.scratch(n_seq, rank, width),
        "swap_q": Exchange.scratch(n_dp),
        "swap_gu": Exchange.scratch(n_seq),
        "got_gu": vm(LOW, *ins["fin"].shape),
    }
    return run(
        functools.partial(back_kernel, n_dp, n_seq, own_ff, ff),
        "attention_backward",
        3,
        {key: (value, ANY if key in ("part_y", "n1", "kv") else VMEM) for key, value in ins.items()},
        outs,
        scratch,
    )


def body(
    n_dp,
    n_seq,
    tokens,
    segment_ids,
    gain_attn,
    w_query,
    w_key,
    w_value,
    w_output,
    gain_mlp,
    w_gate,
    w_up,
    w_down,
    cotangent,
):
    local, width = tokens.shape[1], tokens.shape[2]
    length = n_seq * local
    own_rows = w_query.shape[0]
    own_ff = w_down.shape[0]
    ff = -(-own_ff // 16) * 16
    heads = HEADS // n_dp
    q_width = heads * HEAD_DIM
    x_own = tokens.reshape(local, width)
    dy_own = cotangent.reshape(local, width)

    gain_one = gain_attn.astype(FULL)[:, None]
    gain_two = jnp.broadcast_to(gain_mlp.astype(FULL)[:, None], (own_rows, 2 * HEAD_DIM))
    kv_of = [i * heads // GROUP for i in range(n_dp)]

    def gained(weight):
        return (gain_one * weight.astype(FULL)).astype(LOW)

    pack_q = jnp.stack(
        [
            jnp.concatenate(
                [
                    gained(w_query[:, i * q_width : (i + 1) * q_width]),
                    gained(w_key[:, kv * HEAD_DIM : (kv + 1) * HEAD_DIM]),
                    gained(w_value[:, kv * HEAD_DIM : (kv + 1) * HEAD_DIM]),
                ],
                1,
            )
            for i, kv in enumerate(kv_of)
        ]
    )
    freqs = ROPE_BASE ** (-jnp.arange(0, HEAD_DIM, 2).astype(FULL) / HEAD_DIM)
    ids = segment_ids.reshape(local)
    pair = 2 * HEAD_DIM
    got = front(
        n_dp,
        n_seq,
        own_ff,
        x_own,
        jnp.broadcast_to(ids, (n_seq, 8, local)),
        jnp.broadcast_to(ids[:, None], (local, pair)),
        jnp.broadcast_to(jnp.tile(freqs, 4), (8, pair)),
        pack_q,
        w_gate,
        w_up,
        gain_two,
        w_output,
        jnp.pad(w_down, ((0, ff - own_ff), (0, 0))),
    )
    fed = feed(
        n_dp,
        n_seq,
        got["second"],
        dy_own,
        got["gu"].reshape(n_seq * own_rows, 2 * n_dp * ff),
        got["wd_all"],
    )
    ins = {
        "part_y": fed["part_y"],
        "grad_h": fed["grad_h"],
        "fin": fed["fin"].reshape(got["gu"].shape),
        "wg": w_gate,
        "wu": w_up,
        "gain": gain_two,
        "x": x_own,
        "dy": dy_own,
        "middle": got["middle"],
    }
    for name in ("n1", "q", "kv", "o", "lse", "cos", "sin", "starts", "wq", "wo"):
        ins[name] = got[name + "_out"]
    done = back(n_dp, n_seq, own_ff, ff, tokens.dtype, ins)
    got_q = done["got_q"]
    raw_query = jnp.concatenate([got_q[i, :, :q_width] for i in range(n_dp)], 1).astype(FULL)

    def kv_join(first):
        terms = [got_q[i, :, first : first + HEAD_DIM].astype(FULL) for i in range(n_dp)]
        return jnp.concatenate(
            [
                sum(term for term, kv in zip(terms, kv_of) if kv == head)
                for head in range(KV_HEADS)
            ],
            1,
        )

    raw_key = kv_join(q_width)
    raw_value = kv_join(q_width + HEAD_DIM)

    def gain_grad(*pairs):
        return sum(jnp.sum(weight.astype(FULL) * raw, 1) for weight, raw in pairs)

    return (
        done["out"].reshape(tokens.shape),
        done["grad_x"].reshape(tokens.shape),
        gain_grad((w_query, raw_query), (w_key, raw_key), (w_value, raw_value)),
        gain_one * raw_query,
        gain_one * raw_key,
        gain_one * raw_value,
        done["grad_o"],
        done["grad_gain"][:, 0],
        done["grad_g"],
        done["grad_u"],
        fed["grad_d"][:own_ff],
    )


def solution(mesh):
    rows = P(("dp", "seq"), None)
    vector = P(("dp", "seq"))
    row = P("dp", "seq", None)
    return jax.shard_map(
        functools.partial(body, mesh.shape["dp"], mesh.shape["seq"]),
        mesh=mesh,
        in_specs=(row, P("dp", "seq"), vector, rows, rows, rows, rows, vector, rows, rows, rows, row),
        out_specs=(row, row, vector, rows, rows, rows, rows, vector, rows, rows, rows),
        check_vma=False,
    )
```

```python
import functools

import jax
import jax.numpy as jnp
from jax import lax
from jax.experimental import pallas as pl
from jax.experimental.pallas import tpu as pltpu
from jax.sharding import PartitionSpec as P

HEADS = 32
HEAD_DIM = 64
KV_HEADS = 4
GROUP = HEADS // KV_HEADS

EPS = 1e-05
ROPE_BASE = 10000.0
MASK_VALUE = -1e30
MESH = pl.DeviceIdType.MESH
LOW = jnp.bfloat16
FULL = jnp.float32
VMEM_BYTES = 60 * 1024 * 1024


def matmul(left, right):
    return jnp.dot(left, right, preferred_element_type=FULL)


def matmul_nt(left, right):
    return lax.dot_general(left, right, (((1,), (1,)), ((), ())), preferred_element_type=FULL)


def matmul_tn(left, right):
    return lax.dot_general(left, right, (((0,), (0,)), ((), ())), preferred_element_type=FULL)


def ring_at(place, n):
    upper = lax.div(place, n // 2)
    return (1 - upper) * 2 * place + upper * (2 * (n - place) - 1)


def ring_place(index, n):
    odd = lax.rem(index, 2)
    return (1 - odd) * lax.div(index, 2) + odd * (n - lax.div(index + 1, 2))


class Where:
    def __init__(self, n_dp, n_seq):
        self.n_dp, self.n_seq = n_dp, n_seq
        self.chips = n_dp // 2
        self.dp = lax.axis_index("dp")
        self.seq = lax.axis_index("seq")
        self.core = lax.rem(self.dp, 2)
        self.chip = lax.div(self.dp, 2)
        self.place = ring_place(self.seq, n_seq)

    def ring(self, step):
        return ring_at(lax.rem(self.place + step + self.n_seq, self.n_seq), self.n_seq)

    def ring_ids(self):
        return [(self.dp, self.ring(1)), (self.dp, self.ring(-1))]

    def seq_ids(self):
        return [
            (self.dp, lax.rem(self.seq + k, self.n_seq)) for k in range(1, self.n_seq)
        ]

    def dp_ids(self):
        return [(lax.rem(self.dp + k, self.n_dp), self.seq) for k in range(1, self.n_dp)]

    def core_id(self):
        return (self.dp + 1 - 2 * self.core, self.seq)

    def chip_ids(self):
        return [
            (2 * lax.rem(self.chip + k, self.chips) + self.core, self.seq)
            for k in range(1, self.chips)
        ]


def greet(ids):
    barrier = pltpu.get_barrier_semaphore()
    for one in ids:
        pl.semaphore_signal(barrier, inc=1, device_id=one, device_id_type=MESH)
    pl.semaphore_wait(barrier, len(ids))


def remote(src, dst, send, recv, target):
    return pltpu.make_async_remote_copy(
        src_ref=src,
        dst_ref=dst,
        send_sem=send,
        recv_sem=recv,
        device_id=target,
        device_id_type=MESH,
    )


class Ring:
    def __init__(self, at, shape, send, recv):
        self.at, self.send, self.recv = at, send, recv
        self.steps = at.n_seq // 2
        self.halves = 2 if len(shape) > 2 or shape[0] % 32 == 0 else 1
        self.half = shape[0] // self.halves
        self.copies = {}

    @staticmethod
    def semaphores(n_seq):
        shape = (2, n_seq // 2, 2)
        return [pltpu.SemaphoreType.DMA(shape), pltpu.SemaphoreType.DMA(shape)]

    def opposite(self, h, d):
        return d == h if self.halves == 2 else d == 0

    def rows(self, h):
        return pl.ds(h * self.half, self.half)

    def go(self, src, dst, d, t, h):
        target = self.at.ring_ids()[d]
        copy = remote(src, dst, self.send.at[d, t, h], self.recv.at[d, t, h], target)
        copy.start()
        self.copies[(d, t, h)] = copy

    def pieces(self):
        return [(h, d) for h in range(self.halves) for d in (0, 1)]


class RingGather(Ring):
    def __init__(self, at, own, everything, send, recv, local):
        super().__init__(at, own.shape, send, recv)
        self.own, self.everything = own, everything
        self.kept = pltpu.make_async_copy(own, everything.at[at.seq], local)
        self.waited = set()

    @staticmethod
    def scratch(n_seq):
        return Ring.semaphores(n_seq)

    def wait(self, key):
        self.copies[key].wait_recv()
        self.waited.add(key)

    def step(self, t):
        if t == 0:
            self.kept.start()
        if t == 1:
            self.kept.wait()
        for h, d in self.pieces():
            if t == self.steps - 1 and not self.opposite(h, d):
                continue
            if t > 0:
                self.wait((d, t - 1, h))
            origin = self.at.ring(-t if d == 0 else t)
            dst = self.everything.at[origin, self.rows(h)]
            self.go(self.own.at[self.rows(h)] if t == 0 else dst, dst, d, t, h)

    def rest(self, t):
        for key in self.copies:
            if key not in self.waited and key[1] <= t:
                self.wait(key)

    def finish(self):
        self.rest(self.steps)
        for copy in self.copies.values():
            copy.wait_send()
        if self.steps == 1:
            self.kept.wait()


class RingScatter(Ring):
    def __init__(self, at, parts, slots, send, recv, staged=None, loads=None):
        super().__init__(at, parts.shape[1:], send, recv)
        self.parts, self.slots, self.staged, self.loads = parts, slots, staged, loads

    @staticmethod
    def scratch(n_seq, *block):
        return [pltpu.VMEM((2, n_seq // 2) + block, LOW)] + Ring.semaphores(n_seq)

    @staticmethod
    def staging(*block):
        return [pltpu.VMEM((2,) + block, LOW), pltpu.SemaphoreType.DMA((2, 2))]

    def there(self, t, d):
        return self.at.ring(self.steps - t if d == 0 else t - self.steps)

    def adds(self, t, h, d):
        return t > 1 or (t == 1 and self.opposite(h, d))

    def load(self, t, h, d):
        rows = self.rows(h)
        block = self.parts.at[self.there(t, d), rows]
        return pltpu.make_async_copy(block, self.staged.at[d, rows], self.loads.at[d, h])

    def load_all(self, t):
        if self.staged is not None:
            for h, d in self.pieces():
                if t < self.steps and self.adds(t, h, d):
                    self.load(t, h, d).start()
                elif t == self.steps and d == 0:
                    self.load(t, h, d).start()

    def early(self):
        for h, d in self.pieces():
            if self.steps > 1 and not self.opposite(h, d):
                block = self.parts.at[self.there(1, d), self.rows(h)]
                self.go(block, self.slots.at[d, 1, self.rows(h)], d, 1, h)

    def step(self, t):
        if t == 0:
            self.load_all(1)
        for h, d in self.pieces():
            if (t == 0 and not self.opposite(h, d)) or (d, t, h) in self.copies:
                continue
            rows = self.rows(h)
            src = self.parts.at[self.there(t, d), rows]
            if self.adds(t, h, d):
                if self.staged is not None:
                    self.load(t, h, d).wait()
                    src = self.staged.at[d, rows]
                self.copies[(d, t - 1, h)].wait_recv()
                held = self.slots.at[d, t - 1, rows]
                held[...] = (held[...].astype(FULL) + src[...].astype(FULL)).astype(LOW)
                src = held
            self.go(src, self.slots.at[d, t, rows], d, t, h)
        if t > 0:
            self.load_all(t + 1)

    def finish(self, out):
        last = self.steps - 1
        if last == 0:
            self.load_all(1)
        for h in range(self.halves):
            rows = self.rows(h)
            if self.staged is None:
                total = self.parts[self.at.seq, rows].astype(FULL)
            else:
                self.load(self.steps, h, 0).wait()
                total = self.staged[0, rows].astype(FULL)
            for d in (0, 1):
                if last == 0 and not self.opposite(h, d):
                    continue
                self.copies[(d, last, h)].wait_recv()
                total = total + self.slots[d, last, rows].astype(FULL)
            out[rows] = total.astype(out.dtype)
        for copy in self.copies.values():
            copy.wait_send()


class Exchange:
    def __init__(self, me, ids, axis, packed, landing, send, recv, local):
        self.kept = pltpu.make_async_copy(packed.at[me], landing.at[me], local)
        self.copies = [
            remote(packed.at[one[axis]], landing.at[me], send.at[k], recv.at[k], one)
            for k, one in enumerate(ids)
        ]

    @staticmethod
    def scratch(n):
        return [pltpu.SemaphoreType.DMA((n - 1,)), pltpu.SemaphoreType.DMA((n - 1,))]

    def start(self):
        self.kept.start()
        for copy in self.copies:
            copy.start()

    def arrived(self):
        self.kept.wait()
        for copy in self.copies:
            copy.wait_recv()

    def finish(self):
        for copy in self.copies:
            copy.wait_send()


def seq_exchange(at, *refs):
    return Exchange(at.seq, at.seq_ids(), 1, *refs)


def dp_exchange(at, *refs):
    return Exchange(at.dp, at.dp_ids(), 0, *refs)


class DpGather:
    def __init__(self, at, own, everything, send, recv, local):
        self.kept = pltpu.make_async_copy(own, everything.at[at.dp], local)
        slot = everything.at[at.dp]
        self.out = [
            remote(own, slot, send.at[k], recv.at[k], one) for k, one in enumerate(at.chip_ids())
        ]
        base = at.chips - 1
        self.mate = remote(own, slot, send.at[base], recv.at[base], at.core_id())
        self.handed = []
        for k in range(1, at.chips):
            origin = 2 * lax.rem(at.chip + at.chips - k, at.chips) + at.core
            there = everything.at[origin]
            self.handed.append(
                remote(there, there, send.at[base + k], recv.at[base + k], at.core_id())
            )

    @staticmethod
    def scratch(n_dp):
        return [pltpu.SemaphoreType.DMA((n_dp - 1,)), pltpu.SemaphoreType.DMA((n_dp - 1,))]

    def start(self):
        for copy in self.out:
            copy.start()
        self.mate.start()
        self.kept.start()

    def hand(self):
        for copy, onward in zip(self.out, self.handed):
            copy.wait_recv()
            onward.start()

    def arrived(self):
        self.kept.wait()
        self.mate.wait_recv()
        for copy in self.handed:
            copy.wait_recv()

    def finish(self):
        for copy in self.out + [self.mate] + self.handed:
            copy.wait_send()


def add_rows(rows, chunk, one):
    def step(r, carry):
        one(pl.ds(pl.multiple_of(r * chunk, chunk), chunk))
        return carry

    lax.fori_loop(0, rows // chunk, step, 0)


def chunk_of(rows, columns):
    chunk = rows
    while chunk % 32 == 0 and chunk * columns > 65536:
        chunk //= 2
    return chunk


class DpScatter:
    def __init__(self, at, parts, core, other, send, recv):
        self.at, self.parts, self.core, self.other = at, parts, core, other
        self.send, self.recv = send, recv
        self.rows, self.columns = parts.shape[1], parts.shape[2]

    @staticmethod
    def scratch(n_dp, rows, columns):
        chips = n_dp // 2
        return [
            pltpu.VMEM((chips, rows, columns), LOW),
            pltpu.VMEM((max(chips - 1, 1), rows, columns), LOW),
            pltpu.SemaphoreType.DMA((2 * chips - 1,)),
            pltpu.SemaphoreType.DMA((2 * chips - 1,)),
        ]

    def to_core(self, k):
        at = self.at
        return remote(
            self.parts.at[2 * k + 1 - at.core],
            self.core.at[k],
            self.send.at[k],
            self.recv.at[k],
            at.core_id(),
        )

    def to_chip(self, k):
        at = self.at
        sem = at.chips + k - 1
        return remote(
            self.core.at[lax.rem(at.chip + k, at.chips)],
            self.other.at[k - 1],
            self.send.at[sem],
            self.recv.at[sem],
            at.chip_ids()[k - 1],
        )

    def start(self):
        for k in range(self.at.chips):
            self.to_core(k).start()

    def add_core(self, k):
        held = self.core.at[k]
        mine = self.parts.at[2 * k + self.at.core]

        def one(rows):
            held[rows] = (held[rows].astype(FULL) + mine[rows].astype(FULL)).astype(LOW)

        add_rows(self.rows, chunk_of(self.rows, self.columns), one)

    def across(self):
        at = self.at
        for k in range(1, at.chips):
            there = lax.rem(at.chip + k, at.chips)
            self.to_core(there).wait_recv()
            self.add_core(there)
            self.to_chip(k).start()

    def finish(self, out):
        at = self.at
        self.to_core(at.chip).wait_recv()
        for k in range(1, at.chips):
            self.to_chip(k).wait_recv()
        held = self.core.at[at.chip]
        mine = self.parts.at[2 * at.chip + at.core]

        def one(rows):
            total = held[rows].astype(FULL) + mine[rows].astype(FULL)
            for k in range(1, at.chips):
                total = total + self.other[k - 1, rows].astype(FULL)
            out[rows] = total.astype(out.dtype)

        add_rows(self.rows, chunk_of(self.rows, self.columns), one)
        for k in range(at.chips):
            self.to_core(k).wait_send()
        for k in range(1, at.chips):
            self.to_chip(k).wait_send()


def comm_params(number):
    return pltpu.CompilerParams(
        collective_id=number, has_side_effects=True, vmem_limit_bytes=VMEM_BYTES
    )


ANY = pl.BlockSpec(memory_space=pl.ANY)
VMEM = pl.BlockSpec(memory_space=pltpu.VMEM)


def shape_of(dims, kind):
    return jax.ShapeDtypeStruct(dims, kind)


class Refs:
    def __init__(self, names, refs):
        refs = list(refs)
        for name, count in names:
            taken, refs = refs[: max(count, 1)], refs[max(count, 1) :]
            setattr(self, name, taken if count else taken[0])


def run(kernel, name, number, ins, outs, scratch):
    names = [(key, 0) for key in ins] + [(key, 0) for key in outs]
    shapes = []
    for key, value in scratch.items():
        if isinstance(value, list):
            names.append((key, len(value)))
            shapes += value
        else:
            names.append((key, 0))
            shapes.append(value)
    found = pl.pallas_call(
        lambda *refs: kernel(Refs(names, refs)),
        name=name,
        out_shape=[shape for shape, _ in outs.values()],
        in_specs=[spec for _, spec in ins.values()],
        out_specs=[spec for _, spec in outs.values()],
        scratch_shapes=shapes,
        compiler_params=comm_params(number),
    )(*[array for array, _ in ins.values()])
    return dict(zip(outs, found))


def dma(*dims):
    return pltpu.SemaphoreType.DMA(dims)


def vm(kind, *dims):
    return pltpu.VMEM(dims, kind)


def lanes(rows):
    return lax.broadcasted_iota(jnp.int32, (rows, 2 * HEAD_DIM), 1)


def low_head(rows):
    return lanes(rows) < HEAD_DIM


def swapped(pair):
    half = HEAD_DIM // 2
    first = lax.rem(lanes(pair.shape[0]), HEAD_DIM) < half
    return jnp.where(
        first, pltpu.roll(pair, 2 * HEAD_DIM - half, 1), pltpu.roll(pair, half, 1)
    )


def split_heads(pair):
    wide = pair.astype(FULL)
    low = low_head(pair.shape[0])
    return jnp.concatenate(
        [jnp.where(low, wide, 0.0), jnp.where(low, 0.0, wide)], 0
    ).astype(LOW)


def join_heads(both):
    rows = both.shape[0] // 2
    return jnp.where(low_head(rows), both[:rows], both[rows:])


def spread_kv(kv):
    wide = kv.astype(FULL)
    turned = pltpu.roll(wide, HEAD_DIM, 1)
    low = low_head(kv.shape[0])
    return jnp.where(low, wide, turned).astype(LOW), jnp.where(low, turned, wide).astype(LOW)


def mask_of(position, start, length):
    key = lax.broadcasted_iota(jnp.int32, (start.shape[0], length), 1)
    return jnp.where((key <= position) & (key >= start), 0.0, MASK_VALUE)


def own_positions(at, tok):
    return at.seq * tok + lax.broadcasted_iota(jnp.int32, (tok, 1), 0)


def rows_of(r, count):
    return pl.ds(pl.multiple_of(r * count, count), count)


def to_column(row):
    n = row.shape[1]
    here = lax.broadcasted_iota(jnp.int32, (n, n), 0) == lax.broadcasted_iota(jnp.int32, (n, n), 1)
    return jnp.sum(jnp.where(here, row.astype(FULL), 0.0), 1, keepdims=True)


def front_kernel(n_dp, n_seq, own_ff, ff, kv_of, m):
    at = Where(n_dp, n_seq)
    tok, width = m.x.shape
    q_width = m.q.shape[1]
    groups = q_width // (2 * HEAD_DIM)
    rank = n_seq * m.pq.shape[1]
    length = n_seq * tok
    greet(at.seq_ids() + at.dp_ids())
    swap_q = dp_exchange(at, m.pq, m.landed, *m.swap_q_sem, m.local.at[0])
    x_g = DpGather(at, m.x, m.xs, *m.x_sem, m.local.at[1])
    row_x = seq_exchange(at, m.seg_rows, m.seg_row, *m.row_x_sem, m.local.at[2])
    row_g = DpGather(at, m.seg_row, m.segs, *m.row_g_sem, m.local.at[3])
    col_g = DpGather(at, m.seg_col, m.seg_cols, *m.col_g_sem, m.local.at[4])
    ring_q = RingGather(at, m.landed, m.wq_all, *m.ring_q_sem, m.local.at[5])
    ring_o = RingGather(at, m.wo, m.wo_all, *m.ring_o_sem, m.local.at[6])
    ring_kv = RingGather(at, m.kv_own, m.kv_all, *m.ring_kv_sem, m.local.at[7])
    swap_gu = seq_exchange(at, m.pgu, m.gu, *m.swap_gu_sem, m.local.at[8])
    down = DpGather(at, m.wd, m.wd_all, *m.down_sem, m.local.at[9])
    loads = [
        pltpu.make_async_copy(src, dst, m.load.at[k])
        for k, (src, dst) in enumerate(((m.wg_in, m.wg), (m.wu_in, m.wu), (m.x, m.x_own)))
    ]
    stores = []

    def store(src, dst):
        copy = pltpu.make_async_copy(src, dst, m.local.at[10 + len(stores)])
        copy.start()
        stores.append(copy)

    ring_o.step(0)
    for copy in loads:
        copy.start()

    gain = to_column(m.gain_one[...])
    for i, kv in enumerate(kv_of):
        m.pq[i, :, :q_width] = (
            gain * m.wq[:, i * q_width : (i + 1) * q_width].astype(FULL)
        ).astype(LOW)
        for weight, first in ((m.wk, q_width), (m.wv, q_width + HEAD_DIM)):
            m.pq[i, :, first : first + HEAD_DIM] = (
                gain * weight[:, kv * HEAD_DIM : (kv + 1) * HEAD_DIM].astype(FULL)
            ).astype(LOW)
    swap_q.start()
    x_g.start()
    ids = m.ids[...]
    m.seg_rows[...] = jnp.broadcast_to(ids[None], m.seg_rows.shape)
    m.seg_col[...] = jnp.broadcast_to(to_column(ids).astype(jnp.int32), m.seg_col.shape)
    row_x.start()
    col_g.start()

    def pack(k, weight, first):
        loads[k].wait()
        scale = to_column(m.gain_two[...])
        if ff > own_ff:
            m.pgu[:, :, first : first + n_dp * ff] = jnp.zeros(
                m.pgu.shape[:2] + (n_dp * ff,), LOW
            )
        for s in range(n_seq):
            for i in range(n_dp):
                piece = weight[:, (i * n_seq + s) * own_ff : (i * n_seq + s + 1) * own_ff]
                m.pgu[s, :, first + i * ff : first + i * ff + own_ff] = (
                    scale * piece.astype(FULL)
                ).astype(LOW)

    swap_q.arrived()
    ring_q.step(0)
    row_x.arrived()
    row_g.start()

    def hand():
        x_g.hand()
        row_g.hand()
        col_g.hand()
        down.start()

    def norm():
        x_g.arrived()
        for r in range(n_dp):
            x = m.xs[r].astype(FULL)
            scale = lax.rsqrt(jnp.mean(x * x, -1, keepdims=True) + EPS)
            m.n1[r] = (x * scale).astype(LOW)
        store(m.n1, m.n1_out)

    def place():
        row_g.arrived()
        col_g.arrived()
        position = own_positions(at, tok)
        first = lax.rem(lanes(tok), HEAD_DIM) < HEAD_DIM // 2
        for r in range(n_dp):
            segs = jnp.concatenate([m.segs[r, s, :1] for s in range(n_seq)], 1)
            own = m.seg_cols[r][:, :1]
            start = jnp.sum((segs < own).astype(jnp.int32), 1, keepdims=True)
            turned = (position - start).astype(FULL) * m.freqs[:1]
            rows = slice(r * tok, (r + 1) * tok)
            m.cos[rows] = jnp.cos(turned)
            sines = jnp.sin(turned)
            m.sin[rows] = jnp.where(first, -sines, sines)
            m.starts[rows] = jnp.broadcast_to(start, (tok, 2 * HEAD_DIM))
        store(m.cos, m.cos_out)
        store(m.sin, m.sin_out)
        store(m.starts, m.starts_out)

    pack(0, m.wg, 0)
    ring_q.step(1)
    hand()
    jobs = [lambda: (norm(), place()), lambda: pack(1, m.wu, n_dp * ff)]
    for t in range(2, ring_q.steps):
        ring_q.step(t)
        if jobs:
            jobs.pop(0)()
    for job in jobs:
        job()
    ring_q.finish()
    ring_o.step(1)
    store(m.wq_all, m.wq_out)

    m.qkv[...] = sum(
        matmul(
            m.n1[:, :, i * rank : (i + 1) * rank].reshape(n_dp * tok, rank),
            m.wq_all[:, i].reshape(rank, q_width + 2 * HEAD_DIM),
        )
        for i in range(n_dp)
    )
    factor = HEAD_DIM ** (-0.5)
    for g in range(groups + 1):
        cols = slice(g * 2 * HEAD_DIM, (g + 1) * 2 * HEAD_DIM)
        pair = m.qkv[:, cols]
        turned = pair * m.cos[...] + swapped(pair) * m.sin[...]
        if g < groups:
            m.q[:, cols] = (turned * factor).astype(LOW)
        else:
            m.kv_own[...] = jnp.where(low_head(pair.shape[0]), turned, pair).astype(LOW)
    ring_kv.step(0)
    store(m.q, m.q_out)
    for t in range(1, ring_kv.steps):
        ring_kv.step(t)
    down.hand()
    ring_kv.finish()
    store(m.kv_all, m.kv_out)
    later = list(range(2, ring_o.steps))
    ring_o.step(later.pop(0))
    m.lse[...] = jnp.zeros_like(m.lse)
    for r in range(n_dp):
        rows = slice(r * tok, (r + 1) * tok)
        k, v = spread_kv(m.kv_all[:, rows].reshape(length, 2 * HEAD_DIM))
        m.k2[...] = k
        m.v2[...] = v
        m.mask[...] = mask_of(own_positions(at, tok), m.starts[rows, :1], length)

        def group(g, carry):
            cols = rows_of(g, 2 * HEAD_DIM)
            raw = matmul_nt(split_heads(m.q[rows, cols]), m.k2[...])
            raw = raw + jnp.concatenate([m.mask[...]] * 2, 0)
            top = jnp.max(raw, -1, keepdims=True)
            probs = jnp.exp(raw - top)
            total = jnp.sum(probs, -1, keepdims=True)
            probs = (probs * (1.0 / total)).astype(LOW)
            m.o[rows, cols] = join_heads(matmul(probs, m.v2[...])).astype(LOW)
            here = lanes(2 * tok) == r * groups + g
            m.lse[...] = jnp.where(here, top + jnp.log(total), m.lse[...])
            return carry

        lax.fori_loop(0, groups, group, 0)
        if later and r % 2:
            ring_o.step(later.pop(0))
            if not later:
                swap_gu.start()
    for t in later:
        ring_o.step(t)
    if later:
        swap_gu.start()
    store(m.o, m.o_out)
    store(m.lse, m.lse_out)
    ring_o.finish()
    store(m.wo_all, m.wo_out)
    full = m.wo_all[...].reshape(q_width, width)
    for r in range(n_dp):
        m.parts[r] = matmul(m.o[r * tok : (r + 1) * tok], full).astype(LOW)
    back = DpScatter(at, m.parts, *m.back)
    back.start()
    back.across()
    back.finish(m.middle)
    loads[2].wait()
    middle = m.x_own[...].astype(FULL) + m.middle[...]
    m.middle[...] = middle
    scale = lax.rsqrt(jnp.mean(middle * middle, -1, keepdims=True) + EPS)
    m.second[...] = (middle * scale).astype(LOW)
    swap_gu.arrived()
    down.arrived()
    for one in (swap_q, x_g, row_x, row_g, col_g, swap_gu, down):
        one.finish()
    for copy in stores:
        copy.wait()


def front(n_dp, n_seq, own_ff, kv_of, held, small):
    tok, width = held["x"].shape
    rank = small["wq"].shape[0]
    q_width = width // n_dp
    groups = q_width // (2 * HEAD_DIM)
    pair = 2 * HEAD_DIM
    columns = q_width + pair
    length = n_seq * tok
    every = n_dp * tok
    wd = held["wd"]
    ff = wd.shape[0]
    gu_width = 2 * n_dp * ff
    ins = {key: (value, ANY) for key, value in held.items()}
    ins |= {key: (value, VMEM) for key, value in small.items()}
    kept = {
        "n1": (LOW, n_dp, tok, width),
        "q": (LOW, every, q_width),
        "kv_all": (LOW, n_seq, every, pair),
        "o": (LOW, every, q_width),
        "lse": (FULL, 2 * tok, pair),
        "cos": (FULL, every, pair),
        "sin": (FULL, every, pair),
        "starts": (jnp.int32, every, pair),
        "wq_all": (LOW, n_seq, n_dp, rank, columns),
        "wo_all": (LOW, n_seq, rank, width),
    }
    outs = {
        key.replace("_all", "") + "_out": (shape_of(dims[1:], dims[0]), ANY)
        for key, dims in kept.items()
    }
    outs["gu"] = (shape_of((n_seq, rank, gu_width), LOW), ANY)
    outs["wd_all"] = (shape_of((n_dp,) + wd.shape, LOW), ANY)
    outs["middle"] = (shape_of((tok, width), FULL), VMEM)
    outs["second"] = (shape_of((tok, width), LOW), VMEM)
    scratch = {key: vm(*dims) for key, dims in kept.items()}
    scratch |= {
        "load": dma(3),
        "wg": vm(LOW, *held["wg_in"].shape),
        "wu": vm(LOW, *held["wg_in"].shape),
        "x_own": vm(LOW, tok, width),
        "pq": vm(LOW, n_dp, rank, columns),
        "seg_rows": vm(jnp.int32, n_seq, 8, tok),
        "seg_col": vm(jnp.int32, tok, pair),
        "landed": vm(LOW, n_dp, rank, columns),
        "xs": vm(LOW, n_dp, tok, width),
        "seg_row": vm(jnp.int32, n_seq, 8, tok),
        "segs": vm(jnp.int32, n_dp, n_seq, 8, tok),
        "seg_cols": vm(jnp.int32, n_dp, tok, pair),
        "kv_own": vm(LOW, every, pair),
        "mask": vm(FULL, tok, length),
        "pgu": vm(LOW, n_seq, rank, gu_width),
        "qkv": vm(FULL, every, columns),
        "k2": vm(LOW, length, pair),
        "v2": vm(LOW, length, pair),
        "parts": vm(LOW, n_dp, tok, width),
        "back": DpScatter.scratch(n_dp, tok, width),
        "local": dma(10 + len(kept)),
        "swap_q_sem": Exchange.scratch(n_dp),
        "x_sem": DpGather.scratch(n_dp),
        "row_x_sem": Exchange.scratch(n_seq),
        "row_g_sem": DpGather.scratch(n_dp),
        "col_g_sem": DpGather.scratch(n_dp),
        "ring_q_sem": Ring.semaphores(n_seq),
        "ring_o_sem": Ring.semaphores(n_seq),
        "ring_kv_sem": Ring.semaphores(n_seq),
        "swap_gu_sem": Exchange.scratch(n_seq),
        "down_sem": DpGather.scratch(n_dp),
    }
    return run(
        functools.partial(front_kernel, n_dp, n_seq, own_ff, ff, kv_of), "attention_forward", 1, ins, outs, scratch
    )


def feed_kernel(n_dp, n_seq, m):
    at = Where(n_dp, n_seq)
    tok, width = m.second.shape
    wide = m.wgu.shape[2]
    part = wide // 2
    rank = width // n_dp
    length = n_seq * tok
    greet(at.ring_ids() + at.dp_ids())
    gu = DpGather(at, m.gu, m.wgu, *m.gu_sem, m.local.at[0])
    ring_n = RingGather(at, m.second, m.second_all, *m.ring_n, m.local.at[1])
    ring_dy = RingGather(at, m.dy, m.dy_all, *m.ring_dy, m.local.at[2])
    ring_h = RingScatter(at, m.part, *m.ring_h)
    side = DpScatter(at, m.wgu, *m.side)
    gu.start()
    held = pltpu.make_async_copy(m.wd_all, m.wd, m.local.at[3])
    held.start()
    ring_n.step(0)
    for t in range(1, ring_n.steps):
        ring_n.step(t)
    ring_dy.step(0)
    gu.hand()
    ring_n.finish()
    gu.arrived()
    held.wait()
    stores = []

    def stored():
        while stores:
            stores.pop().wait()

    def forward(c):
        blocks = slice(2 * c, 2 * c + 2)
        normed = m.second_all[blocks].reshape(2 * tok, width)
        both = matmul(normed, m.wgu[...].reshape(width, wide))
        gate, upward = both[:, :part], both[:, part:]
        sigma = jax.nn.sigmoid(gate)
        silu = gate * sigma
        hidden = (silu * upward).astype(LOW)
        m.by_up[blocks] = silu.reshape(2, tok, part)
        m.by_gate[blocks] = (upward * sigma * (1.0 + gate * (1.0 - sigma))).reshape(2, tok, part)
        m.hidden[blocks] = hidden.reshape(2, tok, part)
        out = matmul(hidden, m.wd[...].reshape(part, width))
        m.part[blocks] = out.astype(LOW).reshape(2, tok, width)
        copy = pltpu.make_async_copy(m.part.at[blocks], m.part_y.at[blocks], m.store.at[c])
        copy.start()
        stores.append(copy)

    def backward(blocks):
        rows = len(blocks) * tok
        dy = jnp.concatenate([m.dy_all[b] for b in blocks], 0)
        grad = matmul_nt(dy, m.wd[...].reshape(part, width))
        for k, b in enumerate(blocks):
            one = grad[k * tok : (k + 1) * tok]
            m.grads[b, :, :part] = (one * m.by_gate[b]).astype(LOW)
            m.grads[b, :, part:] = (one * m.by_up[b]).astype(LOW)
        both = jnp.concatenate([m.grads[b] for b in blocks], 0)
        for i in range(n_dp):
            cols = slice(i * rank, (i + 1) * rank)
            out = matmul_nt(both, m.wgu[i]).astype(LOW)
            for k, b in enumerate(blocks):
                m.part[b, :, cols] = out[k * tok : (k + 1) * tok]

    jobs = [functools.partial(forward, c) for c in range(n_seq // 2)]
    jobs.append(stored)
    jobs.append(lambda: backward([at.seq]))
    for t in range(1, ring_dy.steps):
        for _ in range(2):
            if jobs:
                jobs.pop(0)()
        ring_dy.step(t)
        if t < ring_dy.steps - 1:
            jobs.append(functools.partial(backward, [at.ring(-t), at.ring(t)]))
    for job in jobs:
        job()
    if ring_dy.steps > 1:
        ring_dy.rest(ring_dy.steps - 2)
        backward([at.ring(1 - ring_dy.steps), at.ring(ring_dy.steps - 1)])
    ring_h.early()
    ring_dy.finish()
    backward([at.ring(ring_dy.steps)])
    gu.finish()

    ring_h.step(0)

    def grad_gu(k):
        chip = lax.rem(at.chip + 1 + k, at.chips)
        for c in (0, 1):
            normed = m.second_all[:, :, rows_of(2 * chip + c, rank)].reshape(length, rank)
            m.wgu[2 * chip + c] = matmul_tn(normed, m.grads[...].reshape(length, wide)).astype(LOW)
        side.to_core(chip).start()

    def grad_down():
        step = width // n_dp
        for i in range(n_dp):
            cols = slice(i * step, (i + 1) * step)
            dy = m.dy_all[:, :, cols].reshape(length, step)
            m.wd[:, :, cols] = (
                matmul_tn(m.hidden[...].reshape(length, part), dy)
                .astype(LOW)
                .reshape(m.wd.shape[:2] + (step,))
            )
        held = pltpu.make_async_copy(m.wd, m.grad_d, m.local.at[3])
        held.start()
        stores.append(held)

    jobs = [functools.partial(grad_gu, 0)]
    jobs += [functools.partial(grad_gu, k) for k in range(1, at.chips)]
    jobs.insert(max(len(jobs) - 1, 1), side.across)
    jobs.append(grad_down)
    per = -(-len(jobs) // (ring_h.steps))
    for t in range(1, ring_h.steps):
        for _ in range(per):
            if jobs:
                jobs.pop(0)()
        ring_h.step(t)
    for job in jobs:
        job()
    ring_h.finish(m.grad_h)
    side.finish(m.fin)
    stored()


def feed(n_dp, n_seq, second, dy, gu, wd):
    tok, width = second.shape
    deep, wide = gu.shape
    ff = wd.shape[1]
    part = wide // 2
    ins = {"second": (second, ANY), "dy": (dy, ANY), "gu": (gu, ANY), "wd_all": (wd, ANY)}
    outs = {
        "part_y": (shape_of((n_seq, tok, width), LOW), ANY),
        "grad_h": (shape_of((tok, width), FULL), VMEM),
        "fin": (shape_of((deep, wide), LOW), VMEM),
        "grad_d": (shape_of(wd.shape, LOW), ANY),
    }
    scratch = {
        "local": dma(4),
        "wd": vm(LOW, *wd.shape),
        "store": dma(n_seq // 2),
        "second_all": vm(LOW, n_seq, tok, width),
        "dy_all": vm(LOW, n_seq, tok, width),
        "wgu": vm(LOW, n_dp, deep, wide),
        "by_gate": vm(FULL, n_seq, tok, part),
        "by_up": vm(FULL, n_seq, tok, part),
        "hidden": vm(LOW, n_seq, tok, part),
        "grads": vm(LOW, n_seq, tok, wide),
        "part": vm(LOW, n_seq, tok, width),
        "gu_sem": DpGather.scratch(n_dp),
        "ring_n": Ring.semaphores(n_seq),
        "ring_dy": Ring.semaphores(n_seq),
        "ring_h": RingScatter.scratch(n_seq, tok, width),
        "side": DpScatter.scratch(n_dp, deep, wide),
    }
    return run(functools.partial(feed_kernel, n_dp, n_seq), "feed_forward", 2, ins, outs, scratch)


def back_kernel(n_dp, n_seq, own_ff, ff, kv_of, m):
    at = Where(n_dp, n_seq)
    tok, width = m.x.shape
    q_width = m.q.shape[1]
    groups = q_width // (2 * HEAD_DIM)
    rank = n_seq * m.wq.shape[2]
    length = n_seq * tok
    pair = 2 * HEAD_DIM
    greet(at.seq_ids() + at.dp_ids())
    swap_gu = [
        remote(m.fin.at[one[1]], m.got_gu.at[at.seq], m.swap_gu[0].at[k], m.swap_gu[1].at[k], one)
        for k, one in enumerate(at.seq_ids())
    ]
    ring_y = RingScatter(at, m.part_y, *m.ring_y, *m.staged)
    d_g = DpGather(at, m.d_own, m.d_all, *m.d_sem, m.local.at[0])
    ring_kv = RingScatter(at, m.part_kv, *m.ring_kv)
    ring_q = RingScatter(at, m.part_q, *m.ring_q)
    ring_o = RingScatter(at, m.part_o, *m.ring_o)
    down = DpScatter(at, m.part_d, *m.down)
    back = DpScatter(at, m.d_all, *m.back)
    swap_q = dp_exchange(at, m.sum_q, m.got_q, *m.swap_q, m.local.at[1])
    ring_y.step(0)
    loads = [
        pltpu.make_async_copy(getattr(m, key + "_in"), getattr(m, key), m.load.at[2 + k])
        for k, key in enumerate(LOADED)
    ]
    for copy in loads:
        copy.start()

    def load_kv(r):
        block = m.kv.at[:, pl.ds(r * tok, tok)]
        return pltpu.make_async_copy(block, m.kv_row.at[r % 2], m.load.at[r % 2])

    load_kv(0).start()

    def norm_back(grad, value):
        scale = lax.rsqrt(jnp.mean(value * value, -1, keepdims=True) + EPS)
        normed = value * scale
        return scale * (grad - normed * jnp.mean(grad * normed, -1, keepdims=True))

    m.dmid[...] = m.dy[...].astype(FULL) + norm_back(m.grad_h[...], m.middle[...])
    m.d_own[...] = m.dmid[...].astype(LOW)
    d_g.start()
    if ring_y.steps > 1:
        ring_y.step(1)
    d_g.hand()
    for copy in loads:
        copy.wait()
    d_g.arrived()
    down.start()
    m.do[...] = matmul_nt(
        m.d_all[...].reshape(n_dp * tok, width), m.wo[...].reshape(q_width, width)
    ).astype(LOW)
    later = list(range(2, ring_y.steps))
    if later:
        ring_y.step(later.pop(0))
    down.across()
    for r in range(n_dp):
        rows = slice(r * tok, (r + 1) * tok)
        load_kv(r).wait()
        if r + 1 < n_dp:
            load_kv(r + 1).start()
        k, v = spread_kv(m.kv_row[r % 2].reshape(length, pair))
        m.k2[...] = k
        m.v2[...] = v
        m.mask[...] = mask_of(own_positions(at, tok), m.starts[rows, :1], length)
        m.dk2[...] = jnp.zeros_like(m.dk2)
        m.dv2[...] = jnp.zeros_like(m.dv2)

        def group(g, carry):
            cols = rows_of(g, pair)
            q2 = split_heads(m.q[rows, cols])
            do2 = split_heads(m.do[rows, cols])
            raw = matmul_nt(q2, m.k2[...])
            raw = raw + jnp.concatenate([m.mask[...]] * 2, 0)
            here = lanes(2 * tok) == r * groups + g
            lse = jnp.sum(jnp.where(here, m.lse[...], 0.0), 1, keepdims=True)
            probs = jnp.exp(raw - lse)
            grad_probs = matmul_nt(do2, m.v2[...])
            delta = jnp.sum(probs * grad_probs, -1, keepdims=True)
            grad_raw = (probs * (grad_probs - delta)).astype(LOW)
            m.dq[rows, cols] = join_heads(matmul(grad_raw, m.k2[...]))
            m.dk2[...] += matmul_tn(grad_raw, q2)
            m.dv2[...] += matmul_tn(probs.astype(LOW), do2)
            return carry

        lax.fori_loop(0, groups, group, 0)
        dk = m.dk2[...]
        dv = m.dv2[...]
        dkv = jnp.where(
            low_head(length), dk + pltpu.roll(dk, HEAD_DIM, 1), dv + pltpu.roll(dv, HEAD_DIM, 1)
        )
        m.part_kv[:, rows] = dkv.astype(LOW).reshape(n_seq, tok, pair)
        if later and r % 2:
            ring_y.step(later.pop(0))
    for t in later:
        ring_y.step(t)
    ring_kv.step(0)
    m.part_o[...] = (
        matmul_tn(m.o[...], m.d_all[...].reshape(n_dp * tok, width))
        .astype(LOW)
        .reshape(m.part_o.shape)
    )
    d_g.finish()
    for t in range(1, ring_kv.steps):
        ring_kv.step(t)
    ring_kv.finish(m.dkv)
    ring_o.step(0)
    waiting = list(swap_gu)

    def pace(count=1):
        for copy in waiting[:count]:
            copy.start()
        del waiting[:count]

    factor = HEAD_DIM ** (-0.5)
    for g in range(groups + 1):
        cols = slice(g * pair, (g + 1) * pair)
        grad = m.dq[:, cols] * factor if g < groups else m.dkv[...]
        turned = grad * m.cos[...] - swapped(grad) * m.sin[...]
        if g == groups:
            turned = jnp.where(low_head(grad.shape[0]), turned, grad)
        m.dqkv[:, cols] = turned.astype(LOW)
    for i in range(n_dp):
        cols = slice(i * rank, (i + 1) * rank)
        weight = m.wq[:, i].reshape(rank, q_width + pair)
        m.d_all[:, :, cols] = (
            matmul_nt(m.dqkv[...], weight).astype(LOW).reshape(n_dp, tok, rank)
        )
    back.start()
    pace(2)
    ring_y.finish(m.wide)
    n1 = m.ring_y[0].at[0, pl.ds(0, n_dp)]
    fetch = pltpu.make_async_copy(m.n1, n1, m.local.at[2])
    fetch.start()
    m.out[...] = (m.middle[...] + m.wide[...]).astype(m.out.dtype)
    down.finish(m.grad_d)
    back.across()
    pace()
    fetch.wait()
    for i in range(n_dp):
        cols = slice(i * rank, (i + 1) * rank)
        m.part_q[:, i] = (
            matmul_tn(n1[:, :, cols].reshape(n_dp * tok, rank), m.dqkv[...])
            .astype(LOW)
            .reshape(n_seq, rank // n_seq, q_width + pair)
        )
    ring_q.step(0)
    pace()
    if ring_o.steps > 1:
        ring_o.step(1)
    pace()
    back.finish(m.wide)
    pace(len(waiting))
    m.grad_x[...] = m.dmid[...] + norm_back(m.wide[...], m.x[...].astype(FULL))
    for t in range(2, ring_o.steps):
        ring_o.step(t)
    for copy in swap_gu:
        copy.wait()
    m.got_gu[at.seq] = m.fin[at.seq]

    def unpack(grad, first):
        for s in range(n_seq):
            for i in range(n_dp):
                grad[:, (i * n_seq + s) * own_ff : (i * n_seq + s + 1) * own_ff] = m.got_gu[
                    s, :, first + i * ff : first + i * ff + own_ff
                ]

    jobs = [lambda: unpack(m.grad_g, 0), lambda: unpack(m.grad_u, n_dp * ff)]
    for t in range(1, ring_q.steps):
        ring_q.step(t)
        if jobs:
            jobs.pop(0)()
    for job in jobs:
        job()
    ring_o.finish(m.grad_o)
    ring_q.finish(m.sum_q)
    swap_q.start()
    swap_q.arrived()
    m.grad_kv[...] = jnp.zeros_like(m.grad_kv)
    for i, kv in enumerate(kv_of):
        m.grad_q[:, i * q_width : (i + 1) * q_width] = m.got_q[i, :, :q_width]
        for k in (0, 1):
            first = q_width + k * HEAD_DIM
            m.grad_kv[k, :, kv * HEAD_DIM : (kv + 1) * HEAD_DIM] += m.got_q[
                i, :, first : first + HEAD_DIM
            ].astype(FULL)
    swap_q.finish()


LOADED = ("wo", "q", "o", "lse", "cos", "sin", "starts", "wq", "part_d")


def back(n_dp, n_seq, own_ff, ff, kv_of, dtype, ins, shapes):
    tok, width = ins["x"].shape
    every = n_dp * tok
    q_width = ins["q"].shape[1]
    pair = 2 * HEAD_DIM
    length = n_seq * tok
    rank, columns = ins["wq"].shape[2:]
    outs = {
        "out": (shape_of((tok, width), dtype), VMEM),
        "grad_x": (shape_of((tok, width), FULL), VMEM),
        "grad_o": (shape_of((rank, width), FULL), VMEM),
        "grad_d": (shape_of((ff, width), FULL), VMEM),
        "grad_q": (shape_of(shapes["q"], LOW), VMEM),
        "grad_kv": (shape_of((2,) + shapes["k"], FULL), VMEM),
        "grad_g": (shape_of(shapes["gate"], LOW), VMEM),
        "grad_u": (shape_of(shapes["gate"], LOW), VMEM),
    }
    placed = {
        key + "_in" if key in LOADED else key: (
            value,
            ANY if key in LOADED + ("part_y", "n1", "kv") else VMEM,
        )
        for key, value in ins.items()
    }
    scratch = {key: pltpu.VMEM(ins[key].shape, ins[key].dtype) for key in LOADED}
    scratch |= {
        "local": dma(3),
        "load": dma(2 + len(LOADED)),
        "got_q": vm(LOW, n_dp, rank, columns),
        "down": DpScatter.scratch(n_dp, ff, width),
        "kv_row": vm(LOW, 2, n_seq, tok, pair),
        "dmid": vm(FULL, tok, width),
        "d_own": vm(LOW, tok, width),
        "d_all": vm(LOW, n_dp, tok, width),
        "d_sem": DpGather.scratch(n_dp),
        "do": vm(LOW, every, q_width),
        "k2": vm(LOW, length, pair),
        "v2": vm(LOW, length, pair),
        "mask": vm(FULL, tok, length),
        "dk2": vm(FULL, length, pair),
        "dv2": vm(FULL, length, pair),
        "dq": vm(FULL, every, q_width),
        "dkv": vm(FULL, every, pair),
        "dqkv": vm(LOW, every, columns),
        "wide": vm(FULL, tok, width),
        "sum_q": vm(LOW, n_dp, rank, columns),
        "part_kv": vm(LOW, n_seq, every, pair),
        "part_q": vm(LOW, n_seq, n_dp, rank, columns),
        "part_o": vm(LOW, n_seq, rank, width),
        "back": DpScatter.scratch(n_dp, tok, width),
        "ring_y": RingScatter.scratch(n_seq, tok, width),
        "staged": RingScatter.staging(tok, width),
        "ring_kv": RingScatter.scratch(n_seq, every, pair),
        "ring_q": RingScatter.scratch(n_seq, n_dp, rank, columns),
        "ring_o": RingScatter.scratch(n_seq, rank, width),
        "swap_q": Exchange.scratch(n_dp),
        "swap_gu": Exchange.scratch(n_seq),
        "got_gu": vm(LOW, *ins["fin"].shape),
    }
    return run(
        functools.partial(back_kernel, n_dp, n_seq, own_ff, ff, kv_of),
        "attention_backward",
        3,
        placed,
        outs,
        scratch,
    )


def body(
    n_dp,
    n_seq,
    tokens,
    segment_ids,
    gain_attn,
    w_query,
    w_key,
    w_value,
    w_output,
    gain_mlp,
    w_gate,
    w_up,
    w_down,
    cotangent,
):
    local, width = tokens.shape[1], tokens.shape[2]
    length = n_seq * local
    own_rows = w_query.shape[0]
    own_ff = w_down.shape[0]
    ff = -(-own_ff // 16) * 16
    heads = HEADS // n_dp
    q_width = heads * HEAD_DIM
    x_own = tokens.reshape(local, width)
    dy_own = cotangent.reshape(local, width)

    kv_of = [i * heads // GROUP for i in range(n_dp)]
    freqs = ROPE_BASE ** (-jnp.arange(0, HEAD_DIM, 2).astype(FULL) / HEAD_DIM)
    got = front(
        n_dp,
        n_seq,
        own_ff,
        kv_of,
        {
            "x": x_own,
            "wg_in": w_gate,
            "wu_in": w_up,
            "wo": w_output,
            "wd": jnp.pad(w_down, ((0, ff - own_ff), (0, 0))),
        },
        {
            "wq": w_query,
            "wk": w_key,
            "wv": w_value,
            "gain_one": gain_attn.reshape(1, own_rows),
            "gain_two": gain_mlp.reshape(1, own_rows),
            "ids": segment_ids.reshape(1, local),
            "freqs": jnp.broadcast_to(jnp.tile(freqs, 4), (8, 2 * HEAD_DIM)),
        },
    )
    fed = feed(
        n_dp,
        n_seq,
        got["second"],
        dy_own,
        got["gu"].reshape(n_seq * own_rows, 2 * n_dp * ff),
        got["wd_all"],
    )
    ins = {
        "part_y": fed["part_y"],
        "grad_h": fed["grad_h"],
        "fin": fed["fin"].reshape(got["gu"].shape),
        "part_d": fed["grad_d"],
        "x": x_own,
        "dy": dy_own,
        "middle": got["middle"],
    }
    for name in ("n1", "q", "kv", "o", "lse", "cos", "sin", "starts", "wq", "wo"):
        ins[name] = got[name + "_out"]
    done = back(
        n_dp,
        n_seq,
        own_ff,
        ff,
        kv_of,
        tokens.dtype,
        ins,
        {"q": w_query.shape, "k": w_key.shape, "gate": w_gate.shape},
    )
    raw_query = done["grad_q"].astype(FULL)
    raw_key, raw_value = done["grad_kv"]
    raw_gate = done["grad_g"].astype(FULL)
    raw_up = done["grad_u"].astype(FULL)
    gain_one = gain_attn.astype(FULL)[:, None]
    gain_two = gain_mlp.astype(FULL)[:, None]

    def gain_grad(*pairs):
        return sum(jnp.sum(weight.astype(FULL) * raw, 1) for weight, raw in pairs)

    return (
        done["out"].reshape(tokens.shape),
        done["grad_x"].reshape(tokens.shape),
        gain_grad((w_query, raw_query), (w_key, raw_key), (w_value, raw_value)),
        gain_one * raw_query,
        gain_one * raw_key,
        gain_one * raw_value,
        done["grad_o"],
        gain_grad((w_gate, raw_gate), (w_up, raw_up)),
        gain_two * raw_gate,
        gain_two * raw_up,
        done["grad_d"][:own_ff],
    )


def solution(mesh):
    rows = P(("dp", "seq"), None)
    vector = P(("dp", "seq"))
    row = P("dp", "seq", None)
    return jax.shard_map(
        functools.partial(body, mesh.shape["dp"], mesh.shape["seq"]),
        mesh=mesh,
        in_specs=(row, P("dp", "seq"), vector, rows, rows, rows, rows, vector, rows, rows, rows, row),
        out_specs=(row, row, vector, rows, rows, rows, rows, vector, rows, rows, rows),
        check_vma=False,
    )
```

```python
import functools

import jax
import jax.numpy as jnp
from jax import lax
from jax.experimental import pallas as pl
from jax.experimental.pallas import tpu as pltpu
from jax.sharding import PartitionSpec as P

HEADS = 32
HEAD_DIM = 64
KV_HEADS = 4
GROUP = HEADS // KV_HEADS

EPS = 1e-05
ROPE_BASE = 10000.0
MASK_VALUE = -1e30
MESH = pl.DeviceIdType.MESH
LOW = jnp.bfloat16
FULL = jnp.float32
VMEM_BYTES = 60 * 1024 * 1024


def matmul(left, right):
    return jnp.dot(left, right, preferred_element_type=FULL)


def matmul_nt(left, right):
    return lax.dot_general(left, right, (((1,), (1,)), ((), ())), preferred_element_type=FULL)


def matmul_tn(left, right):
    return lax.dot_general(left, right, (((0,), (0,)), ((), ())), preferred_element_type=FULL)


def ring_at(place, n):
    upper = lax.div(place, n // 2)
    return (1 - upper) * 2 * place + upper * (2 * (n - place) - 1)


def ring_place(index, n):
    odd = lax.rem(index, 2)
    return (1 - odd) * lax.div(index, 2) + odd * (n - lax.div(index + 1, 2))


class Where:
    def __init__(self, n_dp, n_seq):
        self.n_dp, self.n_seq = n_dp, n_seq
        self.chips = n_dp // 2
        self.dp = lax.axis_index("dp")
        self.seq = lax.axis_index("seq")
        self.core = lax.rem(self.dp, 2)
        self.chip = lax.div(self.dp, 2)
        self.place = ring_place(self.seq, n_seq)

    def ring(self, step):
        return ring_at(lax.rem(self.place + step + self.n_seq, self.n_seq), self.n_seq)

    def ring_ids(self):
        return [(self.dp, self.ring(1)), (self.dp, self.ring(-1))]

    def seq_ids(self):
        return [
            (self.dp, lax.rem(self.seq + k, self.n_seq)) for k in range(1, self.n_seq)
        ]

    def dp_ids(self):
        return [(lax.rem(self.dp + k, self.n_dp), self.seq) for k in range(1, self.n_dp)]

    def core_id(self):
        return (self.dp + 1 - 2 * self.core, self.seq)

    def chip_ids(self):
        return [
            (2 * lax.rem(self.chip + k, self.chips) + self.core, self.seq)
            for k in range(1, self.chips)
        ]


def greet(ids):
    barrier = pltpu.get_barrier_semaphore()
    for one in ids:
        pl.semaphore_signal(barrier, inc=1, device_id=one, device_id_type=MESH)
    pl.semaphore_wait(barrier, len(ids))


def remote(src, dst, send, recv, target):
    return pltpu.make_async_remote_copy(
        src_ref=src,
        dst_ref=dst,
        send_sem=send,
        recv_sem=recv,
        device_id=target,
        device_id_type=MESH,
    )


class Ring:
    def __init__(self, at, shape, send, recv):
        self.at, self.send, self.recv = at, send, recv
        self.steps = at.n_seq // 2
        self.halves = 2 if len(shape) > 2 or shape[0] % 32 == 0 else 1
        self.half = shape[0] // self.halves
        self.copies = {}

    @staticmethod
    def semaphores(n_seq):
        shape = (2, n_seq // 2, 2)
        return [pltpu.SemaphoreType.DMA(shape), pltpu.SemaphoreType.DMA(shape)]

    def opposite(self, h, d):
        return d == h if self.halves == 2 else d == 0

    def rows(self, h):
        return pl.ds(h * self.half, self.half)

    def go(self, src, dst, d, t, h):
        target = self.at.ring_ids()[d]
        copy = remote(src, dst, self.send.at[d, t, h], self.recv.at[d, t, h], target)
        copy.start()
        self.copies[(d, t, h)] = copy

    def pieces(self):
        return [(h, d) for h in range(self.halves) for d in (0, 1)]


class RingGather(Ring):
    def __init__(self, at, own, everything, send, recv, local):
        super().__init__(at, own.shape, send, recv)
        self.own, self.everything = own, everything
        self.kept = pltpu.make_async_copy(own, everything.at[at.seq], local)
        self.waited = set()

    @staticmethod
    def scratch(n_seq):
        return Ring.semaphores(n_seq)

    def wait(self, key):
        self.copies[key].wait_recv()
        self.waited.add(key)

    def step(self, t):
        if t == 0:
            self.kept.start()
        if t == 1:
            self.kept.wait()
        for h, d in self.pieces():
            if t == self.steps - 1 and not self.opposite(h, d):
                continue
            if t > 0:
                self.wait((d, t - 1, h))
            origin = self.at.ring(-t if d == 0 else t)
            dst = self.everything.at[origin, self.rows(h)]
            self.go(self.own.at[self.rows(h)] if t == 0 else dst, dst, d, t, h)

    def rest(self, t):
        for key in self.copies:
            if key not in self.waited and key[1] <= t:
                self.wait(key)

    def finish(self):
        self.rest(self.steps)
        for copy in self.copies.values():
            copy.wait_send()
        if self.steps == 1:
            self.kept.wait()


class RingScatter(Ring):
    def __init__(self, at, parts, slots, send, recv, staged=None, loads=None, axis=0):
        shape = parts.shape[1:] if axis == 0 else parts.shape[:1] + parts.shape[2:]
        super().__init__(at, shape, send, recv)
        self.axis = axis
        self.parts, self.slots, self.staged, self.loads = parts, slots, staged, loads

    @staticmethod
    def scratch(n_seq, *block):
        return [pltpu.VMEM((2, n_seq // 2) + block, LOW)] + Ring.semaphores(n_seq)

    @staticmethod
    def staging(*block):
        return [pltpu.VMEM((2,) + block, LOW), pltpu.SemaphoreType.DMA((2, 2))]

    def there(self, t, d):
        return self.at.ring(self.steps - t if d == 0 else t - self.steps)

    def block(self, index, h):
        if self.axis:
            return self.parts.at[self.rows(h), index]
        return self.parts.at[index, self.rows(h)]

    def adds(self, t, h, d):
        return t > 1 or (t == 1 and self.opposite(h, d))

    def load(self, t, h, d):
        rows = self.rows(h)
        return pltpu.make_async_copy(self.block(self.there(t, d), h), self.staged.at[d, rows], self.loads.at[d, h])

    def load_all(self, t):
        if self.staged is not None:
            for h, d in self.pieces():
                if t < self.steps and self.adds(t, h, d):
                    self.load(t, h, d).start()
                elif t == self.steps and d == 0:
                    self.load(t, h, d).start()

    def early(self):
        for h, d in self.pieces():
            if self.steps > 1 and not self.opposite(h, d):
                self.go(self.block(self.there(1, d), h), self.slots.at[d, 1, self.rows(h)], d, 1, h)

    def step(self, t):
        if t == 0:
            self.load_all(1)
        for h, d in self.pieces():
            if (t == 0 and not self.opposite(h, d)) or (d, t, h) in self.copies:
                continue
            rows = self.rows(h)
            src = self.block(self.there(t, d), h)
            if self.adds(t, h, d):
                if self.staged is not None:
                    self.load(t, h, d).wait()
                    src = self.staged.at[d, rows]
                self.copies[(d, t - 1, h)].wait_recv()
                held = self.slots.at[d, t - 1, rows]
                held[...] = (held[...].astype(FULL) + src[...].astype(FULL)).astype(LOW)
                src = held
            self.go(src, self.slots.at[d, t, rows], d, t, h)
        if t > 0:
            self.load_all(t + 1)

    def finish(self, out):
        last = self.steps - 1
        if last == 0:
            self.load_all(1)
        for h in range(self.halves):
            rows = self.rows(h)
            if self.staged is None:
                total = self.block(self.at.seq, h)[...].astype(FULL)
            else:
                self.load(self.steps, h, 0).wait()
                total = self.staged[0, rows].astype(FULL)
            for d in (0, 1):
                if last == 0 and not self.opposite(h, d):
                    continue
                self.copies[(d, last, h)].wait_recv()
                total = total + self.slots[d, last, rows].astype(FULL)
            out[rows] = total.astype(out.dtype)
        for copy in self.copies.values():
            copy.wait_send()


class Exchange:
    def __init__(self, me, ids, axis, packed, landing, send, recv, local):
        self.started = 0
        self.kept = pltpu.make_async_copy(packed.at[me], landing.at[me], local)
        self.copies = [
            remote(packed.at[one[axis]], landing.at[me], send.at[k], recv.at[k], one)
            for k, one in enumerate(ids)
        ]

    @staticmethod
    def scratch(n):
        return [pltpu.SemaphoreType.DMA((n - 1,)), pltpu.SemaphoreType.DMA((n - 1,))]

    def start(self, count=None):
        if not self.started:
            self.kept.start()
        first = self.started - 1 if self.started else 0
        last = len(self.copies) if count is None else min(first + count, len(self.copies))
        for copy in self.copies[first:last]:
            copy.start()
        self.started = last + 1

    def arrived(self):
        self.kept.wait()
        for copy in self.copies:
            copy.wait_recv()

    def finish(self):
        for copy in self.copies:
            copy.wait_send()


def seq_exchange(at, *refs):
    return Exchange(at.seq, at.seq_ids(), 1, *refs)


def dp_exchange(at, *refs):
    return Exchange(at.dp, at.dp_ids(), 0, *refs)


class DpGather:
    def __init__(self, at, own, everything, send, recv, local):
        self.kept = pltpu.make_async_copy(own, everything.at[at.dp], local)
        slot = everything.at[at.dp]
        self.out = [
            remote(own, slot, send.at[k], recv.at[k], one) for k, one in enumerate(at.chip_ids())
        ]
        base = at.chips - 1
        self.mate = remote(own, slot, send.at[base], recv.at[base], at.core_id())
        self.handed = []
        for k in range(1, at.chips):
            origin = 2 * lax.rem(at.chip + at.chips - k, at.chips) + at.core
            there = everything.at[origin]
            self.handed.append(
                remote(there, there, send.at[base + k], recv.at[base + k], at.core_id())
            )

    @staticmethod
    def scratch(n_dp):
        return [pltpu.SemaphoreType.DMA((n_dp - 1,)), pltpu.SemaphoreType.DMA((n_dp - 1,))]

    def start(self):
        for copy in self.out:
            copy.start()
        self.mate.start()
        self.kept.start()

    def hand(self):
        for copy, onward in zip(self.out, self.handed):
            copy.wait_recv()
            onward.start()

    def arrived(self):
        self.kept.wait()
        self.mate.wait_recv()
        for copy in self.handed:
            copy.wait_recv()

    def finish(self):
        for copy in self.out + [self.mate] + self.handed:
            copy.wait_send()


def add_rows(rows, chunk, one):
    def step(r, carry):
        one(pl.ds(pl.multiple_of(r * chunk, chunk), chunk))
        return carry

    lax.fori_loop(0, rows // chunk, step, 0)


def chunk_of(rows, columns):
    chunk = rows
    while chunk % 32 == 0 and chunk * columns > 65536:
        chunk //= 2
    return chunk


class DpScatter:
    def __init__(self, at, parts, core, other, send, recv):
        self.at, self.parts, self.core, self.other = at, parts, core, other
        self.send, self.recv = send, recv
        self.rows, self.columns = parts.shape[1], parts.shape[2]

    @staticmethod
    def scratch(n_dp, rows, columns):
        chips = n_dp // 2
        return [
            pltpu.VMEM((chips, rows, columns), LOW),
            pltpu.VMEM((max(chips - 1, 1), rows, columns), LOW),
            pltpu.SemaphoreType.DMA((2 * chips - 1,)),
            pltpu.SemaphoreType.DMA((2 * chips - 1,)),
        ]

    def to_core(self, k):
        at = self.at
        return remote(
            self.parts.at[2 * k + 1 - at.core],
            self.core.at[k],
            self.send.at[k],
            self.recv.at[k],
            at.core_id(),
        )

    def to_chip(self, k):
        at = self.at
        sem = at.chips + k - 1
        return remote(
            self.core.at[lax.rem(at.chip + k, at.chips)],
            self.other.at[k - 1],
            self.send.at[sem],
            self.recv.at[sem],
            at.chip_ids()[k - 1],
        )

    def start(self):
        for k in range(self.at.chips):
            self.to_core(k).start()

    def add_core(self, k):
        held = self.core.at[k]
        mine = self.parts.at[2 * k + self.at.core]

        def one(rows):
            held[rows] = (held[rows].astype(FULL) + mine[rows].astype(FULL)).astype(LOW)

        add_rows(self.rows, chunk_of(self.rows, self.columns), one)

    def across(self):
        at = self.at
        for k in range(1, at.chips):
            there = lax.rem(at.chip + k, at.chips)
            self.to_core(there).wait_recv()
            self.add_core(there)
            self.to_chip(k).start()

    def finish(self, out):
        at = self.at
        self.to_core(at.chip).wait_recv()
        for k in range(1, at.chips):
            self.to_chip(k).wait_recv()
        held = self.core.at[at.chip]
        mine = self.parts.at[2 * at.chip + at.core]

        def one(rows):
            total = held[rows].astype(FULL) + mine[rows].astype(FULL)
            for k in range(1, at.chips):
                total = total + self.other[k - 1, rows].astype(FULL)
            out[rows] = total.astype(out.dtype)

        add_rows(self.rows, chunk_of(self.rows, self.columns), one)
        for k in range(at.chips):
            self.to_core(k).wait_send()
        for k in range(1, at.chips):
            self.to_chip(k).wait_send()


def comm_params(number):
    if number is None:
        return pltpu.CompilerParams(vmem_limit_bytes=VMEM_BYTES)
    return pltpu.CompilerParams(
        collective_id=number, has_side_effects=True, vmem_limit_bytes=VMEM_BYTES
    )


ANY = pl.BlockSpec(memory_space=pl.ANY)
VMEM = pl.BlockSpec(memory_space=pltpu.VMEM)


def shape_of(dims, kind):
    return jax.ShapeDtypeStruct(dims, kind)


class Refs:
    def __init__(self, names, refs):
        refs = list(refs)
        for name, count in names:
            taken, refs = refs[: max(count, 1)], refs[max(count, 1) :]
            setattr(self, name, taken if count else taken[0])


def run(kernel, name, number, ins, outs, scratch):
    names = [(key, 0) for key in ins] + [(key, 0) for key in outs]
    shapes = []
    for key, value in scratch.items():
        if isinstance(value, list):
            names.append((key, len(value)))
            shapes += value
        else:
            names.append((key, 0))
            shapes.append(value)
    found = pl.pallas_call(
        lambda *refs: kernel(Refs(names, refs)),
        name=name,
        out_shape=[shape for shape, _ in outs.values()],
        in_specs=[spec for _, spec in ins.values()],
        out_specs=[spec for _, spec in outs.values()],
        scratch_shapes=shapes,
        compiler_params=comm_params(number),
    )(*[array for array, _ in ins.values()])
    return dict(zip(outs, found))


def dma(*dims):
    return pltpu.SemaphoreType.DMA(dims)


def vm(kind, *dims):
    return pltpu.VMEM(dims, kind)


def lanes(rows):
    return lax.broadcasted_iota(jnp.int32, (rows, 2 * HEAD_DIM), 1)


def low_head(rows):
    return lanes(rows) < HEAD_DIM


def swapped(pair):
    half = HEAD_DIM // 2
    first = lax.rem(lanes(pair.shape[0]), HEAD_DIM) < half
    return jnp.where(
        first, pltpu.roll(pair, 2 * HEAD_DIM - half, 1), pltpu.roll(pair, half, 1)
    )


def split_heads(pair):
    wide = pair.astype(FULL)
    low = low_head(pair.shape[0])
    return jnp.concatenate(
        [jnp.where(low, wide, 0.0), jnp.where(low, 0.0, wide)], 0
    ).astype(LOW)


def join_heads(both):
    rows = both.shape[0] // 2
    return jnp.where(low_head(rows), both[:rows], both[rows:])


def spread_kv(kv):
    wide = kv.astype(FULL)
    turned = pltpu.roll(wide, HEAD_DIM, 1)
    low = low_head(kv.shape[0])
    return jnp.where(low, wide, turned).astype(LOW), jnp.where(low, turned, wide).astype(LOW)


def mask_of(position, start, length):
    key = lax.broadcasted_iota(jnp.int32, (start.shape[0], length), 1)
    return jnp.where((key <= position) & (key >= start), 0.0, MASK_VALUE)


def own_positions(at, tok):
    return at.seq * tok + lax.broadcasted_iota(jnp.int32, (tok, 1), 0)


def rows_of(r, count):
    return pl.ds(pl.multiple_of(r * count, count), count)


def to_column(row):
    n = row.shape[1]
    here = lax.broadcasted_iota(jnp.int32, (n, n), 0) == lax.broadcasted_iota(jnp.int32, (n, n), 1)
    return jnp.sum(jnp.where(here, row.astype(FULL), 0.0), 1, keepdims=True)


def to_row(column):
    n = column.shape[0]
    here = lax.broadcasted_iota(jnp.int32, (n, n), 0) == lax.broadcasted_iota(jnp.int32, (n, n), 1)
    return jnp.sum(jnp.where(here, column, 0.0), 0, keepdims=True)


def front_kernel(n_dp, n_seq, own_ff, ff, kv_of, m):
    at = Where(n_dp, n_seq)
    tok, width = m.x.shape
    q_width = m.q.shape[1]
    groups = q_width // (2 * HEAD_DIM)
    rank = n_seq * m.pq.shape[1]
    length = n_seq * tok
    greet(at.seq_ids() + at.dp_ids())
    swap_q = dp_exchange(at, m.pq, m.landed, *m.swap_q_sem, m.local.at[0])
    x_g = DpGather(at, m.x, m.xs, *m.x_sem, m.local.at[1])
    row_x = seq_exchange(at, m.seg_rows, m.seg_row, *m.row_x_sem, m.local.at[2])
    row_g = DpGather(at, m.seg_row, m.segs, *m.row_g_sem, m.local.at[3])
    col_g = DpGather(at, m.seg_col, m.seg_cols, *m.col_g_sem, m.local.at[4])
    ring_q = RingGather(at, m.landed, m.wq_all, *m.ring_q_sem, m.local.at[5])
    ring_o = RingGather(at, m.wo, m.wo_all, *m.ring_o_sem, m.local.at[6])
    ring_kv = RingGather(at, m.kv_own, m.kv_all, *m.ring_kv_sem, m.local.at[7])
    swap_gu = seq_exchange(at, m.pgu, m.gu, *m.swap_gu_sem, m.local.at[8])
    down = DpGather(at, m.wd, m.wd_all, *m.down_sem, m.local.at[9])
    loads = [
        pltpu.make_async_copy(src, dst, m.load.at[k])
        for k, (src, dst) in enumerate(((m.wg_in, m.wg), (m.wu_in, m.wu), (m.x, m.x_own)))
    ]
    stores = []

    def store(src, dst):
        copy = pltpu.make_async_copy(src, dst, m.local.at[10 + len(stores)])
        copy.start()
        stores.append(copy)

    ring_o.step(0)
    for copy in loads:
        copy.start()

    gain = to_column(m.gain_one[...])
    for i, kv in enumerate(kv_of):
        m.pq[i, :, :q_width] = (
            gain * m.wq[:, i * q_width : (i + 1) * q_width].astype(FULL)
        ).astype(LOW)
        for weight, first in ((m.wk, q_width), (m.wv, q_width + HEAD_DIM)):
            m.pq[i, :, first : first + HEAD_DIM] = (
                gain * weight[:, kv * HEAD_DIM : (kv + 1) * HEAD_DIM].astype(FULL)
            ).astype(LOW)
    swap_q.start()
    x_g.start()
    ids = m.ids[...]
    m.seg_rows[...] = jnp.broadcast_to(ids[None], m.seg_rows.shape)
    m.seg_col[...] = jnp.broadcast_to(to_column(ids).astype(jnp.int32), m.seg_col.shape)
    row_x.start()
    col_g.start()

    def pack(k, weight, first):
        loads[k].wait()
        scale = to_column(m.gain_two[...])
        if ff > own_ff:
            m.pgu[:, :, first : first + n_dp * ff] = jnp.zeros(
                m.pgu.shape[:2] + (n_dp * ff,), LOW
            )
        for s in range(n_seq):
            for i in range(n_dp):
                piece = weight[:, (i * n_seq + s) * own_ff : (i * n_seq + s + 1) * own_ff]
                m.pgu[s, :, first + i * ff : first + i * ff + own_ff] = (
                    scale * piece.astype(FULL)
                ).astype(LOW)

    later = list(range(1, ring_o.steps))
    ring_o.step(later.pop(0))
    swap_q.arrived()
    ring_q.step(0)
    row_x.arrived()
    row_g.start()

    def hand():
        x_g.hand()
        row_g.hand()
        col_g.hand()
        down.start()

    def norm():
        x_g.arrived()
        for r in range(n_dp):
            x = m.xs[r].astype(FULL)
            scale = lax.rsqrt(jnp.mean(x * x, -1, keepdims=True) + EPS)
            m.n1[r] = (x * scale).astype(LOW)
        store(m.n1, m.n1_out)

    def place():
        row_g.arrived()
        col_g.arrived()
        position = own_positions(at, tok)
        first = lax.rem(lanes(tok), HEAD_DIM) < HEAD_DIM // 2
        for r in range(n_dp):
            segs = jnp.concatenate([m.segs[r, s, :1] for s in range(n_seq)], 1)
            own = m.seg_cols[r][:, :1]
            start = jnp.sum((segs < own).astype(jnp.int32), 1, keepdims=True)
            turned = (position - start).astype(FULL) * m.freqs[:1]
            rows = slice(r * tok, (r + 1) * tok)
            m.cos[rows] = jnp.cos(turned)
            sines = jnp.sin(turned)
            m.sin[rows] = jnp.where(first, -sines, sines)
            m.starts[rows] = jnp.broadcast_to(start, (tok, 2 * HEAD_DIM))
        store(m.cos, m.cos_out)
        store(m.sin, m.sin_out)
        store(m.starts, m.starts_out)

    pack(0, m.wg, 0)
    ring_q.step(1)
    jobs = [lambda: (hand(), norm(), place()), lambda: pack(1, m.wu, n_dp * ff)]
    for t in range(2, ring_q.steps):
        ring_q.step(t)
        if jobs:
            jobs.pop(0)()
    for job in jobs:
        job()
    ring_q.finish()
    if later:
        ring_o.step(later.pop(0))
    store(m.wq_all, m.wq_out)

    m.qkv[...] = sum(
        matmul(
            m.n1[:, :, i * rank : (i + 1) * rank].reshape(n_dp * tok, rank),
            m.wq_all[:, i].reshape(rank, q_width + 2 * HEAD_DIM),
        )
        for i in range(n_dp)
    )
    factor = HEAD_DIM ** (-0.5)
    for g in range(groups + 1):
        cols = slice(g * 2 * HEAD_DIM, (g + 1) * 2 * HEAD_DIM)
        pair = m.qkv[:, cols]
        turned = pair * m.cos[...] + swapped(pair) * m.sin[...]
        if g < groups:
            m.q[:, cols] = (turned * factor).astype(LOW)
        else:
            m.kv_own[...] = jnp.where(low_head(pair.shape[0]), turned, pair).astype(LOW)
    ring_kv.step(0)
    store(m.q, m.q_out)
    for t in range(1, ring_kv.steps):
        ring_kv.step(t)
        if later and t > 1:
            ring_o.step(later.pop(0))
    for t in later:
        ring_o.step(t)
    down.hand()
    ring_kv.finish()
    store(m.kv_all, m.kv_out)
    m.lse[...] = jnp.zeros_like(m.lse)
    for r in range(n_dp):
        rows = slice(r * tok, (r + 1) * tok)
        k, v = spread_kv(m.kv_all[:, rows].reshape(length, 2 * HEAD_DIM))
        m.k2[...] = k
        m.v2[...] = v
        m.mask[...] = mask_of(own_positions(at, tok), m.starts[rows, :1], length)

        def group(g, carry):
            cols = rows_of(g, 2 * HEAD_DIM)
            raw = matmul_nt(split_heads(m.q[rows, cols]), m.k2[...])
            raw = raw + jnp.concatenate([m.mask[...]] * 2, 0)
            top = jnp.max(raw, -1, keepdims=True)
            probs = jnp.exp(raw - top)
            total = jnp.sum(probs, -1, keepdims=True)
            probs = (probs * (1.0 / total)).astype(LOW)
            m.o[rows, cols] = join_heads(matmul(probs, m.v2[...])).astype(LOW)
            here = lanes(2 * tok) == r * groups + g
            m.lse[...] = jnp.where(here, top + jnp.log(total), m.lse[...])
            return carry

        lax.fori_loop(0, groups, group, 0)
        if r == 0:
            swap_gu.start()
    store(m.o, m.o_out)
    store(m.lse, m.lse_out)
    ring_o.finish()
    store(m.wo_all, m.wo_out)
    full = m.wo_all[...].reshape(q_width, width)
    for r in range(n_dp):
        m.parts[r] = matmul(m.o[r * tok : (r + 1) * tok], full).astype(LOW)
    back = DpScatter(at, m.parts, *m.back)
    back.start()
    back.across()
    back.finish(m.middle)
    loads[2].wait()
    middle = m.x_own[...].astype(FULL) + m.middle[...]
    m.middle[...] = middle
    scale = lax.rsqrt(jnp.mean(middle * middle, -1, keepdims=True) + EPS)
    m.second[...] = (middle * scale).astype(LOW)
    swap_gu.arrived()
    down.arrived()
    for one in (swap_q, x_g, row_x, row_g, col_g, swap_gu, down):
        one.finish()
    for copy in stores:
        copy.wait()


def front(n_dp, n_seq, own_ff, kv_of, held, small):
    tok, width = held["x"].shape
    rank = small["wq"].shape[0]
    q_width = width // n_dp
    groups = q_width // (2 * HEAD_DIM)
    pair = 2 * HEAD_DIM
    columns = q_width + pair
    length = n_seq * tok
    every = n_dp * tok
    wd = held["wd"]
    ff = wd.shape[0]
    gu_width = 2 * n_dp * ff
    ins = {key: (value, ANY) for key, value in held.items()}
    ins |= {key: (value, VMEM) for key, value in small.items()}
    kept = dict(
        n1=(LOW, n_dp, tok, width),
        q=(LOW, every, q_width),
        kv_all=(LOW, n_seq, every, pair),
        o=(LOW, every, q_width),
        lse=(FULL, 2 * tok, pair),
        cos=(FULL, every, pair),
        sin=(FULL, every, pair),
        starts=(jnp.int32, every, pair),
        wq_all=(LOW, n_seq, n_dp, rank, columns),
        wo_all=(LOW, n_seq, rank, width),
    )
    outs = {
        key.replace("_all", "") + "_out": (shape_of(dims[1:], dims[0]), ANY)
        for key, dims in kept.items()
    }
    outs["gu"] = (shape_of((n_seq, rank, gu_width), LOW), ANY)
    outs["wd_all"] = (shape_of((n_dp,) + wd.shape, LOW), ANY)
    outs["middle"] = (shape_of((tok, width), FULL), VMEM)
    outs["second"] = (shape_of((tok, width), LOW), VMEM)
    scratch = {key: vm(*dims) for key, dims in kept.items()}
    scratch |= dict(
        load=dma(3),
        wg=vm(LOW, *held["wg_in"].shape),
        wu=vm(LOW, *held["wg_in"].shape),
        x_own=vm(LOW, tok, width),
        pq=vm(LOW, n_dp, rank, columns),
        seg_rows=vm(jnp.int32, n_seq, 8, tok),
        seg_col=vm(jnp.int32, tok, pair),
        landed=vm(LOW, n_dp, rank, columns),
        xs=vm(LOW, n_dp, tok, width),
        seg_row=vm(jnp.int32, n_seq, 8, tok),
        segs=vm(jnp.int32, n_dp, n_seq, 8, tok),
        seg_cols=vm(jnp.int32, n_dp, tok, pair),
        kv_own=vm(LOW, every, pair),
        mask=vm(FULL, tok, length),
        pgu=vm(LOW, n_seq, rank, gu_width),
        qkv=vm(FULL, every, columns),
        k2=vm(LOW, length, pair),
        v2=vm(LOW, length, pair),
        parts=vm(LOW, n_dp, tok, width),
        back=DpScatter.scratch(n_dp, tok, width),
        local=dma(10 + len(kept)),
        swap_q_sem=Exchange.scratch(n_dp),
        x_sem=DpGather.scratch(n_dp),
        row_x_sem=Exchange.scratch(n_seq),
        row_g_sem=DpGather.scratch(n_dp),
        col_g_sem=DpGather.scratch(n_dp),
        ring_q_sem=Ring.semaphores(n_seq),
        ring_o_sem=Ring.semaphores(n_seq),
        ring_kv_sem=Ring.semaphores(n_seq),
        swap_gu_sem=Exchange.scratch(n_seq),
        down_sem=DpGather.scratch(n_dp),
    )
    return run(
        functools.partial(front_kernel, n_dp, n_seq, own_ff, ff, kv_of), "attention_forward", 1, ins, outs, scratch
    )


def feed_kernel(n_dp, n_seq, m):
    at = Where(n_dp, n_seq)
    tok, width = m.second.shape
    wide = m.wgu.shape[2]
    part = wide // 2
    rank = width // n_dp
    length = n_seq * tok
    greet(at.ring_ids() + at.dp_ids())
    gu = DpGather(at, m.gu, m.wgu, *m.gu_sem, m.local.at[0])
    ring_n = RingGather(at, m.second, m.second_all, *m.ring_n, m.local.at[1])
    ring_dy = RingGather(at, m.dy, m.dy_all, *m.ring_dy, m.local.at[2])
    ring_h = RingScatter(at, m.part, *m.ring_h)
    side = DpScatter(at, m.wgu, *m.side)
    gu.start()
    held = pltpu.make_async_copy(m.wd_all, m.wd, m.local.at[3])
    held.start()
    ring_n.step(0)
    for t in range(1, ring_n.steps):
        ring_n.step(t)
    ring_dy.step(0)
    gu.hand()
    ring_n.finish()
    gu.arrived()
    held.wait()
    stores = []

    def store(src, dst, k):
        copy = pltpu.make_async_copy(src, dst, m.local.at[k])
        copy.start()
        stores.append(copy)

    def stored():
        while stores:
            stores.pop().wait()

    def forward(c):
        blocks = slice(2 * c, 2 * c + 2)
        normed = m.second_all[blocks].reshape(2 * tok, width)
        both = matmul(normed, m.wgu[...].reshape(width, wide))
        gate, upward = both[:, :part], both[:, part:]
        sigma = jax.nn.sigmoid(gate)
        silu = gate * sigma
        hidden = (silu * upward).astype(LOW)
        m.by_up[blocks] = silu.reshape(2, tok, part)
        m.by_gate[blocks] = (upward * sigma * (1.0 + gate * (1.0 - sigma))).reshape(2, tok, part)
        m.hidden[blocks] = hidden.reshape(2, tok, part)
        out = matmul(hidden, m.wd[...].reshape(part, width))
        m.part[blocks] = out.astype(LOW).reshape(2, tok, width)
        copy = pltpu.make_async_copy(m.part.at[blocks], m.part_y.at[blocks], m.store.at[c])
        copy.start()
        stores.append(copy)

    def backward(blocks):
        rows = len(blocks) * tok
        dy = jnp.concatenate([m.dy_all[b] for b in blocks], 0)
        grad = matmul_nt(dy, m.wd[...].reshape(part, width))
        for k, b in enumerate(blocks):
            one = grad[k * tok : (k + 1) * tok]
            m.grads[b, :, :part] = (one * m.by_gate[b]).astype(LOW)
            m.grads[b, :, part:] = (one * m.by_up[b]).astype(LOW)
        both = jnp.concatenate([m.grads[b] for b in blocks], 0)
        for i in range(n_dp):
            cols = slice(i * rank, (i + 1) * rank)
            out = matmul_nt(both, m.wgu[i]).astype(LOW)
            for k, b in enumerate(blocks):
                m.part[b, :, cols] = out[k * tok : (k + 1) * tok]

    jobs = [functools.partial(forward, c) for c in range(n_seq // 2)]
    jobs.append(stored)
    jobs.append(lambda: backward([at.seq]))
    for t in range(1, ring_dy.steps):
        for _ in range(3 if t == 1 else 4):
            if jobs:
                jobs.pop(0)()
        ring_dy.step(t)
        if t < ring_dy.steps - 1:
            jobs.append(functools.partial(backward, [at.ring(-t), at.ring(t)]))
    for job in jobs:
        job()
    if ring_dy.steps > 1:
        ring_dy.rest(ring_dy.steps - 2)
        backward([at.ring(1 - ring_dy.steps), at.ring(ring_dy.steps - 1)])
    ring_h.early()
    ring_dy.finish()
    backward([at.ring(ring_dy.steps)])
    gu.finish()

    ring_h.step(0)

    def grad_gu(k):
        chip = lax.rem(at.chip + 1 + k, at.chips)
        for c in (1 - at.core, at.core):
            normed = m.second_all[:, :, rows_of(2 * chip + c, rank)].reshape(length, rank)
            m.wgu[2 * chip + c] = matmul_tn(normed, m.grads[...].reshape(length, wide)).astype(LOW)
            if c is not at.core:
                side.to_core(chip).start()

    def grad_down():
        step = width // n_dp
        for i in range(n_dp):
            cols = slice(i * step, (i + 1) * step)
            dy = m.dy_all[:, :, cols].reshape(length, step)
            m.wd[:, :, cols] = (
                matmul_tn(m.hidden[...].reshape(length, part), dy)
                .astype(LOW)
                .reshape(m.wd.shape[:2] + (step,))
            )
        store(m.wd, m.grad_d, 3)

    jobs = [functools.partial(grad_gu, k) for k in range(at.chips)]
    jobs += [side.across, grad_down]
    for t in range(1, ring_h.steps):
        for _ in range(2):
            if jobs:
                jobs.pop(0)()
        ring_h.step(t)
    for job in jobs:
        job()
    ring_h.finish(m.grad_h)
    store(m.grad_h, m.grad_h_to, 4)
    side.finish(m.fin)
    store(m.fin, m.fin_to, 5)
    stored()


def feed(n_dp, n_seq, second, dy, gu, wd):
    tok, width = second.shape
    deep, wide = gu.shape
    ff = wd.shape[1]
    part = wide // 2
    ins = dict(second=(second, ANY), dy=(dy, ANY), gu=(gu, ANY), wd_all=(wd, ANY))
    outs = dict(
        part_y=(shape_of((n_seq, tok, width), LOW), ANY),
        grad_h_to=(shape_of((tok, width), FULL), ANY),
        fin_to=(shape_of((deep, wide), LOW), ANY),
        grad_d=(shape_of(wd.shape, LOW), ANY),
    )
    scratch = dict(
        local=dma(6),
        grad_h=vm(FULL, tok, width),
        fin=vm(LOW, deep, wide),
        wd=vm(LOW, *wd.shape),
        store=dma(n_seq // 2),
        second_all=vm(LOW, n_seq, tok, width),
        dy_all=vm(LOW, n_seq, tok, width),
        wgu=vm(LOW, n_dp, deep, wide),
        by_gate=vm(FULL, n_seq, tok, part),
        by_up=vm(FULL, n_seq, tok, part),
        hidden=vm(LOW, n_seq, tok, part),
        grads=vm(LOW, n_seq, tok, wide),
        part=vm(LOW, n_seq, tok, width),
        gu_sem=DpGather.scratch(n_dp),
        ring_n=Ring.semaphores(n_seq),
        ring_dy=Ring.semaphores(n_seq),
        ring_h=RingScatter.scratch(n_seq, tok, width),
        side=DpScatter.scratch(n_dp, deep, wide),
    )
    return run(functools.partial(feed_kernel, n_dp, n_seq), "feed_forward", 2, ins, outs, scratch)


def back_kernel(n_dp, n_seq, own_ff, ff, kv_of, m):
    at = Where(n_dp, n_seq)
    tok, width = m.x.shape
    q_width = m.q.shape[1]
    groups = q_width // (2 * HEAD_DIM)
    rank = n_seq * m.wq.shape[2]
    length = n_seq * tok
    pair = 2 * HEAD_DIM
    greet(at.seq_ids() + at.dp_ids())
    swap_gu = [
        remote(m.fin.at[one[1]], m.got_gu.at[at.seq], m.swap_gu[0].at[k], m.swap_gu[1].at[k], one)
        for k, one in enumerate(at.seq_ids())
    ]
    ring_y = RingScatter(at, m.part_y, *m.ring_y, *m.staged)
    d_g = DpGather(at, m.d_own, m.d_all, *m.d_sem, m.local.at[0])
    ring_kv = RingScatter(at, m.part_kv, *m.ring_kv)
    ring_q = RingScatter(at, m.landed_q, *m.ring_q, axis=1)
    ring_o = RingScatter(at, m.part_o, *m.ring_o)
    down = DpScatter(at, m.part_d, *m.down)
    back = DpScatter(at, m.d_all, *m.back)
    swap_q = [
        remote(m.part_q.at[one[0]], m.landed_q.at[at.dp], m.swap_q[0].at[k], m.swap_q[1].at[k], one)
        for k, one in enumerate(at.dp_ids())
    ]
    ring_y.step(0)
    stores = []

    def store(key):
        copy = pltpu.make_async_copy(getattr(m, key), getattr(m, key + "_to"), m.store.at[len(stores)])
        copy.start()
        stores.append(copy)

    waiting = list(swap_gu)

    def pace(count=1):
        for copy in waiting[:count]:
            copy.start()
        del waiting[:count]

    loads = [
        pltpu.make_async_copy(getattr(m, key + "_in"), getattr(m, key), m.load.at[2 + k])
        for k, key in enumerate(LOADED)
    ]
    for copy in loads:
        copy.start()

    def load_kv(r):
        block = m.kv.at[:, pl.ds(r * tok, tok)]
        return pltpu.make_async_copy(block, m.kv_row.at[r % 2], m.load.at[r % 2])

    load_kv(0).start()
    own_gu = pltpu.make_async_copy(m.fin.at[at.seq], m.got_gu.at[at.seq], m.local.at[3])
    own_gu.start()

    def norm_back(grad, value):
        scale = lax.rsqrt(jnp.mean(value * value, -1, keepdims=True) + EPS)
        normed = value * scale
        return scale * (grad - normed * jnp.mean(grad * normed, -1, keepdims=True))

    for copy in loads[:3]:
        copy.wait()
    m.dmid[...] = m.dy[...].astype(FULL) + norm_back(m.grad_h[...], m.middle[...])
    m.d_own[...] = m.dmid[...].astype(LOW)
    d_g.start()
    if ring_y.steps > 1:
        ring_y.step(1)
    d_g.hand()
    for copy in loads[3:]:
        copy.wait()
    d_g.arrived()
    down.start()
    m.do[...] = matmul_nt(
        m.d_all[...].reshape(n_dp * tok, width), m.wo[...].reshape(q_width, width)
    ).astype(LOW)
    later = list(range(2, ring_y.steps))
    down.across()
    if later:
        ring_y.step(later.pop(0))
    for r in range(n_dp):
        rows = slice(r * tok, (r + 1) * tok)
        load_kv(r).wait()
        if r + 1 < n_dp:
            load_kv(r + 1).start()
        k, v = spread_kv(m.kv_row[r % 2].reshape(length, pair))
        m.k2[...] = k
        m.v2[...] = v
        m.mask[...] = mask_of(own_positions(at, tok), m.starts[rows, :1], length)
        m.dk2[...] = jnp.zeros_like(m.dk2)
        m.dv2[...] = jnp.zeros_like(m.dv2)

        def group(g, carry):
            cols = rows_of(g, pair)
            q2 = split_heads(m.q[rows, cols])
            do2 = split_heads(m.do[rows, cols])
            raw = matmul_nt(q2, m.k2[...])
            raw = raw + jnp.concatenate([m.mask[...]] * 2, 0)
            here = lanes(2 * tok) == r * groups + g
            lse = jnp.sum(jnp.where(here, m.lse[...], 0.0), 1, keepdims=True)
            probs = jnp.exp(raw - lse)
            grad_probs = matmul_nt(do2, m.v2[...])
            delta = jnp.sum(probs * grad_probs, -1, keepdims=True)
            grad_raw = (probs * (grad_probs - delta)).astype(LOW)
            m.dq[rows, cols] = join_heads(matmul(grad_raw, m.k2[...]))
            m.dk2[...] += matmul_tn(grad_raw, q2)
            m.dv2[...] += matmul_tn(probs.astype(LOW), do2)
            return carry

        lax.fori_loop(0, groups, group, 0)
        dk = m.dk2[...]
        dv = m.dv2[...]
        dkv = jnp.where(
            low_head(length), dk + pltpu.roll(dk, HEAD_DIM, 1), dv + pltpu.roll(dv, HEAD_DIM, 1)
        )
        m.part_kv[:, rows] = dkv.astype(LOW).reshape(n_seq, tok, pair)
        if later and r % 2:
            ring_y.step(later.pop(0))
    for t in later:
        ring_y.step(t)
    ring_kv.step(0)
    m.part_o[...] = (
        matmul_tn(m.o[...], m.d_all[...].reshape(n_dp * tok, width))
        .astype(LOW)
        .reshape(m.part_o.shape)
    )
    d_g.finish()
    for t in range(1, ring_kv.steps):
        ring_kv.step(t)
        pace()
    ring_kv.finish(m.dkv)
    ring_o.step(0)
    factor = HEAD_DIM ** (-0.5)
    for g in range(groups + 1):
        cols = slice(g * pair, (g + 1) * pair)
        grad = m.dq[:, cols] * factor if g < groups else m.dkv[...]
        turned = grad * m.cos[...] - swapped(grad) * m.sin[...]
        if g == groups:
            turned = jnp.where(low_head(grad.shape[0]), turned, grad)
        m.dqkv[:, cols] = turned.astype(LOW)
    ring_y.finish(m.wide)
    n1 = m.ring_y[0].at[0, pl.ds(0, n_dp)]
    fetch = pltpu.make_async_copy(m.n1, n1, m.local.at[2])
    fetch.start()
    m.out[...] = (m.middle[...] + m.wide[...]).astype(m.out.dtype)
    store("out")
    pace()
    fetch.wait()
    for i in range(n_dp):
        cols = slice(i * rank, (i + 1) * rank)
        m.part_q[i] = (
            matmul_tn(n1[:, :, cols].reshape(n_dp * tok, rank), m.dqkv[...])
            .astype(LOW)
            .reshape(n_seq, rank // n_seq, q_width + pair)
        )
    for copy in swap_q:
        copy.start()
    m.landed_q[at.dp] = m.part_q[at.dp]
    pace()
    if ring_o.steps > 1:
        ring_o.step(1)
    pace()
    for i in range(n_dp):
        cols = slice(i * rank, (i + 1) * rank)
        weight = m.wq[:, i].reshape(rank, q_width + pair)
        m.d_all[:, :, cols] = (
            matmul_nt(m.dqkv[...], weight).astype(LOW).reshape(n_dp, tok, rank)
        )
    back.start()
    pace()
    pace(len(waiting))

    def unpack(grad, first):
        for s in range(n_seq):
            for i in range(n_dp):
                grad[:, (i * n_seq + s) * own_ff : (i * n_seq + s + 1) * own_ff] = m.got_gu[
                    s, :, first + i * ff : first + i * ff + own_ff
                ]

    def unpack_gate():
        for copy in swap_gu:
            copy.wait()
        own_gu.wait()
        unpack(m.grad_g, 0)
        store("grad_g")

    def unpack_up():
        unpack(m.grad_u, n_dp * ff)
        store("grad_u")

    def grad_inputs():
        back.finish(m.wide)
        m.grad_x[...] = m.dmid[...] + norm_back(m.wide[...], m.x[...].astype(FULL))
        store("grad_x")

    def finish_down():
        down.finish(m.grad_d)
        store("grad_d")

    jobs = [finish_down, back.across]
    for t in range(2, ring_o.steps):
        ring_o.step(t)
        if jobs:
            jobs.pop(0)()
    jobs += [unpack_gate, unpack_up, grad_inputs]
    for copy in swap_q:
        copy.wait()
    ring_q.step(0)
    for t in range(1, ring_q.steps):
        ring_q.step(t)
        if jobs:
            jobs.pop(0)()
    for job in jobs:
        job()
    ring_o.finish(m.grad_o)
    store("grad_o")
    ring_q.finish(m.got_q)
    m.grad_kv[...] = jnp.zeros_like(m.grad_kv)
    for i, kv in enumerate(kv_of):
        m.grad_q[:, i * q_width : (i + 1) * q_width] = m.got_q[i, :, :q_width]
        for k in (0, 1):
            first = q_width + k * HEAD_DIM
            m.grad_kv[k, :, kv * HEAD_DIM : (kv + 1) * HEAD_DIM] += m.got_q[
                i, :, first : first + HEAD_DIM
            ].astype(FULL)
    store("grad_q")
    store("grad_kv")
    for copy in stores:
        copy.wait()


LOADED = ("grad_h", "dy", "middle", "wo", "q", "o", "lse", "cos", "sin", "starts", "wq", "part_d", "x")


def back(n_dp, n_seq, own_ff, ff, kv_of, dtype, ins, shapes):
    tok, width = ins["x"].shape
    every = n_dp * tok
    q_width = ins["q"].shape[1]
    pair = 2 * HEAD_DIM
    length = n_seq * tok
    rank, columns = ins["wq"].shape[2:]
    outs = dict(
        out=shape_of((tok, width), dtype),
        grad_x=shape_of((tok, width), FULL),
        grad_o=shape_of((rank, width), FULL),
        grad_d=shape_of((ff, width), FULL),
        grad_q=shape_of(shapes["q"], LOW),
        grad_kv=shape_of((2,) + shapes["k"], FULL),
        grad_g=shape_of(shapes["gate"], LOW),
        grad_u=shape_of(shapes["gate"], LOW),
    )
    placed = {
        key + "_in" if key in LOADED else key: (
            value,
            ANY,
        )
        for key, value in ins.items()
    }
    scratch = {key: pltpu.VMEM(ins[key].shape, ins[key].dtype) for key in LOADED}
    scratch |= {key: pltpu.VMEM(value.shape, value.dtype) for key, value in outs.items()}
    scratch |= dict(
        store=dma(len(outs)),
        local=dma(4),
        load=dma(2 + len(LOADED)),
        got_q=vm(LOW, n_dp, rank, columns),
        down=DpScatter.scratch(n_dp, ff, width),
        kv_row=vm(LOW, 2, n_seq, tok, pair),
        dmid=vm(FULL, tok, width),
        d_own=vm(LOW, tok, width),
        d_all=vm(LOW, n_dp, tok, width),
        d_sem=DpGather.scratch(n_dp),
        do=vm(LOW, every, q_width),
        k2=vm(LOW, length, pair),
        v2=vm(LOW, length, pair),
        mask=vm(FULL, tok, length),
        dk2=vm(FULL, length, pair),
        dv2=vm(FULL, length, pair),
        dq=vm(FULL, every, q_width),
        dkv=vm(FULL, every, pair),
        dqkv=vm(LOW, every, columns),
        wide=vm(FULL, tok, width),
        landed_q=vm(LOW, n_dp, n_seq, rank, columns),
        part_kv=vm(LOW, n_seq, every, pair),
        part_q=vm(LOW, n_dp, n_seq, rank, columns),
        part_o=vm(LOW, n_seq, rank, width),
        back=DpScatter.scratch(n_dp, tok, width),
        ring_y=RingScatter.scratch(n_seq, tok, width),
        staged=RingScatter.staging(tok, width),
        ring_kv=RingScatter.scratch(n_seq, every, pair),
        ring_q=RingScatter.scratch(n_seq, n_dp, rank, columns),
        ring_o=RingScatter.scratch(n_seq, rank, width),
        swap_q=Exchange.scratch(n_dp),
        swap_gu=Exchange.scratch(n_seq),
        got_gu=vm(LOW, *ins["fin"].shape),
    )
    return run(
        functools.partial(back_kernel, n_dp, n_seq, own_ff, ff, kv_of),
        "attention_backward",
        3,
        placed,
        {key + "_to": (value, ANY) for key, value in outs.items()},
        scratch,
    )


def body(
    n_dp,
    n_seq,
    tokens,
    segment_ids,
    gain_attn,
    w_query,
    w_key,
    w_value,
    w_output,
    gain_mlp,
    w_gate,
    w_up,
    w_down,
    cotangent,
):
    local, width = tokens.shape[1], tokens.shape[2]
    length = n_seq * local
    own_rows = w_query.shape[0]
    own_ff = w_down.shape[0]
    ff = -(-own_ff // 16) * 16
    heads = HEADS // n_dp
    q_width = heads * HEAD_DIM
    x_own = tokens.reshape(local, width)
    dy_own = cotangent.reshape(local, width)

    kv_of = [i * heads // GROUP for i in range(n_dp)]
    freqs = ROPE_BASE ** (-jnp.arange(0, HEAD_DIM, 2).astype(FULL) / HEAD_DIM)
    got = front(
        n_dp,
        n_seq,
        own_ff,
        kv_of,
        dict(
            x=x_own,
            wg_in=w_gate,
            wu_in=w_up,
            wo=w_output,
            wd=jnp.pad(w_down, ((0, ff - own_ff), (0, 0))),
        ),
        dict(
            wq=w_query,
            wk=w_key,
            wv=w_value,
            gain_one=gain_attn.reshape(1, own_rows),
            gain_two=gain_mlp.reshape(1, own_rows),
            ids=segment_ids.reshape(1, local),
            freqs=jnp.broadcast_to(jnp.tile(freqs, 4), (8, 2 * HEAD_DIM)),
        ),
    )
    fed = feed(
        n_dp,
        n_seq,
        got["second"],
        dy_own,
        got["gu"].reshape(n_seq * own_rows, 2 * n_dp * ff),
        got["wd_all"],
    )
    ins = dict(
        part_y=fed["part_y"],
        grad_h=fed["grad_h_to"],
        fin=fed["fin_to"].reshape(got["gu"].shape),
        part_d=fed["grad_d"],
        x=x_own,
        dy=dy_own,
        middle=got["middle"],
    )
    for name in ("n1", "q", "kv", "o", "lse", "cos", "sin", "starts", "wq", "wo"):
        ins[name] = got[name + "_out"]
    done = back(
        n_dp,
        n_seq,
        own_ff,
        ff,
        kv_of,
        tokens.dtype,
        ins,
        dict(q=w_query.shape, k=w_key.shape, gate=w_gate.shape),
    )
    return finish(
        {key[: -len("_to")]: value for key, value in done.items()}
        | dict(
            gain_one=gain_attn.reshape(1, own_rows),
            gain_two=gain_mlp.reshape(1, own_rows),
            wq=w_query,
            wk=w_key,
            wv=w_value,
            wg=w_gate,
            wu=w_up,
        ),
        tokens.shape,
        own_ff,
    )


def finish_kernel(m):
    names = ("wg", "grad_g", "wu", "grad_u", "wq", "grad_q", "grad_x", "grad_d", "out", "grad_o")
    loads = {
        name: pltpu.make_async_copy(getattr(m, name), getattr(m, name + "_v"), m.load.at[k])
        for k, name in enumerate(names)
    }
    for copy in loads.values():
        copy.start()
    stores = []

    def store(src, dst):
        copy = pltpu.make_async_copy(src, dst, m.store.at[len(stores)])
        copy.start()
        stores.append(copy)

    def one(gain, weight, raw, into):
        raw = raw[...].astype(FULL)
        into[...] = gain * raw
        return jnp.sum(weight[...].astype(FULL) * raw, 1, keepdims=True)

    def whole(gain, weight, raw, into, target):
        loads[weight].wait()
        loads[raw].wait()
        part = one(gain, getattr(m, weight + "_v"), getattr(m, raw + "_v"), into)
        store(into, target)
        return part

    gain_one = to_column(m.gain_one[...])
    gain_two = to_column(m.gain_two[...])
    by_g = whole(gain_two, "wg", "grad_g", m.into_g, m.to_g)
    by_u = whole(gain_two, "wu", "grad_u", m.into_u, m.to_u)
    by_q = whole(gain_one, "wq", "grad_q", m.into_q, m.to_q)
    by_k = one(gain_one, m.wk, m.grad_kv.at[0], m.to_k)
    by_v = one(gain_one, m.wv, m.grad_kv.at[1], m.to_v)
    for name, target in (("grad_x", m.to_x), ("grad_d", m.to_d), ("out", m.to_out), ("grad_o", m.to_o)):
        loads[name].wait()
        store(getattr(m, name + "_v"), target)
    m.to_gain_one[...] = to_row(by_q + by_k + by_v)
    m.to_gain_two[...] = to_row(by_g + by_u)
    for copy in stores:
        copy.wait()


def finish(ins, shape, own_ff):
    rows = ins["wq"].shape[0]
    held = ("gain_one", "gain_two", "wk", "wv", "grad_kv")
    placed = {key: (value, VMEM if key in held else ANY) for key, value in ins.items()}
    outs = dict(
        to_out=(shape_of(ins["out"].shape, ins["out"].dtype), ANY),
        to_x=(shape_of(ins["grad_x"].shape, FULL), ANY),
        to_gain_one=(shape_of((1, rows), FULL), VMEM),
        to_q=(shape_of(ins["wq"].shape, FULL), ANY),
        to_k=(shape_of(ins["wk"].shape, FULL), VMEM),
        to_v=(shape_of(ins["wv"].shape, FULL), VMEM),
        to_o=(shape_of(ins["grad_o"].shape, FULL), ANY),
        to_gain_two=(shape_of((1, rows), FULL), VMEM),
        to_g=(shape_of(ins["wg"].shape, FULL), ANY),
        to_u=(shape_of(ins["wu"].shape, FULL), ANY),
        to_d=(shape_of(ins["grad_d"].shape, FULL), ANY),
    )
    scratch = dict(load=dma(10), store=dma(7))
    for name in ("g", "u", "q"):
        scratch["into_" + name] = vm(FULL, *ins["w" + name].shape)
    for key, value in ins.items():
        if key not in held:
            scratch[key + "_v"] = pltpu.VMEM(value.shape, value.dtype)
    done = run(finish_kernel, "finish", None, placed, outs, scratch)
    done = list(done.values())
    for k in (0, 1):
        done[k] = done[k].reshape(shape)
    for k in (2, 7):
        done[k] = done[k].reshape(rows)
    done[10] = done[10][:own_ff]
    return tuple(done)


def solution(mesh):
    rows = P(("dp", "seq"), None)
    vector = P(("dp", "seq"))
    row = P("dp", "seq", None)
    return jax.shard_map(
        functools.partial(body, mesh.shape["dp"], mesh.shape["seq"]),
        mesh=mesh,
        in_specs=(row, P("dp", "seq"), vector, rows, rows, rows, rows, vector, rows, rows, rows, row),
        out_specs=(row, row, vector, rows, rows, rows, rows, vector, rows, rows, rows),
        check_vma=False,
    )
```

```python
import functools
import math

import jax
import jax.numpy as jnp
from jax import lax
from jax.experimental import pallas as pl
from jax.experimental.pallas import tpu as pltpu
from jax.sharding import PartitionSpec as P

HEADS = 32
HEAD_DIM = 64
KV_HEADS = 4
GROUP = HEADS // KV_HEADS

EPS = 1e-05
ROPE_BASE = 10000.0
MASK_VALUE = -1e30
MESH = pl.DeviceIdType.MESH
LOW = jnp.bfloat16
FULL = jnp.float32
VMEM_BYTES = 61 * 1024 * 1024


def matmul(left, right):
    return jnp.dot(left, right, preferred_element_type=FULL)


def matmul_nt(left, right):
    return lax.dot_general(left, right, (((1,), (1,)), ((), ())), preferred_element_type=FULL)


def matmul_tn(left, right):
    return lax.dot_general(left, right, (((0,), (0,)), ((), ())), preferred_element_type=FULL)


def ring_at(place, n):
    upper = lax.div(place, n // 2)
    return (1 - upper) * 2 * place + upper * (2 * (n - place) - 1)


def ring_place(index, n):
    odd = lax.rem(index, 2)
    return (1 - odd) * lax.div(index, 2) + odd * (n - lax.div(index + 1, 2))


class Where:
    def __init__(self, n_dp, n_seq):
        self.n_dp, self.n_seq = n_dp, n_seq
        self.chips = n_dp // 2
        self.dp = lax.axis_index("dp")
        self.seq = lax.axis_index("seq")
        self.core = lax.rem(self.dp, 2)
        self.chip = lax.div(self.dp, 2)
        self.place = ring_place(self.seq, n_seq)

    def ring(self, step):
        return ring_at(lax.rem(self.place + step + self.n_seq, self.n_seq), self.n_seq)

    def ring_ids(self):
        return [(self.dp, self.ring(1)), (self.dp, self.ring(-1))]

    def seq_ids(self):
        return [
            (self.dp, lax.rem(self.seq + k, self.n_seq)) for k in range(1, self.n_seq)
        ]

    def dp_ids(self):
        return [(lax.rem(self.dp + k, self.n_dp), self.seq) for k in range(1, self.n_dp)]

    def core_id(self):
        return (self.dp + 1 - 2 * self.core, self.seq)

    def chip_ids(self):
        return [
            (2 * lax.rem(self.chip + k, self.chips) + self.core, self.seq)
            for k in range(1, self.chips)
        ]


def greet(ids):
    barrier = pltpu.get_barrier_semaphore()
    for one in ids:
        pl.semaphore_signal(barrier, inc=1, device_id=one, device_id_type=MESH)
    pl.semaphore_wait(barrier, len(ids))


def remote(src, dst, send, recv, target):
    return pltpu.make_async_remote_copy(
        src_ref=src,
        dst_ref=dst,
        send_sem=send,
        recv_sem=recv,
        device_id=target,
        device_id_type=MESH,
    )


class Ring:
    def __init__(self, at, shape, send, recv):
        self.at, self.send, self.recv = at, send, recv
        self.steps = at.n_seq // 2
        self.halves = 2 if len(shape) > 2 or shape[0] % 32 == 0 else 1
        self.half = shape[0] // self.halves
        self.copies = {}

    @staticmethod
    def semaphores(n_seq):
        shape = (2, n_seq // 2, 2)
        return [pltpu.SemaphoreType.DMA(shape), pltpu.SemaphoreType.DMA(shape)]

    def opposite(self, h, d):
        return d == h if self.halves == 2 else d == 0

    def rows(self, h):
        return pl.ds(h * self.half, self.half)

    def go(self, src, dst, d, t, h):
        target = self.at.ring_ids()[d]
        copy = remote(src, dst, self.send.at[d, t, h], self.recv.at[d, t, h], target)
        copy.start()
        self.copies[(d, t, h)] = copy

    def pieces(self):
        return [(h, d) for h in range(self.halves) for d in (0, 1)]


class RingGather(Ring):
    def __init__(self, at, own, everything, send, recv, local):
        super().__init__(at, own.shape, send, recv)
        self.own, self.everything = own, everything
        self.kept = pltpu.make_async_copy(own, everything.at[at.seq], local)
        self.waited = set()

    @staticmethod
    def scratch(n_seq):
        return Ring.semaphores(n_seq)

    def wait(self, key):
        self.copies[key].wait_recv()
        self.waited.add(key)

    def step(self, t):
        if t == 0:
            self.kept.start()
        if t == 1:
            self.kept.wait()
        for h, d in self.pieces():
            if t == self.steps - 1 and not self.opposite(h, d):
                continue
            if t > 0:
                self.wait((d, t - 1, h))
            origin = self.at.ring(-t if d == 0 else t)
            dst = self.everything.at[origin, self.rows(h)]
            self.go(self.own.at[self.rows(h)] if t == 0 else dst, dst, d, t, h)

    def rest(self, t):
        for key in self.copies:
            if key not in self.waited and key[1] <= t:
                self.wait(key)

    def finish(self):
        self.rest(self.steps)
        for copy in self.copies.values():
            copy.wait_send()
        if self.steps == 1:
            self.kept.wait()


class RingScatter(Ring):
    def __init__(self, at, parts, slots, send, recv, staged=None, loads=None, axis=0):
        shape = parts.shape[1:] if axis == 0 else parts.shape[:1] + parts.shape[2:]
        super().__init__(at, shape, send, recv)
        self.axis = axis
        self.parts, self.slots, self.staged, self.loads = parts, slots, staged, loads

    @staticmethod
    def scratch(n_seq, *block):
        return [pltpu.VMEM((2, n_seq // 2) + block, LOW)] + Ring.semaphores(n_seq)

    @staticmethod
    def staging(*block):
        return [pltpu.VMEM((2,) + block, LOW), pltpu.SemaphoreType.DMA((2, 2))]

    def there(self, t, d):
        return self.at.ring(self.steps - t if d == 0 else t - self.steps)

    def block(self, index, h):
        if self.axis:
            return self.parts.at[self.rows(h), index]
        return self.parts.at[index, self.rows(h)]

    def adds(self, t, h, d):
        return t > 1 or (t == 1 and self.opposite(h, d))

    def load(self, t, h, d):
        rows = self.rows(h)
        return pltpu.make_async_copy(self.block(self.there(t, d), h), self.staged.at[d, rows], self.loads.at[d, h])

    def load_all(self, t):
        if self.staged is not None:
            for h, d in self.pieces():
                if t < self.steps and self.adds(t, h, d):
                    self.load(t, h, d).start()
                elif t == self.steps and d == 0:
                    self.load(t, h, d).start()

    def early(self):
        for h, d in self.pieces():
            if self.steps > 1 and not self.opposite(h, d):
                self.go(self.block(self.there(1, d), h), self.slots.at[d, 1, self.rows(h)], d, 1, h)

    def step(self, t):
        if t == 0:
            self.load_all(1)
        for h, d in self.pieces():
            if (t == 0 and not self.opposite(h, d)) or (d, t, h) in self.copies:
                continue
            rows = self.rows(h)
            src = self.block(self.there(t, d), h)
            if self.adds(t, h, d):
                if self.staged is not None:
                    self.load(t, h, d).wait()
                    src = self.staged.at[d, rows]
                self.copies[(d, t - 1, h)].wait_recv()
                held = self.slots.at[d, t - 1, rows]
                held[...] = (held[...].astype(FULL) + src[...].astype(FULL)).astype(LOW)
                src = held
            self.go(src, self.slots.at[d, t, rows], d, t, h)
        if t > 0:
            self.load_all(t + 1)

    def finish(self, out):
        last = self.steps - 1
        if last == 0:
            self.load_all(1)
        for h in range(self.halves):
            rows = self.rows(h)
            if self.staged is None:
                total = self.block(self.at.seq, h)[...].astype(FULL)
            else:
                self.load(self.steps, h, 0).wait()
                total = self.staged[0, rows].astype(FULL)
            for d in (0, 1):
                if last == 0 and not self.opposite(h, d):
                    continue
                self.copies[(d, last, h)].wait_recv()
                total = total + self.slots[d, last, rows].astype(FULL)
            out[rows] = total.astype(out.dtype)
        for copy in self.copies.values():
            copy.wait_send()


class Exchange:
    def __init__(self, me, ids, axis, packed, landing, send, recv, local):
        self.started = 0
        self.kept = pltpu.make_async_copy(packed.at[me], landing.at[me], local)
        self.copies = [
            remote(packed.at[one[axis]], landing.at[me], send.at[k], recv.at[k], one)
            for k, one in enumerate(ids)
        ]

    @staticmethod
    def scratch(n):
        return [pltpu.SemaphoreType.DMA((n - 1,)), pltpu.SemaphoreType.DMA((n - 1,))]

    def start(self, count=None):
        if not self.started:
            self.kept.start()
        first = self.started - 1 if self.started else 0
        last = len(self.copies) if count is None else min(first + count, len(self.copies))
        for copy in self.copies[first:last]:
            copy.start()
        self.started = last + 1

    def arrived(self):
        self.kept.wait()
        for copy in self.copies:
            copy.wait_recv()

    def finish(self):
        for copy in self.copies:
            copy.wait_send()


def seq_exchange(at, *refs):
    return Exchange(at.seq, at.seq_ids(), 1, *refs)


def dp_exchange(at, *refs):
    return Exchange(at.dp, at.dp_ids(), 0, *refs)


class DpGather:
    def __init__(self, at, own, everything, send, recv, local):
        self.kept = pltpu.make_async_copy(own, everything.at[at.dp], local)
        slot = everything.at[at.dp]
        self.out = [
            remote(own, slot, send.at[k], recv.at[k], one) for k, one in enumerate(at.chip_ids())
        ]
        base = at.chips - 1
        self.mate = remote(own, slot, send.at[base], recv.at[base], at.core_id())
        self.handed = []
        for k in range(1, at.chips):
            origin = 2 * lax.rem(at.chip + at.chips - k, at.chips) + at.core
            there = everything.at[origin]
            self.handed.append(
                remote(there, there, send.at[base + k], recv.at[base + k], at.core_id())
            )

    @staticmethod
    def scratch(n_dp):
        return [pltpu.SemaphoreType.DMA((n_dp - 1,)), pltpu.SemaphoreType.DMA((n_dp - 1,))]

    def start(self):
        for copy in self.out:
            copy.start()
        self.mate.start()
        self.kept.start()

    def hand(self):
        for copy, onward in zip(self.out, self.handed):
            copy.wait_recv()
            onward.start()

    def arrived(self):
        self.kept.wait()
        self.mate.wait_recv()
        for copy in self.handed:
            copy.wait_recv()

    def finish(self):
        for copy in self.out + [self.mate] + self.handed:
            copy.wait_send()


def add_rows(rows, chunk, one):
    def step(r, carry):
        one(pl.ds(pl.multiple_of(r * chunk, chunk), chunk))
        return carry

    lax.fori_loop(0, rows // chunk, step, 0)


def chunk_of(rows, columns):
    chunk = rows
    while chunk % 32 == 0 and chunk * columns > 65536:
        chunk //= 2
    return chunk


class DpScatter:
    def __init__(self, at, parts, core, other, send, recv):
        self.at, self.parts, self.core, self.other = at, parts, core, other
        self.send, self.recv = send, recv
        self.rows, self.columns = parts.shape[1], parts.shape[2]

    @staticmethod
    def scratch(n_dp, rows, columns):
        chips = n_dp // 2
        return [
            pltpu.VMEM((chips, rows, columns), LOW),
            pltpu.VMEM((max(chips - 1, 1), rows, columns), LOW),
            pltpu.SemaphoreType.DMA((2 * chips - 1,)),
            pltpu.SemaphoreType.DMA((2 * chips - 1,)),
        ]

    def to_core(self, k):
        at = self.at
        return remote(
            self.parts.at[2 * k + 1 - at.core],
            self.core.at[k],
            self.send.at[k],
            self.recv.at[k],
            at.core_id(),
        )

    def to_chip(self, k):
        at = self.at
        sem = at.chips + k - 1
        return remote(
            self.core.at[lax.rem(at.chip + k, at.chips)],
            self.other.at[k - 1],
            self.send.at[sem],
            self.recv.at[sem],
            at.chip_ids()[k - 1],
        )

    def start(self):
        for k in range(self.at.chips):
            self.to_core(k).start()

    def add_core(self, k):
        held = self.core.at[k]
        mine = self.parts.at[2 * k + self.at.core]

        def one(rows):
            held[rows] = (held[rows].astype(FULL) + mine[rows].astype(FULL)).astype(LOW)

        add_rows(self.rows, chunk_of(self.rows, self.columns), one)

    def across(self):
        at = self.at
        for k in range(1, at.chips):
            there = lax.rem(at.chip + k, at.chips)
            self.to_core(there).wait_recv()
            self.add_core(there)
            self.to_chip(k).start()

    def finish(self, out):
        at = self.at
        self.to_core(at.chip).wait_recv()
        for k in range(1, at.chips):
            self.to_chip(k).wait_recv()
        held = self.core.at[at.chip]
        mine = self.parts.at[2 * at.chip + at.core]

        def one(rows):
            total = held[rows].astype(FULL) + mine[rows].astype(FULL)
            for k in range(1, at.chips):
                total = total + self.other[k - 1, rows].astype(FULL)
            out[rows] = total.astype(out.dtype)

        add_rows(self.rows, chunk_of(self.rows, self.columns), one)
        for k in range(at.chips):
            self.to_core(k).wait_send()
        for k in range(1, at.chips):
            self.to_chip(k).wait_send()


def comm_params(number):
    if number is None:
        return pltpu.CompilerParams(vmem_limit_bytes=VMEM_BYTES)
    return pltpu.CompilerParams(
        collective_id=number, has_side_effects=True, vmem_limit_bytes=VMEM_BYTES
    )


ANY = pl.BlockSpec(memory_space=pl.ANY)
VMEM = pl.BlockSpec(memory_space=pltpu.VMEM)


def shape_of(dims, kind):
    return jax.ShapeDtypeStruct(dims, kind)


class Refs:
    def __init__(self, names, refs):
        refs = list(refs)
        for name, count in names:
            taken, refs = refs[: max(count, 1)], refs[max(count, 1) :]
            setattr(self, name, taken if count else taken[0])


def run(kernel, name, number, ins, outs, scratch):
    names = [(key, 0) for key in ins] + [(key, 0) for key in outs]
    shapes = []
    for key, value in scratch.items():
        if isinstance(value, list):
            names.append((key, len(value)))
            shapes += value
        else:
            names.append((key, 0))
            shapes.append(value)
    found = pl.pallas_call(
        lambda *refs: kernel(Refs(names, refs)),
        name=name,
        out_shape=[shape for shape, _ in outs.values()],
        in_specs=[spec for _, spec in ins.values()],
        out_specs=[spec for _, spec in outs.values()],
        scratch_shapes=shapes,
        compiler_params=comm_params(number),
    )(*[array for array, _ in ins.values()])
    return dict(zip(outs, found))


def dma(*dims):
    return pltpu.SemaphoreType.DMA(dims)


def vm(kind, *dims):
    return pltpu.VMEM(dims, kind)


def lanes(rows):
    return lax.broadcasted_iota(jnp.int32, (rows, 2 * HEAD_DIM), 1)


def low_head(rows):
    return lanes(rows) < HEAD_DIM


def swapped(pair):
    half = HEAD_DIM // 2
    first = lax.rem(lanes(pair.shape[0]), HEAD_DIM) < half
    return jnp.where(
        first, pltpu.roll(pair, 2 * HEAD_DIM - half, 1), pltpu.roll(pair, half, 1)
    )


def split_heads(pair):
    wide = pair.astype(FULL)
    low = low_head(pair.shape[0])
    return jnp.concatenate(
        [jnp.where(low, wide, 0.0), jnp.where(low, 0.0, wide)], 0
    ).astype(LOW)


def join_heads(both):
    rows = both.shape[0] // 2
    return jnp.where(low_head(rows), both[:rows], both[rows:])


def spread_kv(kv):
    wide = kv.astype(FULL)
    turned = pltpu.roll(wide, HEAD_DIM, 1)
    low = low_head(kv.shape[0])
    return jnp.where(low, wide, turned).astype(LOW), jnp.where(low, turned, wide).astype(LOW)


def mask_of(position, start, length):
    key = lax.broadcasted_iota(jnp.int32, (start.shape[0], length), 1)
    return jnp.where((key <= position) & (key >= start), 0.0, MASK_VALUE)


def own_positions(at, tok):
    return at.seq * tok + lax.broadcasted_iota(jnp.int32, (tok, 1), 0)


def rows_of(r, count):
    return pl.ds(pl.multiple_of(r * count, count), count)


def to_column(row):
    n = row.shape[1]
    here = lax.broadcasted_iota(jnp.int32, (n, n), 0) == lax.broadcasted_iota(jnp.int32, (n, n), 1)
    return jnp.sum(jnp.where(here, row.astype(FULL), 0.0), 1, keepdims=True)


def to_row(column):
    n = column.shape[0]
    here = lax.broadcasted_iota(jnp.int32, (n, n), 0) == lax.broadcasted_iota(jnp.int32, (n, n), 1)
    return jnp.sum(jnp.where(here, column, 0.0), 0, keepdims=True)


def front_kernel(n_dp, n_seq, own_ff, ff, kv_of, m):
    at = Where(n_dp, n_seq)
    tok, width = m.x.shape
    q_width = m.q.shape[1]
    groups = q_width // (2 * HEAD_DIM)
    rank = n_seq * m.pq.shape[1]
    length = n_seq * tok
    greet(at.seq_ids() + at.dp_ids())
    swap_q = dp_exchange(at, m.pq, m.landed, *m.swap_q_sem, m.local.at[0])
    x_g = DpGather(at, m.x, m.xs, *m.x_sem, m.local.at[1])
    row_x = seq_exchange(at, m.seg_rows, m.seg_row, *m.row_x_sem, m.local.at[2])
    row_g = DpGather(at, m.seg_row, m.segs, *m.row_g_sem, m.local.at[3])
    col_g = DpGather(at, m.seg_col, m.seg_cols, *m.col_g_sem, m.local.at[4])
    ring_q = RingGather(at, m.landed, m.wq_all, *m.ring_q_sem, m.local.at[5])
    ring_o = RingGather(at, m.wo, m.wo_all, *m.ring_o_sem, m.local.at[6])
    ring_kv = RingGather(at, m.kv_own, m.kv_all, *m.ring_kv_sem, m.local.at[7])
    swap_gu = seq_exchange(at, m.pgu, m.gu, *m.swap_gu_sem, m.local.at[8])
    down = DpGather(at, m.wd, m.wd_all, *m.down_sem, m.local.at[9])
    loads = [
        pltpu.make_async_copy(src, dst, m.load.at[k])
        for k, (src, dst) in enumerate(((m.wg_in, m.wg), (m.wu_in, m.wu), (m.x, m.x_own)))
    ]
    stores = []

    def store(src, dst):
        copy = pltpu.make_async_copy(src, dst, m.local.at[10 + len(stores)])
        copy.start()
        stores.append(copy)

    ring_o.step(0)
    for copy in loads:
        copy.start()

    for i, kv in enumerate(kv_of):
        m.pq[i, :, :q_width] = m.wq[:, i * q_width : (i + 1) * q_width]
        for weight, first in ((m.wk, q_width), (m.wv, q_width + HEAD_DIM)):
            m.pq[i, :, first : first + HEAD_DIM] = weight[:, kv * HEAD_DIM : (kv + 1) * HEAD_DIM]
    swap_q.start()
    x_g.start()
    ids = m.ids[...]
    rank_own = m.pq.shape[1]
    m.seg_rows[...] = jnp.broadcast_to(ids.astype(FULL)[None], m.seg_rows.shape)
    for k, own_gain in ((1, m.gain_one), (2, m.gain_two)):
        m.seg_rows[:, k : k + 1, :rank_own] = jnp.broadcast_to(
            own_gain[...].astype(FULL)[None], (n_seq, 1, rank_own)
        )
    m.seg_col[...] = jnp.broadcast_to(to_column(ids), m.seg_col.shape)
    row_x.start()
    col_g.start()

    def pack(k, weight, first):
        loads[k].wait()
        if ff > own_ff:
            m.pgu[:, :, first : first + n_dp * ff] = jnp.zeros(
                m.pgu.shape[:2] + (n_dp * ff,), LOW
            )
        for s in range(n_seq):
            for i in range(n_dp):
                piece = weight[:, (i * n_seq + s) * own_ff : (i * n_seq + s + 1) * own_ff]
                m.pgu[s, :, first + i * ff : first + i * ff + own_ff] = piece

    later = list(range(1, ring_o.steps))
    ring_o.step(later.pop(0))
    swap_q.arrived()
    ring_q.step(0)
    row_x.arrived()
    row_g.start()

    def hand():
        x_g.hand()
        row_g.hand()
        col_g.hand()
        down.start()

    def norm():
        x_g.arrived()
        row_g.arrived()
        m.gains[...] = jnp.zeros_like(m.gains)
        for k in (0, 1):
            for i in range(n_dp):
                for s in range(n_seq):
                    first = (i * n_seq + s) * rank_own
                    m.gains[k : k + 1, first : first + rank_own] = m.segs[
                        i, s, k + 1 : k + 2, :rank_own
                    ]
        store(m.gains, m.gains_out)
        for r in range(n_dp):
            x = m.xs[r].astype(FULL)
            scale = lax.rsqrt(jnp.mean(x * x, -1, keepdims=True) + EPS)
            m.n1[r] = (x * scale * m.gains[:1]).astype(LOW)
        store(m.n1, m.n1_out)

    def place():
        col_g.arrived()
        position = own_positions(at, tok)
        first = lax.rem(lanes(tok), HEAD_DIM) < HEAD_DIM // 2
        number = lax.rem(lanes(tok), HEAD_DIM // 2).astype(FULL)
        freqs = jnp.exp(number * (-2.0 * math.log(ROPE_BASE) / HEAD_DIM))
        for r in range(n_dp):
            segs = jnp.concatenate([m.segs[r, s, :1] for s in range(n_seq)], 1)
            own = m.seg_cols[r][:, :1]
            start = jnp.sum((segs < own).astype(jnp.int32), 1, keepdims=True)
            turned = (position - start).astype(FULL) * freqs
            rows = slice(r * tok, (r + 1) * tok)
            m.cos[rows] = jnp.cos(turned)
            sines = jnp.sin(turned)
            m.sin[rows] = jnp.where(first, -sines, sines)
            m.starts[rows] = jnp.broadcast_to(start, (tok, 2 * HEAD_DIM))
        store(m.cos, m.cos_out)
        store(m.sin, m.sin_out)
        store(m.starts, m.starts_out)

    pack(0, m.wg, 0)
    ring_q.step(1)
    jobs = [lambda: (hand(), norm(), place()), lambda: pack(1, m.wu, n_dp * ff)]
    for t in range(2, ring_q.steps):
        ring_q.step(t)
        if jobs:
            jobs.pop(0)()
    for job in jobs:
        job()
    ring_q.finish()
    if later:
        ring_o.step(later.pop(0))
    store(m.wq_all, m.wq_out)

    m.qkv[...] = sum(
        matmul(
            m.n1[:, :, i * rank : (i + 1) * rank].reshape(n_dp * tok, rank),
            m.wq_all[:, i].reshape(rank, q_width + 2 * HEAD_DIM),
        )
        for i in range(n_dp)
    )
    factor = HEAD_DIM ** (-0.5)
    for g in range(groups + 1):
        cols = slice(g * 2 * HEAD_DIM, (g + 1) * 2 * HEAD_DIM)
        pair = m.qkv[:, cols]
        turned = pair * m.cos[...] + swapped(pair) * m.sin[...]
        if g < groups:
            m.q[:, cols] = (turned * factor).astype(LOW)
        else:
            m.kv_own[...] = jnp.where(low_head(pair.shape[0]), turned, pair).astype(LOW)
    ring_kv.step(0)
    store(m.q, m.q_out)
    for t in range(1, ring_kv.steps):
        ring_kv.step(t)
        if later and t > 1:
            ring_o.step(later.pop(0))
    for t in later:
        ring_o.step(t)
    down.hand()
    ring_kv.finish()
    store(m.kv_all, m.kv_out)
    m.lse[...] = jnp.zeros_like(m.lse)
    for r in range(n_dp):
        rows = slice(r * tok, (r + 1) * tok)
        k, v = spread_kv(m.kv_all[:, rows].reshape(length, 2 * HEAD_DIM))
        m.k2[...] = k
        m.v2[...] = v
        m.mask[...] = mask_of(own_positions(at, tok), m.starts[rows, :1], length)

        def group(g, carry):
            cols = rows_of(g, 2 * HEAD_DIM)
            raw = matmul_nt(split_heads(m.q[rows, cols]), m.k2[...])
            raw = raw + jnp.concatenate([m.mask[...]] * 2, 0)
            top = jnp.max(raw, -1, keepdims=True)
            probs = jnp.exp(raw - top)
            total = jnp.sum(probs, -1, keepdims=True)
            probs = (probs * (1.0 / total)).astype(LOW)
            m.o[rows, cols] = join_heads(matmul(probs, m.v2[...])).astype(LOW)
            here = lanes(2 * tok) == r * groups + g
            m.lse[...] = jnp.where(here, top + jnp.log(total), m.lse[...])
            return carry

        lax.fori_loop(0, groups, group, 0)
        if r == 0:
            swap_gu.start()
    store(m.o, m.o_out)
    store(m.lse, m.lse_out)
    ring_o.finish()
    store(m.wo_all, m.wo_out)
    full = m.wo_all[...].reshape(q_width, width)
    for r in range(n_dp):
        m.parts[r] = matmul(m.o[r * tok : (r + 1) * tok], full).astype(LOW)
    back = DpScatter(at, m.parts, *m.back)
    back.start()
    back.across()
    back.finish(m.middle)
    loads[2].wait()
    middle = m.x_own[...].astype(FULL) + m.middle[...]
    m.middle[...] = middle
    scale = lax.rsqrt(jnp.mean(middle * middle, -1, keepdims=True) + EPS)
    m.second[...] = (middle * scale * m.gains[1:2]).astype(LOW)
    swap_gu.arrived()
    down.arrived()
    for one in (swap_q, x_g, row_x, row_g, col_g, swap_gu, down):
        one.finish()
    for copy in stores:
        copy.wait()


def front(n_dp, n_seq, own_ff, kv_of, held, small):
    tok, width = held["x"].shape
    rank = small["wq"].shape[0]
    q_width = width // n_dp
    groups = q_width // (2 * HEAD_DIM)
    pair = 2 * HEAD_DIM
    columns = q_width + pair
    length = n_seq * tok
    every = n_dp * tok
    wd = held["wd"]
    ff = wd.shape[0]
    gu_width = 2 * n_dp * ff
    ins = {key: (value, ANY) for key, value in held.items()}
    ins |= {key: (value, VMEM) for key, value in small.items()}
    kept = dict(
        n1=(LOW, n_dp, tok, width),
        q=(LOW, every, q_width),
        kv_all=(LOW, n_seq, every, pair),
        o=(LOW, every, q_width),
        lse=(FULL, 2 * tok, pair),
        cos=(FULL, every, pair),
        sin=(FULL, every, pair),
        starts=(jnp.int32, every, pair),
        gains=(FULL, 8, width),
        wq_all=(LOW, n_seq, n_dp, rank, columns),
        wo_all=(LOW, n_seq, rank, width),
    )
    outs = {
        key.replace("_all", "") + "_out": (shape_of(dims[1:], dims[0]), ANY)
        for key, dims in kept.items()
    }
    outs["gu"] = (shape_of((n_seq, rank, gu_width), LOW), ANY)
    outs["wd_all"] = (shape_of((n_dp,) + wd.shape, LOW), ANY)
    outs["middle"] = (shape_of((tok, width), FULL), VMEM)
    outs["second"] = (shape_of((tok, width), LOW), VMEM)
    scratch = {key: vm(*dims) for key, dims in kept.items()}
    scratch |= dict(
        load=dma(3),
        wg=vm(LOW, *held["wg_in"].shape),
        wu=vm(LOW, *held["wg_in"].shape),
        x_own=vm(LOW, tok, width),
        pq=vm(LOW, n_dp, rank, columns),
        seg_rows=vm(FULL, n_seq, 8, tok),
        seg_col=vm(FULL, tok, pair),
        landed=vm(LOW, n_dp, rank, columns),
        xs=vm(LOW, n_dp, tok, width),
        seg_row=vm(FULL, n_seq, 8, tok),
        segs=vm(FULL, n_dp, n_seq, 8, tok),
        seg_cols=vm(FULL, n_dp, tok, pair),
        kv_own=vm(LOW, every, pair),
        mask=vm(FULL, tok, length),
        pgu=vm(LOW, n_seq, rank, gu_width),
        qkv=vm(FULL, every, columns),
        k2=vm(LOW, length, pair),
        v2=vm(LOW, length, pair),
        parts=vm(LOW, n_dp, tok, width),
        back=DpScatter.scratch(n_dp, tok, width),
        local=dma(10 + len(kept)),
        swap_q_sem=Exchange.scratch(n_dp),
        x_sem=DpGather.scratch(n_dp),
        row_x_sem=Exchange.scratch(n_seq),
        row_g_sem=DpGather.scratch(n_dp),
        col_g_sem=DpGather.scratch(n_dp),
        ring_q_sem=Ring.semaphores(n_seq),
        ring_o_sem=Ring.semaphores(n_seq),
        ring_kv_sem=Ring.semaphores(n_seq),
        swap_gu_sem=Exchange.scratch(n_seq),
        down_sem=DpGather.scratch(n_dp),
    )
    return run(
        functools.partial(front_kernel, n_dp, n_seq, own_ff, ff, kv_of), "attention_forward", 1, ins, outs, scratch
    )


def feed_kernel(n_dp, n_seq, m):
    at = Where(n_dp, n_seq)
    tok, width = m.second.shape
    wide = m.wgu.shape[2]
    part = wide // 2
    rank = width // n_dp
    length = n_seq * tok
    greet(at.ring_ids() + at.dp_ids())
    gu = DpGather(at, m.gu, m.wgu, *m.gu_sem, m.local.at[0])
    ring_n = RingGather(at, m.second, m.second_all, *m.ring_n, m.local.at[1])
    ring_dy = RingGather(at, m.dy, m.dy_all, *m.ring_dy, m.local.at[2])
    ring_h = RingScatter(at, m.part, *m.ring_h)
    side = DpScatter(at, m.wgu, *m.side)
    gu.start()
    held = pltpu.make_async_copy(m.wd_all, m.wd, m.local.at[3])
    held.start()
    ring_n.step(0)
    for t in range(1, ring_n.steps):
        ring_n.step(t)
    ring_dy.step(0)
    gu.hand()
    ring_n.finish()
    gu.arrived()
    held.wait()
    stores = []

    def store(src, dst, k):
        copy = pltpu.make_async_copy(src, dst, m.local.at[k])
        copy.start()
        stores.append(copy)

    def stored():
        while stores:
            stores.pop().wait()

    def forward(c):
        blocks = slice(2 * c, 2 * c + 2)
        normed = m.second_all[blocks].reshape(2 * tok, width)
        both = matmul(normed, m.wgu[...].reshape(width, wide))
        gate, upward = both[:, :part], both[:, part:]
        sigma = jax.nn.sigmoid(gate)
        silu = gate * sigma
        hidden = (silu * upward).astype(LOW)
        m.by_up[blocks] = silu.reshape(2, tok, part)
        m.by_gate[blocks] = (upward * sigma * (1.0 + gate * (1.0 - sigma))).reshape(2, tok, part)
        m.hidden[blocks] = hidden.reshape(2, tok, part)
        out = matmul(hidden, m.wd[...].reshape(part, width))
        m.part[blocks] = out.astype(LOW).reshape(2, tok, width)
        copy = pltpu.make_async_copy(m.part.at[blocks], m.part_y.at[blocks], m.store.at[c])
        copy.start()
        stores.append(copy)

    def backward(blocks):
        rows = len(blocks) * tok
        dy = jnp.concatenate([m.dy_all[b] for b in blocks], 0)
        grad = matmul_nt(dy, m.wd[...].reshape(part, width))
        for k, b in enumerate(blocks):
            one = grad[k * tok : (k + 1) * tok]
            m.grads[b, :, :part] = (one * m.by_gate[b]).astype(LOW)
            m.grads[b, :, part:] = (one * m.by_up[b]).astype(LOW)
        both = jnp.concatenate([m.grads[b] for b in blocks], 0)
        for i in range(n_dp):
            cols = slice(i * rank, (i + 1) * rank)
            out = matmul_nt(both, m.wgu[i]).astype(LOW)
            for k, b in enumerate(blocks):
                m.part[b, :, cols] = out[k * tok : (k + 1) * tok]

    jobs = [functools.partial(forward, c) for c in range(n_seq // 2)]
    jobs.append(stored)
    jobs.append(lambda: backward([at.seq]))
    for t in range(1, ring_dy.steps):
        for _ in range(3 if t == 1 else 4):
            if jobs:
                jobs.pop(0)()
        ring_dy.step(t)
        if t < ring_dy.steps - 1:
            jobs.append(functools.partial(backward, [at.ring(-t), at.ring(t)]))
    for job in jobs:
        job()
    if ring_dy.steps > 1:
        ring_dy.rest(ring_dy.steps - 2)
        backward([at.ring(1 - ring_dy.steps), at.ring(ring_dy.steps - 1)])
    ring_h.early()
    ring_dy.finish()
    backward([at.ring(ring_dy.steps)])
    gu.finish()

    ring_h.step(0)

    def grad_gu(k):
        chip = lax.rem(at.chip + 1 + k, at.chips)
        for c in (1 - at.core, at.core):
            normed = m.second_all[:, :, rows_of(2 * chip + c, rank)].reshape(length, rank)
            m.wgu[2 * chip + c] = matmul_tn(normed, m.grads[...].reshape(length, wide)).astype(LOW)
            if c is not at.core:
                side.to_core(chip).start()

    def grad_down():
        step = width // n_dp
        for i in range(n_dp):
            cols = slice(i * step, (i + 1) * step)
            dy = m.dy_all[:, :, cols].reshape(length, step)
            m.wd[:, :, cols] = (
                matmul_tn(m.hidden[...].reshape(length, part), dy)
                .astype(LOW)
                .reshape(m.wd.shape[:2] + (step,))
            )
        store(m.wd, m.grad_d, 3)

    jobs = [functools.partial(grad_gu, k) for k in range(at.chips)]
    jobs += [side.across, grad_down]
    for t in range(1, ring_h.steps):
        for _ in range(2):
            if jobs:
                jobs.pop(0)()
        ring_h.step(t)
    for job in jobs:
        job()
    ring_h.finish(m.grad_h)
    store(m.grad_h, m.grad_h_to, 4)
    side.finish(m.fin)
    store(m.fin, m.fin_to, 5)
    stored()


def feed(n_dp, n_seq, second, dy, gu, wd):
    tok, width = second.shape
    deep, wide = gu.shape
    ff = wd.shape[1]
    part = wide // 2
    ins = dict(second=(second, ANY), dy=(dy, ANY), gu=(gu, ANY), wd_all=(wd, ANY))
    outs = dict(
        part_y=(shape_of((n_seq, tok, width), LOW), ANY),
        grad_h_to=(shape_of((tok, width), FULL), ANY),
        fin_to=(shape_of((deep, wide), LOW), ANY),
        grad_d=(shape_of(wd.shape, LOW), ANY),
    )
    scratch = dict(
        local=dma(6),
        grad_h=vm(FULL, tok, width),
        fin=vm(LOW, deep, wide),
        wd=vm(LOW, *wd.shape),
        store=dma(n_seq // 2),
        second_all=vm(LOW, n_seq, tok, width),
        dy_all=vm(LOW, n_seq, tok, width),
        wgu=vm(LOW, n_dp, deep, wide),
        by_gate=vm(FULL, n_seq, tok, part),
        by_up=vm(FULL, n_seq, tok, part),
        hidden=vm(LOW, n_seq, tok, part),
        grads=vm(LOW, n_seq, tok, wide),
        part=vm(LOW, n_seq, tok, width),
        gu_sem=DpGather.scratch(n_dp),
        ring_n=Ring.semaphores(n_seq),
        ring_dy=Ring.semaphores(n_seq),
        ring_h=RingScatter.scratch(n_seq, tok, width),
        side=DpScatter.scratch(n_dp, deep, wide),
    )
    return run(functools.partial(feed_kernel, n_dp, n_seq), "feed_forward", 2, ins, outs, scratch)


def back_kernel(n_dp, n_seq, own_ff, ff, kv_of, m):
    at = Where(n_dp, n_seq)
    tok, width = m.x.shape
    q_width = m.q.shape[1]
    groups = q_width // (2 * HEAD_DIM)
    rank = n_seq * m.wq.shape[2]
    length = n_seq * tok
    pair = 2 * HEAD_DIM
    greet(at.seq_ids() + at.dp_ids())
    swap_gu = [
        remote(m.fin.at[one[1]], m.got_gu.at[at.seq], m.swap_gu[0].at[k], m.swap_gu[1].at[k], one)
        for k, one in enumerate(at.seq_ids())
    ]
    ring_y = RingScatter(at, m.part_y, *m.ring_y, *m.staged)
    d_g = DpGather(at, m.d_own, m.d_all, *m.d_sem, m.local.at[0])
    ring_kv = RingScatter(at, m.part_kv, *m.ring_kv)
    ring_q = RingScatter(at, m.landed_q, *m.ring_q, axis=1)
    ring_o = RingScatter(at, m.part_o, *m.ring_o)
    down = DpScatter(at, m.part_d, *m.down)
    back = DpScatter(at, m.d_all, *m.back)
    swap_q = [
        remote(m.part_q.at[one[0]], m.landed_q.at[at.dp], m.swap_q[0].at[k], m.swap_q[1].at[k], one)
        for k, one in enumerate(at.dp_ids())
    ]
    ring_y.step(0)
    stores = []

    def store(key):
        copy = pltpu.make_async_copy(getattr(m, key), getattr(m, key + "_to"), m.store.at[len(stores)])
        copy.start()
        stores.append(copy)

    waiting = list(swap_gu)

    def pace(count=1):
        for copy in waiting[:count]:
            copy.start()
        del waiting[:count]

    loads = [
        pltpu.make_async_copy(getattr(m, key + "_in"), getattr(m, key), m.load.at[2 + k])
        for k, key in enumerate(LOADED)
    ]
    for copy in loads:
        copy.start()

    def load_kv(r):
        block = m.kv.at[:, pl.ds(r * tok, tok)]
        return pltpu.make_async_copy(block, m.kv_row.at[r % 2], m.load.at[r % 2])

    load_kv(0).start()
    own_gu = pltpu.make_async_copy(m.fin.at[at.seq], m.got_gu.at[at.seq], m.local.at[3])
    own_gu.start()

    def norm_back(grad, gain, value):
        grad = grad * gain
        scale = lax.rsqrt(jnp.mean(value * value, -1, keepdims=True) + EPS)
        normed = value * scale
        return scale * (grad - normed * jnp.mean(grad * normed, -1, keepdims=True))

    for copy in loads[:4]:
        copy.wait()
    m.dmid[...] = m.dy[...].astype(FULL) + norm_back(
        m.grad_h[...], m.gains[1:2], m.middle[...]
    )
    m.d_own[...] = m.dmid[...].astype(LOW)
    d_g.start()
    if ring_y.steps > 1:
        ring_y.step(1)
    d_g.hand()
    for copy in loads[4:]:
        copy.wait()
    d_g.arrived()
    down.start()
    m.do[...] = matmul_nt(
        m.d_all[...].reshape(n_dp * tok, width), m.wo[...].reshape(q_width, width)
    ).astype(LOW)
    later = list(range(2, ring_y.steps))
    down.across()
    if later:
        ring_y.step(later.pop(0))
    for r in range(n_dp):
        rows = slice(r * tok, (r + 1) * tok)
        load_kv(r).wait()
        if r + 1 < n_dp:
            load_kv(r + 1).start()
        k, v = spread_kv(m.kv_row[r % 2].reshape(length, pair))
        m.k2[...] = k
        m.v2[...] = v
        m.mask[...] = mask_of(own_positions(at, tok), m.starts[rows, :1], length)
        m.dk2[...] = jnp.zeros_like(m.dk2)
        m.dv2[...] = jnp.zeros_like(m.dv2)

        def group(g, carry):
            cols = rows_of(g, pair)
            q2 = split_heads(m.q[rows, cols])
            do2 = split_heads(m.do[rows, cols])
            raw = matmul_nt(q2, m.k2[...])
            raw = raw + jnp.concatenate([m.mask[...]] * 2, 0)
            here = lanes(2 * tok) == r * groups + g
            lse = jnp.sum(jnp.where(here, m.lse[...], 0.0), 1, keepdims=True)
            probs = jnp.exp(raw - lse)
            grad_probs = matmul_nt(do2, m.v2[...])
            delta = jnp.sum(probs * grad_probs, -1, keepdims=True)
            grad_raw = (probs * (grad_probs - delta)).astype(LOW)
            m.dq[rows, cols] = join_heads(matmul(grad_raw, m.k2[...]))
            m.dk2[...] += matmul_tn(grad_raw, q2)
            m.dv2[...] += matmul_tn(probs.astype(LOW), do2)
            return carry

        lax.fori_loop(0, groups, group, 0)
        dk = m.dk2[...]
        dv = m.dv2[...]
        dkv = jnp.where(
            low_head(length), dk + pltpu.roll(dk, HEAD_DIM, 1), dv + pltpu.roll(dv, HEAD_DIM, 1)
        )
        m.part_kv[:, rows] = dkv.astype(LOW).reshape(n_seq, tok, pair)
        if later and r % 2:
            ring_y.step(later.pop(0))
    for t in later:
        ring_y.step(t)
    ring_kv.step(0)
    m.part_o[...] = (
        matmul_tn(m.o[...], m.d_all[...].reshape(n_dp * tok, width))
        .astype(LOW)
        .reshape(m.part_o.shape)
    )
    d_g.finish()
    for t in range(1, ring_kv.steps):
        ring_kv.step(t)
        pace()
    ring_kv.finish(m.dkv)
    ring_o.step(0)
    factor = HEAD_DIM ** (-0.5)
    for g in range(groups + 1):
        cols = slice(g * pair, (g + 1) * pair)
        grad = m.dq[:, cols] * factor if g < groups else m.dkv[...]
        turned = grad * m.cos[...] - swapped(grad) * m.sin[...]
        if g == groups:
            turned = jnp.where(low_head(grad.shape[0]), turned, grad)
        m.dqkv[:, cols] = turned.astype(LOW)
    ring_y.finish(m.wide)
    n1 = m.ring_y[0].at[0, pl.ds(0, n_dp)]
    fetch = pltpu.make_async_copy(m.n1, n1, m.local.at[2])
    fetch.start()
    m.out[...] = (m.middle[...] + m.wide[...]).astype(m.out.dtype)
    store("out")
    pace()
    fetch.wait()
    for i in range(n_dp):
        cols = slice(i * rank, (i + 1) * rank)
        m.part_q[i] = (
            matmul_tn(n1[:, :, cols].reshape(n_dp * tok, rank), m.dqkv[...])
            .astype(LOW)
            .reshape(n_seq, rank // n_seq, q_width + pair)
        )
    for copy in swap_q:
        copy.start()
    m.landed_q[at.dp] = m.part_q[at.dp]
    pace()
    if ring_o.steps > 1:
        ring_o.step(1)
    pace()
    for i in range(n_dp):
        cols = slice(i * rank, (i + 1) * rank)
        weight = m.wq[:, i].reshape(rank, q_width + pair)
        m.d_all[:, :, cols] = (
            matmul_nt(m.dqkv[...], weight).astype(LOW).reshape(n_dp, tok, rank)
        )
    back.start()
    pace()
    pace(len(waiting))

    def unpack(grad, first):
        for s in range(n_seq):
            for i in range(n_dp):
                grad[:, (i * n_seq + s) * own_ff : (i * n_seq + s + 1) * own_ff] = m.got_gu[
                    s, :, first + i * ff : first + i * ff + own_ff
                ]

    def unpack_gate():
        for copy in swap_gu:
            copy.wait()
        own_gu.wait()
        unpack(m.grad_g, 0)
        store("grad_g")

    def unpack_up():
        unpack(m.grad_u, n_dp * ff)
        store("grad_u")

    def grad_inputs():
        back.finish(m.wide)
        m.grad_x[...] = m.dmid[...] + norm_back(
            m.wide[...], m.gains[:1], m.x[...].astype(FULL)
        )
        store("grad_x")

    def finish_down():
        down.finish(m.grad_d)
        store("grad_d")

    jobs = [finish_down, back.across]
    for t in range(2, ring_o.steps):
        ring_o.step(t)
        if jobs:
            jobs.pop(0)()
    jobs += [unpack_gate, unpack_up, grad_inputs]
    for copy in swap_q:
        copy.wait()
    ring_q.step(0)
    for t in range(1, ring_q.steps):
        ring_q.step(t)
        if jobs:
            jobs.pop(0)()
    for job in jobs:
        job()
    ring_o.finish(m.grad_o)
    store("grad_o")
    ring_q.finish(m.got_q)
    m.grad_kv[...] = jnp.zeros_like(m.grad_kv)
    for i, kv in enumerate(kv_of):
        m.grad_q[:, i * q_width : (i + 1) * q_width] = m.got_q[i, :, :q_width]
        for k in (0, 1):
            first = q_width + k * HEAD_DIM
            m.grad_kv[k, :, kv * HEAD_DIM : (kv + 1) * HEAD_DIM] += m.got_q[
                i, :, first : first + HEAD_DIM
            ].astype(FULL)
    store("grad_q")
    store("grad_kv")
    for copy in stores:
        copy.wait()


LOADED = ("grad_h", "dy", "middle", "gains", "wo", "q", "o", "lse", "cos", "sin", "starts", "wq", "part_d", "x")


def back(n_dp, n_seq, own_ff, ff, kv_of, dtype, ins, shapes):
    tok, width = ins["x"].shape
    every = n_dp * tok
    q_width = ins["q"].shape[1]
    pair = 2 * HEAD_DIM
    length = n_seq * tok
    rank, columns = ins["wq"].shape[2:]
    outs = dict(
        out=shape_of((tok, width), dtype),
        grad_x=shape_of((tok, width), FULL),
        grad_o=shape_of((rank, width), FULL),
        grad_d=shape_of((ff, width), FULL),
        grad_q=shape_of(shapes["q"], LOW),
        grad_kv=shape_of((2,) + shapes["k"], FULL),
        grad_g=shape_of(shapes["gate"], LOW),
        grad_u=shape_of(shapes["gate"], LOW),
    )
    placed = {
        key + "_in" if key in LOADED else key: (
            value,
            ANY,
        )
        for key, value in ins.items()
    }
    scratch = {key: pltpu.VMEM(ins[key].shape, ins[key].dtype) for key in LOADED}
    scratch |= {key: pltpu.VMEM(value.shape, value.dtype) for key, value in outs.items()}
    scratch |= dict(
        store=dma(len(outs)),
        local=dma(4),
        load=dma(2 + len(LOADED)),
        got_q=vm(LOW, n_dp, rank, columns),
        down=DpScatter.scratch(n_dp, ff, width),
        kv_row=vm(LOW, 2, n_seq, tok, pair),
        dmid=vm(FULL, tok, width),
        d_own=vm(LOW, tok, width),
        d_all=vm(LOW, n_dp, tok, width),
        d_sem=DpGather.scratch(n_dp),
        do=vm(LOW, every, q_width),
        k2=vm(LOW, length, pair),
        v2=vm(LOW, length, pair),
        mask=vm(FULL, tok, length),
        dk2=vm(FULL, length, pair),
        dv2=vm(FULL, length, pair),
        dq=vm(FULL, every, q_width),
        dkv=vm(FULL, every, pair),
        dqkv=vm(LOW, every, columns),
        wide=vm(FULL, tok, width),
        landed_q=vm(LOW, n_dp, n_seq, rank, columns),
        part_kv=vm(LOW, n_seq, every, pair),
        part_q=vm(LOW, n_dp, n_seq, rank, columns),
        part_o=vm(LOW, n_seq, rank, width),
        back=DpScatter.scratch(n_dp, tok, width),
        ring_y=RingScatter.scratch(n_seq, tok, width),
        staged=RingScatter.staging(tok, width),
        ring_kv=RingScatter.scratch(n_seq, every, pair),
        ring_q=RingScatter.scratch(n_seq, n_dp, rank, columns),
        ring_o=RingScatter.scratch(n_seq, rank, width),
        swap_q=Exchange.scratch(n_dp),
        swap_gu=Exchange.scratch(n_seq),
        got_gu=vm(LOW, *ins["fin"].shape),
    )
    return run(
        functools.partial(back_kernel, n_dp, n_seq, own_ff, ff, kv_of),
        "attention_backward",
        3,
        placed,
        {key + "_to": (value, ANY) for key, value in outs.items()},
        scratch,
    )


def body(
    n_dp,
    n_seq,
    tokens,
    segment_ids,
    gain_attn,
    w_query,
    w_key,
    w_value,
    w_output,
    gain_mlp,
    w_gate,
    w_up,
    w_down,
    cotangent,
):
    local, width = tokens.shape[1], tokens.shape[2]
    length = n_seq * local
    own_rows = w_query.shape[0]
    own_ff = w_down.shape[0]
    ff = -(-own_ff // 16) * 16
    heads = HEADS // n_dp
    q_width = heads * HEAD_DIM
    x_own = tokens.reshape(local, width)
    dy_own = cotangent.reshape(local, width)

    kv_of = [i * heads // GROUP for i in range(n_dp)]
    got = front(
        n_dp,
        n_seq,
        own_ff,
        kv_of,
        dict(
            x=x_own,
            wg_in=w_gate,
            wu_in=w_up,
            wo=w_output,
            wd=jnp.pad(w_down, ((0, ff - own_ff), (0, 0))),
        ),
        dict(
            wq=w_query,
            wk=w_key,
            wv=w_value,
            gain_one=gain_attn.reshape(1, own_rows),
            gain_two=gain_mlp.reshape(1, own_rows),
            ids=segment_ids.reshape(1, local),
        ),
    )
    fed = feed(
        n_dp,
        n_seq,
        got["second"],
        dy_own,
        got["gu"].reshape(n_seq * own_rows, 2 * n_dp * ff),
        got["wd_all"],
    )
    ins = dict(
        part_y=fed["part_y"],
        grad_h=fed["grad_h_to"],
        fin=fed["fin_to"].reshape(got["gu"].shape),
        part_d=fed["grad_d"],
        x=x_own,
        dy=dy_own,
        middle=got["middle"],
    )
    for name in ("n1", "q", "kv", "o", "lse", "cos", "sin", "starts", "gains", "wq", "wo"):
        ins[name] = got[name + "_out"]
    done = back(
        n_dp,
        n_seq,
        own_ff,
        ff,
        kv_of,
        tokens.dtype,
        ins,
        dict(q=w_query.shape, k=w_key.shape, gate=w_gate.shape),
    )
    return finish(
        {key[: -len("_to")]: value for key, value in done.items()}
        | dict(
            gain_one=gain_attn.reshape(1, own_rows),
            gain_two=gain_mlp.reshape(1, own_rows),
            wq=w_query,
            wk=w_key,
            wv=w_value,
            wg=w_gate,
            wu=w_up,
        ),
        tokens.shape,
        own_ff,
    )


def finish_kernel(m):
    names = ("wg", "grad_g", "grad_x", "grad_d", "out", "grad_o", "wu", "grad_u", "wq", "grad_q")
    loads = {
        name: pltpu.make_async_copy(getattr(m, name), getattr(m, name + "_v"), m.load.at[k])
        for k, name in enumerate(names)
    }
    for copy in loads.values():
        copy.start()
    stores = []

    def store(src, dst):
        copy = pltpu.make_async_copy(src, dst, m.store.at[len(stores)])
        copy.start()
        stores.append(copy)

    def one(weight, raw, into):
        raw = raw[...].astype(FULL)
        into[...] = raw
        return jnp.sum(weight[...].astype(FULL) * raw, 1, keepdims=True)

    def whole(weight, raw, into, target):
        loads[weight].wait()
        loads[raw].wait()
        part = one(getattr(m, weight + "_v"), getattr(m, raw + "_v"), into)
        store(into, target)
        return part

    by_g = whole("wg", "grad_g", m.into_g, m.to_g)
    for name, target in (("grad_x", m.to_x), ("grad_d", m.to_d), ("out", m.to_out), ("grad_o", m.to_o)):
        loads[name].wait()
        store(getattr(m, name + "_v"), target)
    by_u = whole("wu", "grad_u", m.into_u, m.to_u)
    by_q = whole("wq", "grad_q", m.into_q, m.to_q)
    by_k = one(m.wk, m.grad_kv.at[0], m.to_k)
    by_v = one(m.wv, m.grad_kv.at[1], m.to_v)
    m.to_gain_one[...] = to_row(by_q + by_k + by_v) / m.gain_one[...].astype(FULL)
    m.to_gain_two[...] = to_row(by_g + by_u) / m.gain_two[...].astype(FULL)
    for copy in stores:
        copy.wait()


def finish(ins, shape, own_ff):
    rows = ins["wq"].shape[0]
    held = ("gain_one", "gain_two", "wk", "wv", "grad_kv")
    placed = {key: (value, VMEM if key in held else ANY) for key, value in ins.items()}
    outs = dict(
        to_out=(shape_of(ins["out"].shape, ins["out"].dtype), ANY),
        to_x=(shape_of(ins["grad_x"].shape, FULL), ANY),
        to_gain_one=(shape_of((1, rows), FULL), VMEM),
        to_q=(shape_of(ins["wq"].shape, FULL), ANY),
        to_k=(shape_of(ins["wk"].shape, FULL), VMEM),
        to_v=(shape_of(ins["wv"].shape, FULL), VMEM),
        to_o=(shape_of(ins["grad_o"].shape, FULL), ANY),
        to_gain_two=(shape_of((1, rows), FULL), VMEM),
        to_g=(shape_of(ins["wg"].shape, FULL), ANY),
        to_u=(shape_of(ins["wu"].shape, FULL), ANY),
        to_d=(shape_of(ins["grad_d"].shape, FULL), ANY),
    )
    scratch = dict(load=dma(10), store=dma(7))
    for name in ("g", "u", "q"):
        scratch["into_" + name] = vm(FULL, *ins["w" + name].shape)
    for key, value in ins.items():
        if key not in held:
            scratch[key + "_v"] = pltpu.VMEM(value.shape, value.dtype)
    done = run(finish_kernel, "finish", None, placed, outs, scratch)
    done = list(done.values())
    for k in (0, 1):
        done[k] = done[k].reshape(shape)
    for k in (2, 7):
        done[k] = done[k].reshape(rows)
    done[10] = done[10][:own_ff]
    return tuple(done)


def solution(mesh):
    rows = P(("dp", "seq"), None)
    vector = P(("dp", "seq"))
    row = P("dp", "seq", None)
    return jax.shard_map(
        functools.partial(body, mesh.shape["dp"], mesh.shape["seq"]),
        mesh=mesh,
        in_specs=(row, P("dp", "seq"), vector, rows, rows, rows, rows, vector, rows, rows, rows, row),
        out_specs=(row, row, vector, rows, rows, rows, rows, vector, rows, rows, rows),
        check_vma=False,
    )
```

```python
import functools
import math

import jax
import jax.numpy as jnp
from jax import lax
from jax.experimental import pallas as pl
from jax.experimental.pallas import tpu as pltpu
from jax.sharding import PartitionSpec as P

HEADS = 32
HEAD_DIM = 64
KV_HEADS = 4
GROUP = HEADS // KV_HEADS

EPS = 1e-05
ROPE_BASE = 10000.0
MASK_VALUE = -1e30
MESH = pl.DeviceIdType.MESH
LOW = jnp.bfloat16
FULL = jnp.float32
VMEM_BYTES = 61 * 1024 * 1024


def matmul(left, right):
    return jnp.dot(left, right, preferred_element_type=FULL)


def matmul_nt(left, right):
    return lax.dot_general(left, right, (((1,), (1,)), ((), ())), preferred_element_type=FULL)


def matmul_tn(left, right):
    return lax.dot_general(left, right, (((0,), (0,)), ((), ())), preferred_element_type=FULL)


def ring_at(place, n):
    upper = lax.div(place, n // 2)
    return (1 - upper) * 2 * place + upper * (2 * (n - place) - 1)


def ring_place(index, n):
    odd = lax.rem(index, 2)
    return (1 - odd) * lax.div(index, 2) + odd * (n - lax.div(index + 1, 2))


class Where:
    def __init__(self, n_dp, n_seq):
        self.n_dp, self.n_seq = n_dp, n_seq
        self.chips = n_dp // 2
        self.dp = lax.axis_index("dp")
        self.seq = lax.axis_index("seq")
        self.core = lax.rem(self.dp, 2)
        self.chip = lax.div(self.dp, 2)
        self.place = ring_place(self.seq, n_seq)

    def ring(self, step):
        return ring_at(lax.rem(self.place + step + self.n_seq, self.n_seq), self.n_seq)

    def ring_ids(self):
        return [(self.dp, self.ring(1)), (self.dp, self.ring(-1))]

    def seq_ids(self):
        return [
            (self.dp, lax.rem(self.seq + k, self.n_seq)) for k in range(1, self.n_seq)
        ]

    def dp_ids(self):
        return [(lax.rem(self.dp + k, self.n_dp), self.seq) for k in range(1, self.n_dp)]

    def core_id(self):
        return (self.dp + 1 - 2 * self.core, self.seq)

    def chip_ids(self):
        return [
            (2 * lax.rem(self.chip + k, self.chips) + self.core, self.seq)
            for k in range(1, self.chips)
        ]


def greet(ids):
    barrier = pltpu.get_barrier_semaphore()
    for one in ids:
        pl.semaphore_signal(barrier, inc=1, device_id=one, device_id_type=MESH)
    pl.semaphore_wait(barrier, len(ids))


def remote(src, dst, send, recv, target):
    return pltpu.make_async_remote_copy(
        src_ref=src,
        dst_ref=dst,
        send_sem=send,
        recv_sem=recv,
        device_id=target,
        device_id_type=MESH,
    )


class Ring:
    def __init__(self, at, shape, send, recv):
        self.at, self.send, self.recv = at, send, recv
        self.steps = at.n_seq // 2
        self.halves = 2 if len(shape) > 2 or shape[0] % 32 == 0 else 1
        self.half = shape[0] // self.halves
        self.copies = {}

    @staticmethod
    def semaphores(n_seq):
        shape = (2, n_seq // 2, 2)
        return [pltpu.SemaphoreType.DMA(shape), pltpu.SemaphoreType.DMA(shape)]

    def opposite(self, h, d):
        return d == h if self.halves == 2 else d == 0

    def rows(self, h):
        return pl.ds(h * self.half, self.half)

    def go(self, src, dst, d, t, h):
        target = self.at.ring_ids()[d]
        copy = remote(src, dst, self.send.at[d, t, h], self.recv.at[d, t, h], target)
        copy.start()
        self.copies[(d, t, h)] = copy

    def pieces(self):
        return [(h, d) for h in range(self.halves) for d in (0, 1)]


class RingGather(Ring):
    def __init__(self, at, own, everything, send, recv, local):
        super().__init__(at, own.shape, send, recv)
        self.own, self.everything = own, everything
        self.kept = pltpu.make_async_copy(own, everything.at[at.seq], local)
        self.waited = set()

    @staticmethod
    def scratch(n_seq):
        return Ring.semaphores(n_seq)

    def wait(self, key):
        self.copies[key].wait_recv()
        self.waited.add(key)

    def step(self, t):
        if t == 0:
            self.kept.start()
        if t == 1:
            self.kept.wait()
        for h, d in self.pieces():
            if t == self.steps - 1 and not self.opposite(h, d):
                continue
            if t > 0:
                self.wait((d, t - 1, h))
            origin = self.at.ring(-t if d == 0 else t)
            dst = self.everything.at[origin, self.rows(h)]
            self.go(self.own.at[self.rows(h)] if t == 0 else dst, dst, d, t, h)

    def rest(self, t):
        for key in self.copies:
            if key not in self.waited and key[1] <= t:
                self.wait(key)

    def finish(self):
        self.rest(self.steps)
        for copy in self.copies.values():
            copy.wait_send()
        if self.steps == 1:
            self.kept.wait()


class RingScatter(Ring):
    def __init__(self, at, parts, slots, send, recv, staged=None, loads=None, axis=0):
        shape = parts.shape[1:] if axis == 0 else parts.shape[:1] + parts.shape[2:]
        super().__init__(at, shape, send, recv)
        self.axis = axis
        self.parts, self.slots, self.staged, self.loads = parts, slots, staged, loads

    @staticmethod
    def scratch(n_seq, *block):
        return [pltpu.VMEM((2, n_seq // 2) + block, LOW)] + Ring.semaphores(n_seq)

    @staticmethod
    def staging(*block):
        return [pltpu.VMEM((2,) + block, LOW), pltpu.SemaphoreType.DMA((2, 2))]

    def there(self, t, d):
        return self.at.ring(self.steps - t if d == 0 else t - self.steps)

    def block(self, index, h):
        if self.axis:
            return self.parts.at[self.rows(h), index]
        return self.parts.at[index, self.rows(h)]

    def adds(self, t, h, d):
        return t > 1 or (t == 1 and self.opposite(h, d))

    def load(self, t, h, d):
        rows = self.rows(h)
        return pltpu.make_async_copy(self.block(self.there(t, d), h), self.staged.at[d, rows], self.loads.at[d, h])

    def load_all(self, t):
        if self.staged is not None:
            for h, d in self.pieces():
                if t < self.steps and self.adds(t, h, d):
                    self.load(t, h, d).start()
                elif t == self.steps and d == 0:
                    self.load(t, h, d).start()

    def early(self):
        for h, d in self.pieces():
            if self.steps > 1 and not self.opposite(h, d):
                self.go(self.block(self.there(1, d), h), self.slots.at[d, 1, self.rows(h)], d, 1, h)

    def step(self, t):
        if t == 0:
            self.load_all(1)
        for h, d in self.pieces():
            if (t == 0 and not self.opposite(h, d)) or (d, t, h) in self.copies:
                continue
            rows = self.rows(h)
            src = self.block(self.there(t, d), h)
            if self.adds(t, h, d):
                if self.staged is not None:
                    self.load(t, h, d).wait()
                    src = self.staged.at[d, rows]
                self.copies[(d, t - 1, h)].wait_recv()
                held = self.slots.at[d, t - 1, rows]
                held[...] = (held[...].astype(FULL) + src[...].astype(FULL)).astype(LOW)
                src = held
            self.go(src, self.slots.at[d, t, rows], d, t, h)
        if t > 0:
            self.load_all(t + 1)

    def finish(self, out):
        last = self.steps - 1
        if last == 0:
            self.load_all(1)
        for h in range(self.halves):
            rows = self.rows(h)
            if self.staged is None:
                total = self.block(self.at.seq, h)[...].astype(FULL)
            else:
                self.load(self.steps, h, 0).wait()
                total = self.staged[0, rows].astype(FULL)
            for d in (0, 1):
                if last == 0 and not self.opposite(h, d):
                    continue
                self.copies[(d, last, h)].wait_recv()
                total = total + self.slots[d, last, rows].astype(FULL)
            out[rows] = total.astype(out.dtype)
        for copy in self.copies.values():
            copy.wait_send()


class Exchange:
    def __init__(self, me, ids, axis, packed, landing, send, recv, local):
        self.started = 0
        self.kept = pltpu.make_async_copy(packed.at[me], landing.at[me], local)
        self.copies = [
            remote(packed.at[one[axis]], landing.at[me], send.at[k], recv.at[k], one)
            for k, one in enumerate(ids)
        ]

    @staticmethod
    def scratch(n):
        return [pltpu.SemaphoreType.DMA((n - 1,)), pltpu.SemaphoreType.DMA((n - 1,))]

    def start(self, count=None):
        if not self.started:
            self.kept.start()
        first = self.started - 1 if self.started else 0
        last = len(self.copies) if count is None else min(first + count, len(self.copies))
        for copy in self.copies[first:last]:
            copy.start()
        self.started = last + 1

    def arrived(self):
        self.kept.wait()
        for copy in self.copies:
            copy.wait_recv()

    def finish(self):
        for copy in self.copies:
            copy.wait_send()


def seq_exchange(at, *refs):
    return Exchange(at.seq, at.seq_ids(), 1, *refs)


def dp_exchange(at, *refs):
    return Exchange(at.dp, at.dp_ids(), 0, *refs)


class DpGather:
    def __init__(self, at, own, everything, send, recv, local):
        self.kept = pltpu.make_async_copy(own, everything.at[at.dp], local)
        slot = everything.at[at.dp]
        self.out = [
            remote(own, slot, send.at[k], recv.at[k], one) for k, one in enumerate(at.chip_ids())
        ]
        base = at.chips - 1
        self.mate = remote(own, slot, send.at[base], recv.at[base], at.core_id())
        self.handed = []
        for k in range(1, at.chips):
            origin = 2 * lax.rem(at.chip + at.chips - k, at.chips) + at.core
            there = everything.at[origin]
            self.handed.append(
                remote(there, there, send.at[base + k], recv.at[base + k], at.core_id())
            )

    @staticmethod
    def scratch(n_dp):
        return [pltpu.SemaphoreType.DMA((n_dp - 1,)), pltpu.SemaphoreType.DMA((n_dp - 1,))]

    def start(self):
        for copy in self.out:
            copy.start()
        self.mate.start()
        self.kept.start()

    def hand(self):
        for copy, onward in zip(self.out, self.handed):
            copy.wait_recv()
            onward.start()

    def arrived(self):
        self.kept.wait()
        self.mate.wait_recv()
        for copy in self.handed:
            copy.wait_recv()

    def finish(self):
        for copy in self.out + [self.mate] + self.handed:
            copy.wait_send()


def add_rows(rows, chunk, one):
    def step(r, carry):
        one(pl.ds(pl.multiple_of(r * chunk, chunk), chunk))
        return carry

    lax.fori_loop(0, rows // chunk, step, 0)


def chunk_of(rows, columns):
    chunk = rows
    while chunk % 32 == 0 and chunk * columns > 65536:
        chunk //= 2
    return chunk


class DpScatter:
    def __init__(self, at, parts, core, other, send, recv):
        self.at, self.parts, self.core, self.other = at, parts, core, other
        self.send, self.recv = send, recv
        self.rows, self.columns = parts.shape[1], parts.shape[2]

    @staticmethod
    def scratch(n_dp, rows, columns):
        chips = n_dp // 2
        return [
            pltpu.VMEM((chips, rows, columns), LOW),
            pltpu.VMEM((max(chips - 1, 1), rows, columns), LOW),
            pltpu.SemaphoreType.DMA((2 * chips - 1,)),
            pltpu.SemaphoreType.DMA((2 * chips - 1,)),
        ]

    def to_core(self, k):
        at = self.at
        return remote(
            self.parts.at[2 * k + 1 - at.core],
            self.core.at[k],
            self.send.at[k],
            self.recv.at[k],
            at.core_id(),
        )

    def to_chip(self, k):
        at = self.at
        sem = at.chips + k - 1
        return remote(
            self.core.at[lax.rem(at.chip + k, at.chips)],
            self.other.at[k - 1],
            self.send.at[sem],
            self.recv.at[sem],
            at.chip_ids()[k - 1],
        )

    def start(self):
        for k in range(self.at.chips):
            self.to_core(k).start()

    def add_core(self, k):
        held = self.core.at[k]
        mine = self.parts.at[2 * k + self.at.core]

        def one(rows):
            held[rows] = (held[rows].astype(FULL) + mine[rows].astype(FULL)).astype(LOW)

        add_rows(self.rows, chunk_of(self.rows, self.columns), one)

    def across(self):
        at = self.at
        for k in range(1, at.chips):
            there = lax.rem(at.chip + k, at.chips)
            self.to_core(there).wait_recv()
            self.add_core(there)
            self.to_chip(k).start()

    def finish(self, out):
        at = self.at
        self.to_core(at.chip).wait_recv()
        for k in range(1, at.chips):
            self.to_chip(k).wait_recv()
        held = self.core.at[at.chip]
        mine = self.parts.at[2 * at.chip + at.core]

        def one(rows):
            total = held[rows].astype(FULL) + mine[rows].astype(FULL)
            for k in range(1, at.chips):
                total = total + self.other[k - 1, rows].astype(FULL)
            out[rows] = total.astype(out.dtype)

        add_rows(self.rows, chunk_of(self.rows, self.columns), one)
        for k in range(at.chips):
            self.to_core(k).wait_send()
        for k in range(1, at.chips):
            self.to_chip(k).wait_send()


def comm_params(number):
    if number is None:
        return pltpu.CompilerParams(vmem_limit_bytes=VMEM_BYTES)
    return pltpu.CompilerParams(
        collective_id=number, has_side_effects=True, vmem_limit_bytes=VMEM_BYTES
    )


ANY = pl.BlockSpec(memory_space=pl.ANY)
VMEM = pl.BlockSpec(memory_space=pltpu.VMEM)


def shape_of(dims, kind):
    return jax.ShapeDtypeStruct(dims, kind)


class Refs:
    def __init__(self, names, refs):
        refs = list(refs)
        for name, count in names:
            taken, refs = refs[: max(count, 1)], refs[max(count, 1) :]
            setattr(self, name, taken if count else taken[0])


def run(kernel, name, number, ins, outs, scratch):
    names = [(key, 0) for key in ins] + [(key, 0) for key in outs]
    shapes = []
    for key, value in scratch.items():
        if isinstance(value, list):
            names.append((key, len(value)))
            shapes += value
        else:
            names.append((key, 0))
            shapes.append(value)
    found = pl.pallas_call(
        lambda *refs: kernel(Refs(names, refs)),
        name=name,
        out_shape=[shape for shape, _ in outs.values()],
        in_specs=[spec for _, spec in ins.values()],
        out_specs=[spec for _, spec in outs.values()],
        scratch_shapes=shapes,
        compiler_params=comm_params(number),
    )(*[array for array, _ in ins.values()])
    return dict(zip(outs, found))


def dma(*dims):
    return pltpu.SemaphoreType.DMA(dims)


def vm(kind, *dims):
    return pltpu.VMEM(dims, kind)


def lanes(rows):
    return lax.broadcasted_iota(jnp.int32, (rows, 2 * HEAD_DIM), 1)


def low_head(rows):
    return lanes(rows) < HEAD_DIM


def swapped(pair):
    half = HEAD_DIM // 2
    first = lax.rem(lanes(pair.shape[0]), HEAD_DIM) < half
    return jnp.where(
        first, pltpu.roll(pair, 2 * HEAD_DIM - half, 1), pltpu.roll(pair, half, 1)
    )


def split_heads(pair):
    wide = pair.astype(FULL)
    low = low_head(pair.shape[0])
    return jnp.concatenate(
        [jnp.where(low, wide, 0.0), jnp.where(low, 0.0, wide)], 0
    ).astype(LOW)


def join_heads(both):
    rows = both.shape[0] // 2
    return jnp.where(low_head(rows), both[:rows], both[rows:])


def spread_kv(kv):
    wide = kv.astype(FULL)
    turned = pltpu.roll(wide, HEAD_DIM, 1)
    low = low_head(kv.shape[0])
    return jnp.where(low, wide, turned).astype(LOW), jnp.where(low, turned, wide).astype(LOW)


def mask_of(position, start, length):
    key = lax.broadcasted_iota(jnp.int32, (start.shape[0], length), 1)
    return jnp.where((key <= position) & (key >= start), 0.0, MASK_VALUE)


def own_positions(at, tok):
    return at.seq * tok + lax.broadcasted_iota(jnp.int32, (tok, 1), 0)


def rows_of(r, count):
    return pl.ds(pl.multiple_of(r * count, count), count)


def to_column(row):
    n = row.shape[1]
    here = lax.broadcasted_iota(jnp.int32, (n, n), 0) == lax.broadcasted_iota(jnp.int32, (n, n), 1)
    return jnp.sum(jnp.where(here, row.astype(FULL), 0.0), 1, keepdims=True)


def to_row(column):
    n = column.shape[0]
    here = lax.broadcasted_iota(jnp.int32, (n, n), 0) == lax.broadcasted_iota(jnp.int32, (n, n), 1)
    return jnp.sum(jnp.where(here, column, 0.0), 0, keepdims=True)


def front_kernel(n_dp, n_seq, own_ff, ff, kv_of, m):
    at = Where(n_dp, n_seq)
    tok, width = m.x.shape
    q_width = m.q.shape[1]
    groups = q_width // (2 * HEAD_DIM)
    rank = n_seq * m.pq.shape[1]
    length = n_seq * tok
    greet(at.seq_ids() + at.dp_ids())
    swap_q = dp_exchange(at, m.pq, m.landed, *m.swap_q_sem, m.local.at[0])
    x_g = DpGather(at, m.x, m.xs, *m.x_sem, m.local.at[1])
    row_x = seq_exchange(at, m.seg_rows, m.seg_row, *m.row_x_sem, m.local.at[2])
    row_g = DpGather(at, m.seg_row, m.segs, *m.row_g_sem, m.local.at[3])
    col_g = DpGather(at, m.seg_col, m.seg_cols, *m.col_g_sem, m.local.at[4])
    ring_q = RingGather(at, m.landed, m.wq_all, *m.ring_q_sem, m.local.at[5])
    ring_o = RingGather(at, m.wo, m.wo_all, *m.ring_o_sem, m.local.at[6])
    ring_kv = RingGather(at, m.kv_own, m.kv_all, *m.ring_kv_sem, m.local.at[7])
    swap_gu = seq_exchange(at, m.pgu, m.gu, *m.swap_gu_sem, m.local.at[8])
    down = DpGather(at, m.wd, m.wd_all, *m.down_sem, m.local.at[9])
    loads = [
        pltpu.make_async_copy(src, dst, m.load.at[k])
        for k, (src, dst) in enumerate(((m.wg_in, m.wg), (m.wu_in, m.wu), (m.x, m.x_own)))
    ]
    stores = []

    def store(src, dst):
        copy = pltpu.make_async_copy(src, dst, m.local.at[10 + len(stores)])
        copy.start()
        stores.append(copy)

    ring_o.step(0)
    for copy in loads:
        copy.start()

    for i, kv in enumerate(kv_of):
        m.pq[i, :, :q_width] = m.wq[:, i * q_width : (i + 1) * q_width]
        for weight, first in ((m.wk, q_width), (m.wv, q_width + HEAD_DIM)):
            m.pq[i, :, first : first + HEAD_DIM] = weight[:, kv * HEAD_DIM : (kv + 1) * HEAD_DIM]
    swap_q.start()
    x_g.start()
    ids = m.ids[...]
    rank_own = m.pq.shape[1]
    m.seg_rows[...] = jnp.broadcast_to(ids.astype(FULL)[None], m.seg_rows.shape)
    for k, own_gain in ((1, m.gain_one), (2, m.gain_two)):
        m.seg_rows[:, k : k + 1, :rank_own] = jnp.broadcast_to(
            own_gain[...].astype(FULL)[None], (n_seq, 1, rank_own)
        )
    m.seg_col[...] = jnp.broadcast_to(to_column(ids), m.seg_col.shape)
    row_x.start()
    col_g.start()

    def pack(k, weight, first):
        loads[k].wait()
        if ff > own_ff:
            m.pgu[:, :, first : first + n_dp * ff] = jnp.zeros(
                m.pgu.shape[:2] + (n_dp * ff,), LOW
            )
        for s in range(n_seq):
            for i in range(n_dp):
                piece = weight[:, (i * n_seq + s) * own_ff : (i * n_seq + s + 1) * own_ff]
                m.pgu[s, :, first + i * ff : first + i * ff + own_ff] = piece

    later = list(range(1, ring_o.steps))
    ring_o.step(later.pop(0))
    swap_q.arrived()
    ring_q.step(0)
    row_x.arrived()
    row_g.start()

    def hand():
        x_g.hand()
        row_g.hand()
        col_g.hand()
        down.start()

    def norm():
        x_g.arrived()
        row_g.arrived()
        m.gains[...] = jnp.zeros_like(m.gains)
        for k in (0, 1):
            for i in range(n_dp):
                for s in range(n_seq):
                    first = (i * n_seq + s) * rank_own
                    m.gains[k : k + 1, first : first + rank_own] = m.segs[
                        i, s, k + 1 : k + 2, :rank_own
                    ]
        store(m.gains, m.gains_out)
        for r in range(n_dp):
            x = m.xs[r].astype(FULL)
            scale = lax.rsqrt(jnp.mean(x * x, -1, keepdims=True) + EPS)
            m.n1[r] = (x * scale * m.gains[:1]).astype(LOW)
        store(m.n1, m.n1_out)

    def place():
        col_g.arrived()
        position = own_positions(at, tok)
        first = lax.rem(lanes(tok), HEAD_DIM) < HEAD_DIM // 2
        number = lax.rem(lanes(tok), HEAD_DIM // 2).astype(FULL)
        freqs = jnp.exp(number * (-2.0 * math.log(ROPE_BASE) / HEAD_DIM))
        for r in range(n_dp):
            segs = jnp.concatenate([m.segs[r, s, :1] for s in range(n_seq)], 1)
            own = m.seg_cols[r][:, :1]
            start = jnp.sum((segs < own).astype(jnp.int32), 1, keepdims=True)
            turned = (position - start).astype(FULL) * freqs
            rows = slice(r * tok, (r + 1) * tok)
            m.cos[rows] = jnp.cos(turned)
            sines = jnp.sin(turned)
            m.sin[rows] = jnp.where(first, -sines, sines)
            m.starts[rows] = jnp.broadcast_to(start, (tok, 2 * HEAD_DIM))
        store(m.cos, m.cos_out)
        store(m.sin, m.sin_out)
        store(m.starts, m.starts_out)

    pack(0, m.wg, 0)
    ring_q.step(1)
    jobs = [lambda: (hand(), norm(), place()), lambda: pack(1, m.wu, n_dp * ff)]
    for t in range(2, ring_q.steps):
        ring_q.step(t)
        if jobs:
            jobs.pop(0)()
    for job in jobs:
        job()
    ring_q.finish()
    if later:
        ring_o.step(later.pop(0))
    store(m.wq_all, m.wq_out)

    m.qkv[...] = sum(
        matmul(
            m.n1[:, :, i * rank : (i + 1) * rank].reshape(n_dp * tok, rank),
            m.wq_all[:, i].reshape(rank, q_width + 2 * HEAD_DIM),
        )
        for i in range(n_dp)
    )
    factor = HEAD_DIM ** (-0.5)
    for g in range(groups + 1):
        cols = slice(g * 2 * HEAD_DIM, (g + 1) * 2 * HEAD_DIM)
        pair = m.qkv[:, cols]
        turned = pair * m.cos[...] + swapped(pair) * m.sin[...]
        if g < groups:
            m.q[:, cols] = (turned * factor).astype(LOW)
        else:
            m.kv_own[...] = jnp.where(low_head(pair.shape[0]), turned, pair).astype(LOW)
    ring_kv.step(0)
    store(m.q, m.q_out)
    for t in range(1, ring_kv.steps):
        ring_kv.step(t)
        if later and t > 1:
            ring_o.step(later.pop(0))
    for t in later:
        ring_o.step(t)
    down.hand()
    ring_kv.finish()
    swap_gu.start(2)
    store(m.kv_all, m.kv_out)
    m.lse[...] = jnp.zeros_like(m.lse)
    for r in range(n_dp):
        rows = slice(r * tok, (r + 1) * tok)
        k, v = spread_kv(m.kv_all[:, rows].reshape(length, 2 * HEAD_DIM))
        m.k2[...] = k
        m.v2[...] = v
        m.mask[...] = mask_of(own_positions(at, tok), m.starts[rows, :1], length)

        def group(g, carry):
            cols = rows_of(g, 2 * HEAD_DIM)
            raw = matmul_nt(split_heads(m.q[rows, cols]), m.k2[...])
            raw = raw + jnp.concatenate([m.mask[...]] * 2, 0)
            top = jnp.max(raw, -1, keepdims=True)
            probs = jnp.exp(raw - top)
            total = jnp.sum(probs, -1, keepdims=True)
            probs = (probs * (1.0 / total)).astype(LOW)
            m.o[rows, cols] = join_heads(matmul(probs, m.v2[...])).astype(LOW)
            here = lanes(2 * tok) == r * groups + g
            m.lse[...] = jnp.where(here, top + jnp.log(total), m.lse[...])
            return carry

        lax.fori_loop(0, groups, group, 0)
        if r == 0:
            swap_gu.start()
    store(m.o, m.o_out)
    store(m.lse, m.lse_out)
    ring_o.finish()
    store(m.wo_all, m.wo_out)
    full = m.wo_all[...].reshape(q_width, width)
    for r in range(n_dp):
        m.parts[r] = matmul(m.o[r * tok : (r + 1) * tok], full).astype(LOW)
    back = DpScatter(at, m.parts, *m.back)
    back.start()
    back.across()
    back.finish(m.middle)
    loads[2].wait()
    middle = m.x_own[...].astype(FULL) + m.middle[...]
    m.middle[...] = middle
    scale = lax.rsqrt(jnp.mean(middle * middle, -1, keepdims=True) + EPS)
    m.second[...] = (middle * scale * m.gains[1:2]).astype(LOW)
    swap_gu.arrived()
    down.arrived()
    for one in (swap_q, x_g, row_x, row_g, col_g, swap_gu, down):
        one.finish()
    for copy in stores:
        copy.wait()


def front(n_dp, n_seq, own_ff, kv_of, held, small):
    tok, width = held["x"].shape
    rank = small["wq"].shape[0]
    q_width = width // n_dp
    groups = q_width // (2 * HEAD_DIM)
    pair = 2 * HEAD_DIM
    columns = q_width + pair
    length = n_seq * tok
    every = n_dp * tok
    wd = held["wd"]
    ff = wd.shape[0]
    gu_width = 2 * n_dp * ff
    ins = {key: (value, ANY) for key, value in held.items()}
    ins |= {key: (value, VMEM) for key, value in small.items()}
    kept = dict(
        n1=(LOW, n_dp, tok, width),
        q=(LOW, every, q_width),
        kv_all=(LOW, n_seq, every, pair),
        o=(LOW, every, q_width),
        lse=(FULL, 2 * tok, pair),
        cos=(FULL, every, pair),
        sin=(FULL, every, pair),
        starts=(jnp.int32, every, pair),
        gains=(FULL, 8, width),
        wq_all=(LOW, n_seq, n_dp, rank, columns),
        wo_all=(LOW, n_seq, rank, width),
    )
    outs = {
        key.replace("_all", "") + "_out": (shape_of(dims[1:], dims[0]), ANY)
        for key, dims in kept.items()
    }
    outs["gu"] = (shape_of((n_seq, rank, gu_width), LOW), ANY)
    outs["wd_all"] = (shape_of((n_dp,) + wd.shape, LOW), ANY)
    outs["middle"] = (shape_of((tok, width), FULL), VMEM)
    outs["second"] = (shape_of((tok, width), LOW), VMEM)
    scratch = {key: vm(*dims) for key, dims in kept.items()}
    scratch |= dict(
        load=dma(3),
        wg=vm(LOW, *held["wg_in"].shape),
        wu=vm(LOW, *held["wg_in"].shape),
        x_own=vm(LOW, tok, width),
        pq=vm(LOW, n_dp, rank, columns),
        seg_rows=vm(FULL, n_seq, 8, tok),
        seg_col=vm(FULL, tok, pair),
        landed=vm(LOW, n_dp, rank, columns),
        xs=vm(LOW, n_dp, tok, width),
        seg_row=vm(FULL, n_seq, 8, tok),
        segs=vm(FULL, n_dp, n_seq, 8, tok),
        seg_cols=vm(FULL, n_dp, tok, pair),
        kv_own=vm(LOW, every, pair),
        mask=vm(FULL, tok, length),
        pgu=vm(LOW, n_seq, rank, gu_width),
        qkv=vm(FULL, every, columns),
        k2=vm(LOW, length, pair),
        v2=vm(LOW, length, pair),
        parts=vm(LOW, n_dp, tok, width),
        back=DpScatter.scratch(n_dp, tok, width),
        local=dma(10 + len(kept)),
        swap_q_sem=Exchange.scratch(n_dp),
        x_sem=DpGather.scratch(n_dp),
        row_x_sem=Exchange.scratch(n_seq),
        row_g_sem=DpGather.scratch(n_dp),
        col_g_sem=DpGather.scratch(n_dp),
        ring_q_sem=Ring.semaphores(n_seq),
        ring_o_sem=Ring.semaphores(n_seq),
        ring_kv_sem=Ring.semaphores(n_seq),
        swap_gu_sem=Exchange.scratch(n_seq),
        down_sem=DpGather.scratch(n_dp),
    )
    return run(
        functools.partial(front_kernel, n_dp, n_seq, own_ff, ff, kv_of), "attention_forward", 1, ins, outs, scratch
    )


def feed_kernel(n_dp, n_seq, m):
    at = Where(n_dp, n_seq)
    tok, width = m.second.shape
    wide = m.wgu.shape[2]
    part = wide // 2
    rank = width // n_dp
    length = n_seq * tok
    greet(at.ring_ids() + at.dp_ids())
    gu = DpGather(at, m.gu, m.wgu, *m.gu_sem, m.local.at[0])
    ring_n = RingGather(at, m.second, m.second_all, *m.ring_n, m.local.at[1])
    ring_dy = RingGather(at, m.dy, m.dy_all, *m.ring_dy, m.local.at[2])
    ring_h = RingScatter(at, m.part, *m.ring_h)
    side = DpScatter(at, m.wgu, *m.side)
    gu.start()
    held = pltpu.make_async_copy(m.wd_all, m.wd, m.local.at[3])
    held.start()
    ring_n.step(0)
    for t in range(1, ring_n.steps):
        ring_n.step(t)
    ring_dy.step(0)
    gu.hand()
    ring_n.finish()
    gu.arrived()
    held.wait()
    stores = []

    def store(src, dst, k):
        copy = pltpu.make_async_copy(src, dst, m.local.at[k])
        copy.start()
        stores.append(copy)

    def stored():
        while stores:
            stores.pop().wait()

    def forward(c):
        blocks = slice(2 * c, 2 * c + 2)
        normed = m.second_all[blocks].reshape(2 * tok, width)
        both = matmul(normed, m.wgu[...].reshape(width, wide))
        gate, upward = both[:, :part], both[:, part:]
        sigma = jax.nn.sigmoid(gate)
        silu = gate * sigma
        hidden = (silu * upward).astype(LOW)
        m.by_up[blocks] = silu.reshape(2, tok, part)
        m.by_gate[blocks] = (upward * sigma * (1.0 + gate * (1.0 - sigma))).reshape(2, tok, part)
        m.hidden[blocks] = hidden.reshape(2, tok, part)
        out = matmul(hidden, m.wd[...].reshape(part, width))
        m.part[blocks] = out.astype(LOW).reshape(2, tok, width)
        copy = pltpu.make_async_copy(m.part.at[blocks], m.part_y.at[blocks], m.store.at[c])
        copy.start()
        stores.append(copy)

    def backward(blocks):
        rows = len(blocks) * tok
        dy = jnp.concatenate([m.dy_all[b] for b in blocks], 0)
        grad = matmul_nt(dy, m.wd[...].reshape(part, width))
        for k, b in enumerate(blocks):
            one = grad[k * tok : (k + 1) * tok]
            m.grads[b, :, :part] = (one * m.by_gate[b]).astype(LOW)
            m.grads[b, :, part:] = (one * m.by_up[b]).astype(LOW)
        both = jnp.concatenate([m.grads[b] for b in blocks], 0)
        for i in range(n_dp):
            cols = slice(i * rank, (i + 1) * rank)
            out = matmul_nt(both, m.wgu[i]).astype(LOW)
            for k, b in enumerate(blocks):
                m.part[b, :, cols] = out[k * tok : (k + 1) * tok]

    jobs = [functools.partial(forward, c) for c in range(n_seq // 2)]
    jobs.append(stored)
    jobs.append(lambda: backward([at.seq]))
    for t in range(1, ring_dy.steps):
        for _ in range(3 if t == 1 else 4):
            if jobs:
                jobs.pop(0)()
        ring_dy.step(t)
        if t < ring_dy.steps - 1:
            jobs.append(functools.partial(backward, [at.ring(-t), at.ring(t)]))
    for job in jobs:
        job()
    if ring_dy.steps > 1:
        ring_dy.rest(ring_dy.steps - 2)
        backward([at.ring(1 - ring_dy.steps), at.ring(ring_dy.steps - 1)])
    ring_h.early()
    ring_dy.finish()
    backward([at.ring(ring_dy.steps)])
    gu.finish()

    ring_h.step(0)

    def grad_gu(k):
        chip = lax.rem(at.chip + 1 + k, at.chips)
        for c in (1 - at.core, at.core):
            normed = m.second_all[:, :, rows_of(2 * chip + c, rank)].reshape(length, rank)
            m.wgu[2 * chip + c] = matmul_tn(normed, m.grads[...].reshape(length, wide)).astype(LOW)
            if c is not at.core:
                side.to_core(chip).start()

    def grad_down():
        step = width // n_dp
        for i in range(n_dp):
            cols = slice(i * step, (i + 1) * step)
            dy = m.dy_all[:, :, cols].reshape(length, step)
            m.wd[:, :, cols] = (
                matmul_tn(m.hidden[...].reshape(length, part), dy)
                .astype(LOW)
                .reshape(m.wd.shape[:2] + (step,))
            )
        store(m.wd, m.grad_d, 3)

    jobs = [functools.partial(grad_gu, k) for k in range(at.chips)]
    jobs += [side.across, grad_down]
    for t in range(1, ring_h.steps):
        for _ in range(2):
            if jobs:
                jobs.pop(0)()
        ring_h.step(t)
    for job in jobs:
        job()
    ring_h.finish(m.grad_h)
    store(m.grad_h, m.grad_h_to, 4)
    side.finish(m.fin)
    store(m.fin, m.fin_to, 5)
    stored()


def feed(n_dp, n_seq, second, dy, gu, wd):
    tok, width = second.shape
    deep, wide = gu.shape
    ff = wd.shape[1]
    part = wide // 2
    ins = dict(second=(second, ANY), dy=(dy, ANY), gu=(gu, ANY), wd_all=(wd, ANY))
    outs = dict(
        part_y=(shape_of((n_seq, tok, width), LOW), ANY),
        grad_h_to=(shape_of((tok, width), FULL), ANY),
        fin_to=(shape_of((deep, wide), LOW), ANY),
        grad_d=(shape_of(wd.shape, LOW), ANY),
    )
    scratch = dict(
        local=dma(6),
        grad_h=vm(FULL, tok, width),
        fin=vm(LOW, deep, wide),
        wd=vm(LOW, *wd.shape),
        store=dma(n_seq // 2),
        second_all=vm(LOW, n_seq, tok, width),
        dy_all=vm(LOW, n_seq, tok, width),
        wgu=vm(LOW, n_dp, deep, wide),
        by_gate=vm(FULL, n_seq, tok, part),
        by_up=vm(FULL, n_seq, tok, part),
        hidden=vm(LOW, n_seq, tok, part),
        grads=vm(LOW, n_seq, tok, wide),
        part=vm(LOW, n_seq, tok, width),
        gu_sem=DpGather.scratch(n_dp),
        ring_n=Ring.semaphores(n_seq),
        ring_dy=Ring.semaphores(n_seq),
        ring_h=RingScatter.scratch(n_seq, tok, width),
        side=DpScatter.scratch(n_dp, deep, wide),
    )
    return run(functools.partial(feed_kernel, n_dp, n_seq), "feed_forward", 2, ins, outs, scratch)


def back_kernel(n_dp, n_seq, own_ff, ff, kv_of, m):
    at = Where(n_dp, n_seq)
    tok, width = m.x.shape
    q_width = m.q.shape[1]
    groups = q_width // (2 * HEAD_DIM)
    rank = n_seq * m.wq.shape[2]
    length = n_seq * tok
    pair = 2 * HEAD_DIM
    greet(at.seq_ids() + at.dp_ids())
    swap_gu = [
        remote(m.fin.at[one[1]], m.got_gu.at[at.seq], m.swap_gu[0].at[k], m.swap_gu[1].at[k], one)
        for k, one in enumerate(at.seq_ids())
    ]
    ring_y = RingScatter(at, m.part_y, *m.ring_y, *m.staged)
    d_g = DpGather(at, m.d_own, m.d_all, *m.d_sem, m.local.at[0])
    ring_kv = RingScatter(at, m.part_kv, *m.ring_kv)
    ring_q = RingScatter(at, m.landed_q, *m.ring_q, axis=1)
    ring_o = RingScatter(at, m.part_o, *m.ring_o)
    down = DpScatter(at, m.part_d, *m.down)
    back = DpScatter(at, m.d_all, *m.back)
    swap_q = [
        remote(m.part_q.at[one[0]], m.landed_q.at[at.dp], m.swap_q[0].at[k], m.swap_q[1].at[k], one)
        for k, one in enumerate(at.dp_ids())
    ]
    ring_y.step(0)
    stores = []

    def store(key):
        copy = pltpu.make_async_copy(getattr(m, key), getattr(m, key + "_to"), m.store.at[len(stores)])
        copy.start()
        stores.append(copy)

    waiting = list(swap_gu)

    def pace(count=1):
        for copy in waiting[:count]:
            copy.start()
        del waiting[:count]

    loads = [
        pltpu.make_async_copy(getattr(m, key + "_in"), getattr(m, key), m.load.at[2 + k])
        for k, key in enumerate(LOADED)
    ]
    for copy in loads:
        copy.start()

    def load_kv(r):
        block = m.kv.at[:, pl.ds(r * tok, tok)]
        return pltpu.make_async_copy(block, m.kv_row.at[r % 2], m.load.at[r % 2])

    load_kv(0).start()
    own_gu = pltpu.make_async_copy(m.fin.at[at.seq], m.got_gu.at[at.seq], m.local.at[3])
    own_gu.start()

    def norm_back(grad, gain, value):
        grad = grad * gain
        scale = lax.rsqrt(jnp.mean(value * value, -1, keepdims=True) + EPS)
        normed = value * scale
        return scale * (grad - normed * jnp.mean(grad * normed, -1, keepdims=True))

    for copy in loads[:4]:
        copy.wait()
    m.dmid[...] = m.dy[...].astype(FULL) + norm_back(
        m.grad_h[...], m.gains[1:2], m.middle[...]
    )
    m.d_own[...] = m.dmid[...].astype(LOW)
    d_g.start()
    if ring_y.steps > 1:
        ring_y.step(1)
    d_g.hand()
    for copy in loads[4:]:
        copy.wait()
    d_g.arrived()
    down.start()
    m.do[...] = matmul_nt(
        m.d_all[...].reshape(n_dp * tok, width), m.wo[...].reshape(q_width, width)
    ).astype(LOW)
    later = list(range(2, ring_y.steps))
    down.across()
    if later:
        ring_y.step(later.pop(0))
    for r in range(n_dp):
        rows = slice(r * tok, (r + 1) * tok)
        load_kv(r).wait()
        if r + 1 < n_dp:
            load_kv(r + 1).start()
        k, v = spread_kv(m.kv_row[r % 2].reshape(length, pair))
        m.k2[...] = k
        m.v2[...] = v
        m.mask[...] = mask_of(own_positions(at, tok), m.starts[rows, :1], length)
        m.dk2[...] = jnp.zeros_like(m.dk2)
        m.dv2[...] = jnp.zeros_like(m.dv2)

        def group(g, carry):
            cols = rows_of(g, pair)
            q2 = split_heads(m.q[rows, cols])
            do2 = split_heads(m.do[rows, cols])
            raw = matmul_nt(q2, m.k2[...])
            raw = raw + jnp.concatenate([m.mask[...]] * 2, 0)
            here = lanes(2 * tok) == r * groups + g
            lse = jnp.sum(jnp.where(here, m.lse[...], 0.0), 1, keepdims=True)
            probs = jnp.exp(raw - lse)
            grad_probs = matmul_nt(do2, m.v2[...])
            delta = jnp.sum(probs * grad_probs, -1, keepdims=True)
            grad_raw = (probs * (grad_probs - delta)).astype(LOW)
            m.dq[rows, cols] = join_heads(matmul(grad_raw, m.k2[...]))
            m.dk2[...] += matmul_tn(grad_raw, q2)
            m.dv2[...] += matmul_tn(probs.astype(LOW), do2)
            return carry

        lax.fori_loop(0, groups, group, 0)
        dk = m.dk2[...]
        dv = m.dv2[...]
        dkv = jnp.where(
            low_head(length), dk + pltpu.roll(dk, HEAD_DIM, 1), dv + pltpu.roll(dv, HEAD_DIM, 1)
        )
        m.part_kv[:, rows] = dkv.astype(LOW).reshape(n_seq, tok, pair)
        if later and r % 2:
            ring_y.step(later.pop(0))
    for t in later:
        ring_y.step(t)
    ring_kv.step(0)
    m.part_o[...] = (
        matmul_tn(m.o[...], m.d_all[...].reshape(n_dp * tok, width))
        .astype(LOW)
        .reshape(m.part_o.shape)
    )
    d_g.finish()
    for t in range(1, ring_kv.steps):
        ring_kv.step(t)
        pace()
    ring_kv.finish(m.dkv)
    ring_o.step(0)
    factor = HEAD_DIM ** (-0.5)
    for g in range(groups + 1):
        cols = slice(g * pair, (g + 1) * pair)
        grad = m.dq[:, cols] * factor if g < groups else m.dkv[...]
        turned = grad * m.cos[...] - swapped(grad) * m.sin[...]
        if g == groups:
            turned = jnp.where(low_head(grad.shape[0]), turned, grad)
        m.dqkv[:, cols] = turned.astype(LOW)
    ring_y.finish(m.wide)
    n1 = m.ring_y[0].at[0, pl.ds(0, n_dp)]
    fetch = pltpu.make_async_copy(m.n1, n1, m.local.at[2])
    fetch.start()
    m.out[...] = (m.middle[...] + m.wide[...]).astype(m.out.dtype)
    store("out")
    pace()
    fetch.wait()
    for i in range(n_dp):
        cols = slice(i * rank, (i + 1) * rank)
        m.part_q[i] = (
            matmul_tn(n1[:, :, cols].reshape(n_dp * tok, rank), m.dqkv[...])
            .astype(LOW)
            .reshape(n_seq, rank // n_seq, q_width + pair)
        )
    for copy in swap_q:
        copy.start()
    m.landed_q[at.dp] = m.part_q[at.dp]
    pace()
    if ring_o.steps > 1:
        ring_o.step(1)
    pace()
    for i in range(n_dp):
        cols = slice(i * rank, (i + 1) * rank)
        weight = m.wq[:, i].reshape(rank, q_width + pair)
        m.d_all[:, :, cols] = (
            matmul_nt(m.dqkv[...], weight).astype(LOW).reshape(n_dp, tok, rank)
        )
    back.start()
    pace()
    pace(len(waiting))

    def unpack(grad, first):
        for s in range(n_seq):
            for i in range(n_dp):
                grad[:, (i * n_seq + s) * own_ff : (i * n_seq + s + 1) * own_ff] = m.got_gu[
                    s, :, first + i * ff : first + i * ff + own_ff
                ]

    def unpack_gate():
        for copy in swap_gu:
            copy.wait()
        own_gu.wait()
        unpack(m.grad_g, 0)
        store("grad_g")

    def unpack_up():
        unpack(m.grad_u, n_dp * ff)
        store("grad_u")

    def grad_inputs():
        back.finish(m.wide)
        m.grad_x[...] = m.dmid[...] + norm_back(
            m.wide[...], m.gains[:1], m.x[...].astype(FULL)
        )
        store("grad_x")

    def finish_down():
        down.finish(m.grad_d)
        store("grad_d")

    jobs = [finish_down, back.across]
    for t in range(2, ring_o.steps):
        ring_o.step(t)
        if jobs:
            jobs.pop(0)()
    jobs += [unpack_gate, unpack_up, grad_inputs]
    for copy in swap_q:
        copy.wait()
    ring_q.step(0)
    for t in range(1, ring_q.steps):
        ring_q.step(t)
        if jobs:
            jobs.pop(0)()
    for job in jobs:
        job()
    ring_o.finish(m.grad_o)
    store("grad_o")
    ring_q.finish(m.got_q)
    m.grad_kv[...] = jnp.zeros_like(m.grad_kv)
    for i, kv in enumerate(kv_of):
        m.grad_q[:, i * q_width : (i + 1) * q_width] = m.got_q[i, :, :q_width]
        for k in (0, 1):
            first = q_width + k * HEAD_DIM
            m.grad_kv[k, :, kv * HEAD_DIM : (kv + 1) * HEAD_DIM] += m.got_q[
                i, :, first : first + HEAD_DIM
            ].astype(FULL)
    store("grad_q")
    store("grad_kv")
    for copy in stores:
        copy.wait()


LOADED = ("grad_h", "dy", "middle", "gains", "wo", "q", "o", "lse", "cos", "sin", "starts", "wq", "part_d", "x")


def back(n_dp, n_seq, own_ff, ff, kv_of, dtype, ins, shapes):
    tok, width = ins["x"].shape
    every = n_dp * tok
    q_width = ins["q"].shape[1]
    pair = 2 * HEAD_DIM
    length = n_seq * tok
    rank, columns = ins["wq"].shape[2:]
    outs = dict(
        out=shape_of((tok, width), dtype),
        grad_x=shape_of((tok, width), FULL),
        grad_o=shape_of((rank, width), FULL),
        grad_d=shape_of((ff, width), FULL),
        grad_q=shape_of(shapes["q"], LOW),
        grad_kv=shape_of((2,) + shapes["k"], FULL),
        grad_g=shape_of(shapes["gate"], LOW),
        grad_u=shape_of(shapes["gate"], LOW),
    )
    placed = {
        key + "_in" if key in LOADED else key: (
            value,
            ANY,
        )
        for key, value in ins.items()
    }
    scratch = {key: pltpu.VMEM(ins[key].shape, ins[key].dtype) for key in LOADED}
    scratch |= {key: pltpu.VMEM(value.shape, value.dtype) for key, value in outs.items()}
    scratch |= dict(
        store=dma(len(outs)),
        local=dma(4),
        load=dma(2 + len(LOADED)),
        got_q=vm(LOW, n_dp, rank, columns),
        down=DpScatter.scratch(n_dp, ff, width),
        kv_row=vm(LOW, 2, n_seq, tok, pair),
        dmid=vm(FULL, tok, width),
        d_own=vm(LOW, tok, width),
        d_all=vm(LOW, n_dp, tok, width),
        d_sem=DpGather.scratch(n_dp),
        do=vm(LOW, every, q_width),
        k2=vm(LOW, length, pair),
        v2=vm(LOW, length, pair),
        mask=vm(FULL, tok, length),
        dk2=vm(FULL, length, pair),
        dv2=vm(FULL, length, pair),
        dq=vm(FULL, every, q_width),
        dkv=vm(FULL, every, pair),
        dqkv=vm(LOW, every, columns),
        wide=vm(FULL, tok, width),
        landed_q=vm(LOW, n_dp, n_seq, rank, columns),
        part_kv=vm(LOW, n_seq, every, pair),
        part_q=vm(LOW, n_dp, n_seq, rank, columns),
        part_o=vm(LOW, n_seq, rank, width),
        back=DpScatter.scratch(n_dp, tok, width),
        ring_y=RingScatter.scratch(n_seq, tok, width),
        staged=RingScatter.staging(tok, width),
        ring_kv=RingScatter.scratch(n_seq, every, pair),
        ring_q=RingScatter.scratch(n_seq, n_dp, rank, columns),
        ring_o=RingScatter.scratch(n_seq, rank, width),
        swap_q=Exchange.scratch(n_dp),
        swap_gu=Exchange.scratch(n_seq),
        got_gu=vm(LOW, *ins["fin"].shape),
    )
    return run(
        functools.partial(back_kernel, n_dp, n_seq, own_ff, ff, kv_of),
        "attention_backward",
        3,
        placed,
        {key + "_to": (value, ANY) for key, value in outs.items()},
        scratch,
    )


def body(
    n_dp,
    n_seq,
    tokens,
    segment_ids,
    gain_attn,
    w_query,
    w_key,
    w_value,
    w_output,
    gain_mlp,
    w_gate,
    w_up,
    w_down,
    cotangent,
):
    local, width = tokens.shape[1], tokens.shape[2]
    length = n_seq * local
    own_rows = w_query.shape[0]
    own_ff = w_down.shape[0]
    ff = -(-own_ff // 16) * 16
    heads = HEADS // n_dp
    q_width = heads * HEAD_DIM
    x_own = tokens.reshape(local, width)
    dy_own = cotangent.reshape(local, width)

    kv_of = [i * heads // GROUP for i in range(n_dp)]
    got = front(
        n_dp,
        n_seq,
        own_ff,
        kv_of,
        dict(
            x=x_own,
            wg_in=w_gate,
            wu_in=w_up,
            wo=w_output,
            wd=jnp.pad(w_down, ((0, ff - own_ff), (0, 0))),
        ),
        dict(
            wq=w_query,
            wk=w_key,
            wv=w_value,
            gain_one=gain_attn.reshape(1, own_rows),
            gain_two=gain_mlp.reshape(1, own_rows),
            ids=segment_ids.reshape(1, local),
        ),
    )
    fed = feed(
        n_dp,
        n_seq,
        got["second"],
        dy_own,
        got["gu"].reshape(n_seq * own_rows, 2 * n_dp * ff),
        got["wd_all"],
    )
    ins = dict(
        part_y=fed["part_y"],
        grad_h=fed["grad_h_to"],
        fin=fed["fin_to"].reshape(got["gu"].shape),
        part_d=fed["grad_d"],
        x=x_own,
        dy=dy_own,
        middle=got["middle"],
    )
    for name in ("n1", "q", "kv", "o", "lse", "cos", "sin", "starts", "gains", "wq", "wo"):
        ins[name] = got[name + "_out"]
    done = back(
        n_dp,
        n_seq,
        own_ff,
        ff,
        kv_of,
        tokens.dtype,
        ins,
        dict(q=w_query.shape, k=w_key.shape, gate=w_gate.shape),
    )
    return finish(
        {key[: -len("_to")]: value for key, value in done.items()}
        | dict(
            gain_one=gain_attn.reshape(1, own_rows),
            gain_two=gain_mlp.reshape(1, own_rows),
            wq=w_query,
            wk=w_key,
            wv=w_value,
            wg=w_gate,
            wu=w_up,
        ),
        tokens.shape,
        own_ff,
    )


def finish_kernel(m):
    names = ("wg", "grad_g", "grad_x", "grad_d", "out", "grad_o", "wu", "grad_u", "wq", "grad_q")
    loads = {
        name: pltpu.make_async_copy(getattr(m, name), getattr(m, name + "_v"), m.load.at[k])
        for k, name in enumerate(names)
    }
    for copy in loads.values():
        copy.start()
    stores = []

    def store(src, dst):
        copy = pltpu.make_async_copy(src, dst, m.store.at[len(stores)])
        copy.start()
        stores.append(copy)

    def one(weight, raw, into):
        raw = raw[...].astype(FULL)
        into[...] = raw
        return jnp.sum(weight[...].astype(FULL) * raw, 1, keepdims=True)

    def whole(weight, raw, into, target):
        loads[weight].wait()
        loads[raw].wait()
        part = one(getattr(m, weight + "_v"), getattr(m, raw + "_v"), into)
        store(into, target)
        return part

    by_g = whole("wg", "grad_g", m.into_g, m.to_g)
    for name, target in (("grad_x", m.to_x), ("grad_d", m.to_d), ("out", m.to_out), ("grad_o", m.to_o)):
        loads[name].wait()
        store(getattr(m, name + "_v"), target)
    by_u = whole("wu", "grad_u", m.into_u, m.to_u)
    by_q = whole("wq", "grad_q", m.into_q, m.to_q)
    by_k = one(m.wk, m.grad_kv.at[0], m.to_k)
    by_v = one(m.wv, m.grad_kv.at[1], m.to_v)
    m.to_gain_one[...] = to_row(by_q + by_k + by_v) / m.gain_one[...].astype(FULL)
    m.to_gain_two[...] = to_row(by_g + by_u) / m.gain_two[...].astype(FULL)
    for copy in stores:
        copy.wait()


def finish(ins, shape, own_ff):
    rows = ins["wq"].shape[0]
    held = ("gain_one", "gain_two", "wk", "wv", "grad_kv")
    placed = {key: (value, VMEM if key in held else ANY) for key, value in ins.items()}
    outs = dict(
        to_out=(shape_of(ins["out"].shape, ins["out"].dtype), ANY),
        to_x=(shape_of(ins["grad_x"].shape, FULL), ANY),
        to_gain_one=(shape_of((1, rows), FULL), VMEM),
        to_q=(shape_of(ins["wq"].shape, FULL), ANY),
        to_k=(shape_of(ins["wk"].shape, FULL), VMEM),
        to_v=(shape_of(ins["wv"].shape, FULL), VMEM),
        to_o=(shape_of(ins["grad_o"].shape, FULL), ANY),
        to_gain_two=(shape_of((1, rows), FULL), VMEM),
        to_g=(shape_of(ins["wg"].shape, FULL), ANY),
        to_u=(shape_of(ins["wu"].shape, FULL), ANY),
        to_d=(shape_of(ins["grad_d"].shape, FULL), ANY),
    )
    scratch = dict(load=dma(10), store=dma(7))
    for name in ("g", "u", "q"):
        scratch["into_" + name] = vm(FULL, *ins["w" + name].shape)
    for key, value in ins.items():
        if key not in held:
            scratch[key + "_v"] = pltpu.VMEM(value.shape, value.dtype)
    done = run(finish_kernel, "finish", None, placed, outs, scratch)
    done = list(done.values())
    for k in (0, 1):
        done[k] = done[k].reshape(shape)
    for k in (2, 7):
        done[k] = done[k].reshape(rows)
    done[10] = done[10][:own_ff]
    return tuple(done)


def solution(mesh):
    rows = P(("dp", "seq"), None)
    vector = P(("dp", "seq"))
    row = P("dp", "seq", None)
    return jax.shard_map(
        functools.partial(body, mesh.shape["dp"], mesh.shape["seq"]),
        mesh=mesh,
        in_specs=(row, P("dp", "seq"), vector, rows, rows, rows, rows, vector, rows, rows, rows, row),
        out_specs=(row, row, vector, rows, rows, rows, rows, vector, rows, rows, rows),
        check_vma=False,
    )
```

```python
import functools
import math

import jax
import jax.numpy as jnp
from jax import lax
from jax.experimental import pallas as pl
from jax.experimental.pallas import tpu as pltpu
from jax.sharding import PartitionSpec as P

HEADS = 32
HEAD_DIM = 64
KV_HEADS = 4
GROUP = HEADS // KV_HEADS

EPS = 1e-05
ROPE_BASE = 10000.0
MASK_VALUE = -1e30
MESH = pl.DeviceIdType.MESH
LOW = jnp.bfloat16
FULL = jnp.float32
VMEM_BYTES = 61 * 1024 * 1024


def matmul(left, right):
    return jnp.dot(left, right, preferred_element_type=FULL)


def matmul_nt(left, right):
    return lax.dot_general(left, right, (((1,), (1,)), ((), ())), preferred_element_type=FULL)


def matmul_tn(left, right):
    return lax.dot_general(left, right, (((0,), (0,)), ((), ())), preferred_element_type=FULL)


def ring_at(place, n):
    upper = lax.div(place, n // 2)
    return (1 - upper) * 2 * place + upper * (2 * (n - place) - 1)


def ring_place(index, n):
    odd = lax.rem(index, 2)
    return (1 - odd) * lax.div(index, 2) + odd * (n - lax.div(index + 1, 2))


class Where:
    def __init__(self, n_dp, n_seq):
        self.n_dp, self.n_seq = n_dp, n_seq
        self.chips = n_dp // 2
        self.dp = lax.axis_index("dp")
        self.seq = lax.axis_index("seq")
        self.core = lax.rem(self.dp, 2)
        self.chip = lax.div(self.dp, 2)
        self.place = ring_place(self.seq, n_seq)

    def ring(self, step):
        return ring_at(lax.rem(self.place + step + self.n_seq, self.n_seq), self.n_seq)

    def ring_ids(self):
        return [(self.dp, self.ring(1)), (self.dp, self.ring(-1))]

    def seq_ids(self):
        return [
            (self.dp, lax.rem(self.seq + k, self.n_seq)) for k in range(1, self.n_seq)
        ]

    def dp_ids(self):
        return [(lax.rem(self.dp + k, self.n_dp), self.seq) for k in range(1, self.n_dp)]

    def core_id(self):
        return (self.dp + 1 - 2 * self.core, self.seq)

    def chip_ids(self):
        return [
            (2 * lax.rem(self.chip + k, self.chips) + self.core, self.seq)
            for k in range(1, self.chips)
        ]


def greet(ids):
    barrier = pltpu.get_barrier_semaphore()
    for one in ids:
        pl.semaphore_signal(barrier, inc=1, device_id=one, device_id_type=MESH)
    pl.semaphore_wait(barrier, len(ids))


def remote(src, dst, send, recv, target):
    return pltpu.make_async_remote_copy(
        src_ref=src,
        dst_ref=dst,
        send_sem=send,
        recv_sem=recv,
        device_id=target,
        device_id_type=MESH,
    )


class Ring:
    def __init__(self, at, shape, send, recv):
        self.at, self.send, self.recv = at, send, recv
        self.steps = at.n_seq // 2
        self.halves = 2 if len(shape) > 2 or shape[0] % 32 == 0 else 1
        self.half = shape[0] // self.halves
        self.copies = {}

    @staticmethod
    def semaphores(n_seq):
        shape = (2, n_seq // 2, 2)
        return [pltpu.SemaphoreType.DMA(shape), pltpu.SemaphoreType.DMA(shape)]

    def opposite(self, h, d):
        return d == h if self.halves == 2 else d == 0

    def rows(self, h):
        return pl.ds(h * self.half, self.half)

    def go(self, src, dst, d, t, h):
        target = self.at.ring_ids()[d]
        copy = remote(src, dst, self.send.at[d, t, h], self.recv.at[d, t, h], target)
        copy.start()
        self.copies[(d, t, h)] = copy

    def pieces(self):
        return [(h, d) for h in range(self.halves) for d in (0, 1)]


class RingGather(Ring):
    def __init__(self, at, own, everything, send, recv, local):
        super().__init__(at, own.shape, send, recv)
        self.own, self.everything = own, everything
        self.kept = pltpu.make_async_copy(own, everything.at[at.seq], local)
        self.waited = set()

    @staticmethod
    def scratch(n_seq):
        return Ring.semaphores(n_seq)

    def wait(self, key):
        self.copies[key].wait_recv()
        self.waited.add(key)

    def step(self, t):
        if t == 0:
            self.kept.start()
        if t == 1:
            self.kept.wait()
        for h, d in self.pieces():
            if t == self.steps - 1 and not self.opposite(h, d):
                continue
            if t > 0:
                self.wait((d, t - 1, h))
            origin = self.at.ring(-t if d == 0 else t)
            dst = self.everything.at[origin, self.rows(h)]
            self.go(self.own.at[self.rows(h)] if t == 0 else dst, dst, d, t, h)

    def rest(self, t):
        for key in self.copies:
            if key not in self.waited and key[1] <= t:
                self.wait(key)

    def finish(self):
        self.rest(self.steps)
        for copy in self.copies.values():
            copy.wait_send()
        if self.steps == 1:
            self.kept.wait()


class RingScatter(Ring):
    def __init__(self, at, parts, slots, send, recv, staged=None, loads=None, axis=0):
        shape = parts.shape[1:] if axis == 0 else parts.shape[:1] + parts.shape[2:]
        super().__init__(at, shape, send, recv)
        self.axis = axis
        self.parts, self.slots, self.staged, self.loads = parts, slots, staged, loads

    @staticmethod
    def scratch(n_seq, *block):
        return [pltpu.VMEM((2, n_seq // 2) + block, LOW)] + Ring.semaphores(n_seq)

    @staticmethod
    def staging(*block):
        return [pltpu.VMEM((2,) + block, LOW), pltpu.SemaphoreType.DMA((2, 2))]

    def there(self, t, d):
        return self.at.ring(self.steps - t if d == 0 else t - self.steps)

    def block(self, index, h):
        if self.axis:
            return self.parts.at[self.rows(h), index]
        return self.parts.at[index, self.rows(h)]

    def adds(self, t, h, d):
        return t > 1 or (t == 1 and self.opposite(h, d))

    def load(self, t, h, d):
        rows = self.rows(h)
        return pltpu.make_async_copy(self.block(self.there(t, d), h), self.staged.at[d, rows], self.loads.at[d, h])

    def load_all(self, t):
        if self.staged is not None:
            for h, d in self.pieces():
                if t < self.steps and self.adds(t, h, d):
                    self.load(t, h, d).start()
                elif t == self.steps and d == 0:
                    self.load(t, h, d).start()

    def early(self):
        for h, d in self.pieces():
            if self.steps > 1 and not self.opposite(h, d):
                self.go(self.block(self.there(1, d), h), self.slots.at[d, 1, self.rows(h)], d, 1, h)

    def step(self, t):
        if t == 0:
            self.load_all(1)
        for h, d in self.pieces():
            if (t == 0 and not self.opposite(h, d)) or (d, t, h) in self.copies:
                continue
            rows = self.rows(h)
            src = self.block(self.there(t, d), h)
            if self.adds(t, h, d):
                if self.staged is not None:
                    self.load(t, h, d).wait()
                    src = self.staged.at[d, rows]
                self.copies[(d, t - 1, h)].wait_recv()
                held = self.slots.at[d, t - 1, rows]
                held[...] = (held[...].astype(FULL) + src[...].astype(FULL)).astype(LOW)
                src = held
            self.go(src, self.slots.at[d, t, rows], d, t, h)
        if t > 0:
            self.load_all(t + 1)

    def finish(self, out):
        last = self.steps - 1
        if last == 0:
            self.load_all(1)
        for h in range(self.halves):
            rows = self.rows(h)
            if self.staged is None:
                total = self.block(self.at.seq, h)[...].astype(FULL)
            else:
                self.load(self.steps, h, 0).wait()
                total = self.staged[0, rows].astype(FULL)
            for d in (0, 1):
                if last == 0 and not self.opposite(h, d):
                    continue
                self.copies[(d, last, h)].wait_recv()
                total = total + self.slots[d, last, rows].astype(FULL)
            out[rows] = total.astype(out.dtype)
        for copy in self.copies.values():
            copy.wait_send()


class Exchange:
    def __init__(self, me, ids, axis, packed, landing, send, recv, local):
        self.started = 0
        self.kept = pltpu.make_async_copy(packed.at[me], landing.at[me], local)
        self.copies = [
            remote(packed.at[one[axis]], landing.at[me], send.at[k], recv.at[k], one)
            for k, one in enumerate(ids)
        ]

    @staticmethod
    def scratch(n):
        return [pltpu.SemaphoreType.DMA((n - 1,)), pltpu.SemaphoreType.DMA((n - 1,))]

    def start(self, count=None):
        if not self.started:
            self.kept.start()
        first = self.started - 1 if self.started else 0
        last = len(self.copies) if count is None else min(first + count, len(self.copies))
        for copy in self.copies[first:last]:
            copy.start()
        self.started = last + 1

    def arrived(self):
        self.kept.wait()
        for copy in self.copies:
            copy.wait_recv()

    def finish(self):
        for copy in self.copies:
            copy.wait_send()


def seq_exchange(at, *refs):
    return Exchange(at.seq, at.seq_ids(), 1, *refs)


def dp_exchange(at, *refs):
    return Exchange(at.dp, at.dp_ids(), 0, *refs)


class DpGather:
    def __init__(self, at, own, everything, send, recv, local):
        self.kept = pltpu.make_async_copy(own, everything.at[at.dp], local)
        slot = everything.at[at.dp]
        self.out = [
            remote(own, slot, send.at[k], recv.at[k], one) for k, one in enumerate(at.chip_ids())
        ]
        base = at.chips - 1
        self.mate = remote(own, slot, send.at[base], recv.at[base], at.core_id())
        self.handed = []
        for k in range(1, at.chips):
            origin = 2 * lax.rem(at.chip + at.chips - k, at.chips) + at.core
            there = everything.at[origin]
            self.handed.append(
                remote(there, there, send.at[base + k], recv.at[base + k], at.core_id())
            )

    @staticmethod
    def scratch(n_dp):
        return [pltpu.SemaphoreType.DMA((n_dp - 1,)), pltpu.SemaphoreType.DMA((n_dp - 1,))]

    def start(self):
        for copy in self.out:
            copy.start()
        self.mate.start()
        self.kept.start()

    def hand(self):
        for copy, onward in zip(self.out, self.handed):
            copy.wait_recv()
            onward.start()

    def arrived(self):
        self.kept.wait()
        self.mate.wait_recv()
        for copy in self.handed:
            copy.wait_recv()

    def finish(self):
        for copy in self.out + [self.mate] + self.handed:
            copy.wait_send()


def add_rows(rows, chunk, one):
    def step(r, carry):
        one(pl.ds(pl.multiple_of(r * chunk, chunk), chunk))
        return carry

    lax.fori_loop(0, rows // chunk, step, 0)


def chunk_of(rows, columns):
    chunk = rows
    while chunk % 32 == 0 and chunk * columns > 65536:
        chunk //= 2
    return chunk


class DpScatter:
    def __init__(self, at, parts, core, other, send, recv):
        self.at, self.parts, self.core, self.other = at, parts, core, other
        self.send, self.recv = send, recv
        self.rows, self.columns = parts.shape[1], parts.shape[2]

    @staticmethod
    def scratch(n_dp, rows, columns):
        chips = n_dp // 2
        return [
            pltpu.VMEM((chips, rows, columns), LOW),
            pltpu.VMEM((max(chips - 1, 1), rows, columns), LOW),
            pltpu.SemaphoreType.DMA((2 * chips - 1,)),
            pltpu.SemaphoreType.DMA((2 * chips - 1,)),
        ]

    def to_core(self, k):
        at = self.at
        return remote(
            self.parts.at[2 * k + 1 - at.core],
            self.core.at[k],
            self.send.at[k],
            self.recv.at[k],
            at.core_id(),
        )

    def to_chip(self, k):
        at = self.at
        sem = at.chips + k - 1
        return remote(
            self.core.at[lax.rem(at.chip + k, at.chips)],
            self.other.at[k - 1],
            self.send.at[sem],
            self.recv.at[sem],
            at.chip_ids()[k - 1],
        )

    def start(self):
        for k in range(self.at.chips):
            self.to_core(k).start()

    def add_core(self, k):
        held = self.core.at[k]
        mine = self.parts.at[2 * k + self.at.core]

        def one(rows):
            held[rows] = (held[rows].astype(FULL) + mine[rows].astype(FULL)).astype(LOW)

        add_rows(self.rows, chunk_of(self.rows, self.columns), one)

    def across(self):
        at = self.at
        for k in range(1, at.chips):
            there = lax.rem(at.chip + k, at.chips)
            self.to_core(there).wait_recv()
            self.add_core(there)
            self.to_chip(k).start()

    def finish(self, out):
        at = self.at
        self.to_core(at.chip).wait_recv()
        for k in range(1, at.chips):
            self.to_chip(k).wait_recv()
        held = self.core.at[at.chip]
        mine = self.parts.at[2 * at.chip + at.core]

        def one(rows):
            total = held[rows].astype(FULL) + mine[rows].astype(FULL)
            for k in range(1, at.chips):
                total = total + self.other[k - 1, rows].astype(FULL)
            out[rows] = total.astype(out.dtype)

        add_rows(self.rows, chunk_of(self.rows, self.columns), one)
        for k in range(at.chips):
            self.to_core(k).wait_send()
        for k in range(1, at.chips):
            self.to_chip(k).wait_send()


def comm_params(number):
    if number is None:
        return pltpu.CompilerParams(vmem_limit_bytes=VMEM_BYTES)
    return pltpu.CompilerParams(
        collective_id=number, has_side_effects=True, vmem_limit_bytes=VMEM_BYTES
    )


ANY = pl.BlockSpec(memory_space=pl.ANY)
VMEM = pl.BlockSpec(memory_space=pltpu.VMEM)


def shape_of(dims, kind):
    return jax.ShapeDtypeStruct(dims, kind)


class Refs:
    def __init__(self, names, refs):
        refs = list(refs)
        for name, count in names:
            taken, refs = refs[: max(count, 1)], refs[max(count, 1) :]
            setattr(self, name, taken if count else taken[0])


def run(kernel, name, number, ins, outs, scratch):
    names = [(key, 0) for key in ins] + [(key, 0) for key in outs]
    shapes = []
    for key, value in scratch.items():
        if isinstance(value, list):
            names.append((key, len(value)))
            shapes += value
        else:
            names.append((key, 0))
            shapes.append(value)
    found = pl.pallas_call(
        lambda *refs: kernel(Refs(names, refs)),
        name=name,
        out_shape=[shape for shape, _ in outs.values()],
        in_specs=[spec for _, spec in ins.values()],
        out_specs=[spec for _, spec in outs.values()],
        scratch_shapes=shapes,
        compiler_params=comm_params(number),
    )(*[array for array, _ in ins.values()])
    return dict(zip(outs, found))


def dma(*dims):
    return pltpu.SemaphoreType.DMA(dims)


def vm(kind, *dims):
    return pltpu.VMEM(dims, kind)


def lanes(rows):
    return lax.broadcasted_iota(jnp.int32, (rows, 2 * HEAD_DIM), 1)


def low_head(rows):
    return lanes(rows) < HEAD_DIM


def swapped(pair):
    half = HEAD_DIM // 2
    first = lax.rem(lanes(pair.shape[0]), HEAD_DIM) < half
    return jnp.where(
        first, pltpu.roll(pair, 2 * HEAD_DIM - half, 1), pltpu.roll(pair, half, 1)
    )


def split_heads(pair):
    wide = pair.astype(FULL)
    low = low_head(pair.shape[0])
    return jnp.concatenate(
        [jnp.where(low, wide, 0.0), jnp.where(low, 0.0, wide)], 0
    ).astype(LOW)


def join_heads(both):
    rows = both.shape[0] // 2
    return jnp.where(low_head(rows), both[:rows], both[rows:])


def spread_kv(kv):
    wide = kv.astype(FULL)
    turned = pltpu.roll(wide, HEAD_DIM, 1)
    low = low_head(kv.shape[0])
    return jnp.where(low, wide, turned).astype(LOW), jnp.where(low, turned, wide).astype(LOW)


def mask_of(position, start, length):
    key = lax.broadcasted_iota(jnp.int32, (start.shape[0], length), 1)
    return jnp.where((key <= position) & (key >= start), 0.0, MASK_VALUE)


def own_positions(at, tok):
    return at.seq * tok + lax.broadcasted_iota(jnp.int32, (tok, 1), 0)


def rows_of(r, count):
    return pl.ds(pl.multiple_of(r * count, count), count)


def to_column(row):
    n = row.shape[1]
    here = lax.broadcasted_iota(jnp.int32, (n, n), 0) == lax.broadcasted_iota(jnp.int32, (n, n), 1)
    return jnp.sum(jnp.where(here, row.astype(FULL), 0.0), 1, keepdims=True)


def to_row(column):
    n = column.shape[0]
    here = lax.broadcasted_iota(jnp.int32, (n, n), 0) == lax.broadcasted_iota(jnp.int32, (n, n), 1)
    return jnp.sum(jnp.where(here, column, 0.0), 0, keepdims=True)


def front_kernel(n_dp, n_seq, own_ff, ff, kv_of, m):
    at = Where(n_dp, n_seq)
    tok, width = m.x.shape
    q_width = m.q.shape[1]
    groups = q_width // (2 * HEAD_DIM)
    rank = n_seq * m.pq.shape[1]
    length = n_seq * tok
    greet(at.seq_ids() + at.dp_ids())
    swap_q = dp_exchange(at, m.pq, m.landed, *m.swap_q_sem, m.local.at[0])
    x_g = DpGather(at, m.x, m.xs, *m.x_sem, m.local.at[1])
    row_x = seq_exchange(at, m.seg_rows, m.seg_row, *m.row_x_sem, m.local.at[2])
    row_g = DpGather(at, m.seg_row, m.segs, *m.row_g_sem, m.local.at[3])
    col_g = DpGather(at, m.seg_col, m.seg_cols, *m.col_g_sem, m.local.at[4])
    ring_q = RingGather(at, m.landed, m.wq_all, *m.ring_q_sem, m.local.at[5])
    ring_o = RingGather(at, m.wo, m.wo_all, *m.ring_o_sem, m.local.at[6])
    ring_kv = RingGather(at, m.kv_own, m.kv_all, *m.ring_kv_sem, m.local.at[7])
    swap_gu = seq_exchange(at, m.pgu, m.gu, *m.swap_gu_sem, m.local.at[8])
    down = DpGather(at, m.wd, m.wd_all, *m.down_sem, m.local.at[9])
    loads = [
        pltpu.make_async_copy(src, dst, m.load.at[k])
        for k, (src, dst) in enumerate(((m.wg_in, m.wg), (m.wu_in, m.wu), (m.x, m.x_own)))
    ]
    stores = []

    def store(src, dst):
        copy = pltpu.make_async_copy(src, dst, m.local.at[10 + len(stores)])
        copy.start()
        stores.append(copy)

    ring_o.step(0)
    for copy in loads:
        copy.start()

    for i, kv in enumerate(kv_of):
        m.pq[i, :, :q_width] = m.wq[:, i * q_width : (i + 1) * q_width]
        for weight, first in ((m.wk, q_width), (m.wv, q_width + HEAD_DIM)):
            m.pq[i, :, first : first + HEAD_DIM] = weight[:, kv * HEAD_DIM : (kv + 1) * HEAD_DIM]
    swap_q.start()
    x_g.start()
    ids = m.ids[...]
    rank_own = m.pq.shape[1]
    m.seg_rows[...] = jnp.broadcast_to(ids.astype(FULL)[None], m.seg_rows.shape)
    for k, own_gain in ((1, m.gain_one), (2, m.gain_two)):
        m.seg_rows[:, k : k + 1, :rank_own] = jnp.broadcast_to(
            own_gain[...].astype(FULL)[None], (n_seq, 1, rank_own)
        )
    m.seg_col[...] = jnp.broadcast_to(to_column(ids), m.seg_col.shape)
    row_x.start()
    col_g.start()

    def pack(k, weight, first):
        loads[k].wait()
        if ff > own_ff:
            m.pgu[:, :, first : first + n_dp * ff] = jnp.zeros(
                m.pgu.shape[:2] + (n_dp * ff,), LOW
            )
        for s in range(n_seq):
            for i in range(n_dp):
                piece = weight[:, (i * n_seq + s) * own_ff : (i * n_seq + s + 1) * own_ff]
                m.pgu[s, :, first + i * ff : first + i * ff + own_ff] = piece

    later = list(range(1, ring_o.steps))
    ring_o.step(later.pop(0))
    swap_q.arrived()
    ring_q.step(0)
    row_x.arrived()
    row_g.start()

    def hand():
        x_g.hand()
        row_g.hand()
        col_g.hand()
        down.start()

    def norm():
        x_g.arrived()
        row_g.arrived()
        m.gains[...] = jnp.zeros_like(m.gains)
        for k in (0, 1):
            for i in range(n_dp):
                for s in range(n_seq):
                    first = (i * n_seq + s) * rank_own
                    m.gains[k : k + 1, first : first + rank_own] = m.segs[
                        i, s, k + 1 : k + 2, :rank_own
                    ]
        store(m.gains, m.gains_out)
        for r in range(n_dp):
            x = m.xs[r].astype(FULL)
            scale = lax.rsqrt(jnp.mean(x * x, -1, keepdims=True) + EPS)
            m.n1[r] = (x * scale * m.gains[:1]).astype(LOW)
        store(m.n1, m.n1_out)

    def place():
        col_g.arrived()
        position = own_positions(at, tok)
        first = lax.rem(lanes(tok), HEAD_DIM) < HEAD_DIM // 2
        number = lax.rem(lanes(tok), HEAD_DIM // 2).astype(FULL)
        freqs = jnp.exp(number * (-2.0 * math.log(ROPE_BASE) / HEAD_DIM))
        for r in range(n_dp):
            segs = jnp.concatenate([m.segs[r, s, :1] for s in range(n_seq)], 1)
            own = m.seg_cols[r][:, :1]
            start = jnp.sum((segs < own).astype(jnp.int32), 1, keepdims=True)
            turned = (position - start).astype(FULL) * freqs
            rows = slice(r * tok, (r + 1) * tok)
            m.cos[rows] = jnp.cos(turned)
            sines = jnp.sin(turned)
            m.sin[rows] = jnp.where(first, -sines, sines)
            m.starts[rows] = jnp.broadcast_to(start, (tok, 2 * HEAD_DIM))
        store(m.cos, m.cos_out)
        store(m.sin, m.sin_out)
        store(m.starts, m.starts_out)

    pack(0, m.wg, 0)
    ring_q.step(1)
    jobs = [lambda: (hand(), norm(), place()), lambda: pack(1, m.wu, n_dp * ff)]
    for t in range(2, ring_q.steps):
        ring_q.step(t)
        if jobs:
            jobs.pop(0)()
    for job in jobs:
        job()
    ring_q.finish()
    if later:
        ring_o.step(later.pop(0))
    store(m.wq_all, m.wq_out)

    m.qkv[...] = sum(
        matmul(
            m.n1[:, :, i * rank : (i + 1) * rank].reshape(n_dp * tok, rank),
            m.wq_all[:, i].reshape(rank, q_width + 2 * HEAD_DIM),
        )
        for i in range(n_dp)
    )
    factor = HEAD_DIM ** (-0.5)
    for g in range(groups + 1):
        cols = slice(g * 2 * HEAD_DIM, (g + 1) * 2 * HEAD_DIM)
        pair = m.qkv[:, cols]
        turned = pair * m.cos[...] + swapped(pair) * m.sin[...]
        if g < groups:
            m.q[:, cols] = (turned * factor).astype(LOW)
        else:
            m.kv_own[...] = jnp.where(low_head(pair.shape[0]), turned, pair).astype(LOW)
    ring_kv.step(0)
    store(m.q, m.q_out)
    for t in range(1, ring_kv.steps):
        ring_kv.step(t)
        if later and t > 1:
            ring_o.step(later.pop(0))
    for t in later:
        ring_o.step(t)
    down.hand()
    ring_kv.finish()
    swap_gu.start(2)
    store(m.kv_all, m.kv_out)
    m.lse[...] = jnp.zeros_like(m.lse)
    back = DpScatter(at, m.parts, *m.back)
    chips = [lax.rem(at.chip + k, at.chips) for k in range(1, at.chips)] + [at.chip]
    order = [2 * chip + c for chip in chips for c in (1 - at.core, at.core)]
    for place_of, r in enumerate(order):
        rows = rows_of(r, tok)
        k, v = spread_kv(m.kv_all[:, rows].reshape(length, 2 * HEAD_DIM))
        m.k2[...] = k
        m.v2[...] = v
        m.mask[...] = mask_of(own_positions(at, tok), m.starts[rows, :1], length)

        def group(g, carry):
            cols = rows_of(g, 2 * HEAD_DIM)
            raw = matmul_nt(split_heads(m.q[rows, cols]), m.k2[...])
            raw = raw + jnp.concatenate([m.mask[...]] * 2, 0)
            top = jnp.max(raw, -1, keepdims=True)
            probs = jnp.exp(raw - top)
            total = jnp.sum(probs, -1, keepdims=True)
            probs = (probs * (1.0 / total)).astype(LOW)
            m.o[rows, cols] = join_heads(matmul(probs, m.v2[...])).astype(LOW)
            here = lanes(2 * tok) == r * groups + g
            m.lse[...] = jnp.where(here, top + jnp.log(total), m.lse[...])
            return carry

        lax.fori_loop(0, groups, group, 0)
        if place_of == 0:
            swap_gu.start()
            ring_o.finish()
            store(m.wo_all, m.wo_out)
        m.parts[r] = matmul(m.o[rows], m.wo_all[...].reshape(q_width, width)).astype(LOW)
        if place_of % 2 == 0:
            back.to_core(chips[place_of // 2]).start()
        if place_of == n_dp - 2:
            back.across()
    store(m.o, m.o_out)
    store(m.lse, m.lse_out)
    back.finish(m.middle)
    loads[2].wait()
    middle = m.x_own[...].astype(FULL) + m.middle[...]
    m.middle[...] = middle
    scale = lax.rsqrt(jnp.mean(middle * middle, -1, keepdims=True) + EPS)
    m.second[...] = (middle * scale * m.gains[1:2]).astype(LOW)
    swap_gu.arrived()
    down.arrived()
    for one in (swap_q, x_g, row_x, row_g, col_g, swap_gu, down):
        one.finish()
    for copy in stores:
        copy.wait()


def front(n_dp, n_seq, own_ff, kv_of, held, small):
    tok, width = held["x"].shape
    rank = small["wq"].shape[0]
    q_width = width // n_dp
    groups = q_width // (2 * HEAD_DIM)
    pair = 2 * HEAD_DIM
    columns = q_width + pair
    length = n_seq * tok
    every = n_dp * tok
    wd = held["wd"]
    ff = wd.shape[0]
    gu_width = 2 * n_dp * ff
    ins = {key: (value, ANY) for key, value in held.items()}
    ins |= {key: (value, VMEM) for key, value in small.items()}
    kept = dict(
        n1=(LOW, n_dp, tok, width),
        q=(LOW, every, q_width),
        kv_all=(LOW, n_seq, every, pair),
        o=(LOW, every, q_width),
        lse=(FULL, 2 * tok, pair),
        cos=(FULL, every, pair),
        sin=(FULL, every, pair),
        starts=(jnp.int32, every, pair),
        gains=(FULL, 8, width),
        wq_all=(LOW, n_seq, n_dp, rank, columns),
        wo_all=(LOW, n_seq, rank, width),
    )
    outs = {
        key.replace("_all", "") + "_out": (shape_of(dims[1:], dims[0]), ANY)
        for key, dims in kept.items()
    }
    outs["gu"] = (shape_of((n_seq, rank, gu_width), LOW), ANY)
    outs["wd_all"] = (shape_of((n_dp,) + wd.shape, LOW), ANY)
    outs["middle"] = (shape_of((tok, width), FULL), VMEM)
    outs["second"] = (shape_of((tok, width), LOW), VMEM)
    scratch = {key: vm(*dims) for key, dims in kept.items()}
    scratch |= dict(
        load=dma(3),
        wg=vm(LOW, *held["wg_in"].shape),
        wu=vm(LOW, *held["wg_in"].shape),
        x_own=vm(LOW, tok, width),
        pq=vm(LOW, n_dp, rank, columns),
        seg_rows=vm(FULL, n_seq, 8, tok),
        seg_col=vm(FULL, tok, pair),
        landed=vm(LOW, n_dp, rank, columns),
        xs=vm(LOW, n_dp, tok, width),
        seg_row=vm(FULL, n_seq, 8, tok),
        segs=vm(FULL, n_dp, n_seq, 8, tok),
        seg_cols=vm(FULL, n_dp, tok, pair),
        kv_own=vm(LOW, every, pair),
        mask=vm(FULL, tok, length),
        pgu=vm(LOW, n_seq, rank, gu_width),
        qkv=vm(FULL, every, columns),
        k2=vm(LOW, length, pair),
        v2=vm(LOW, length, pair),
        parts=vm(LOW, n_dp, tok, width),
        back=DpScatter.scratch(n_dp, tok, width),
        local=dma(10 + len(kept)),
        swap_q_sem=Exchange.scratch(n_dp),
        x_sem=DpGather.scratch(n_dp),
        row_x_sem=Exchange.scratch(n_seq),
        row_g_sem=DpGather.scratch(n_dp),
        col_g_sem=DpGather.scratch(n_dp),
        ring_q_sem=Ring.semaphores(n_seq),
        ring_o_sem=Ring.semaphores(n_seq),
        ring_kv_sem=Ring.semaphores(n_seq),
        swap_gu_sem=Exchange.scratch(n_seq),
        down_sem=DpGather.scratch(n_dp),
    )
    return run(
        functools.partial(front_kernel, n_dp, n_seq, own_ff, ff, kv_of), "attention_forward", 1, ins, outs, scratch
    )


def feed_kernel(n_dp, n_seq, m):
    at = Where(n_dp, n_seq)
    tok, width = m.second.shape
    wide = m.wgu.shape[2]
    part = wide // 2
    rank = width // n_dp
    length = n_seq * tok
    greet(at.ring_ids() + at.dp_ids())
    gu = DpGather(at, m.gu, m.wgu, *m.gu_sem, m.local.at[0])
    ring_n = RingGather(at, m.second, m.second_all, *m.ring_n, m.local.at[1])
    ring_dy = RingGather(at, m.dy, m.dy_all, *m.ring_dy, m.local.at[2])
    ring_h = RingScatter(at, m.part, *m.ring_h)
    side = DpScatter(at, m.wgu, *m.side)
    gu.start()
    held = pltpu.make_async_copy(m.wd_all, m.wd, m.local.at[3])
    held.start()
    ring_n.step(0)
    for t in range(1, ring_n.steps):
        ring_n.step(t)
    ring_dy.step(0)
    gu.hand()
    ring_n.finish()
    gu.arrived()
    held.wait()
    stores = []

    def store(src, dst, k):
        copy = pltpu.make_async_copy(src, dst, m.local.at[k])
        copy.start()
        stores.append(copy)

    def stored():
        while stores:
            stores.pop().wait()

    def forward(c):
        blocks = slice(2 * c, 2 * c + 2)
        normed = m.second_all[blocks].reshape(2 * tok, width)
        both = matmul(normed, m.wgu[...].reshape(width, wide))
        gate, upward = both[:, :part], both[:, part:]
        sigma = jax.nn.sigmoid(gate)
        silu = gate * sigma
        hidden = (silu * upward).astype(LOW)
        m.by_up[blocks] = silu.reshape(2, tok, part)
        m.by_gate[blocks] = (upward * sigma * (1.0 + gate * (1.0 - sigma))).reshape(2, tok, part)
        m.hidden[blocks] = hidden.reshape(2, tok, part)
        out = matmul(hidden, m.wd[...].reshape(part, width))
        m.part[blocks] = out.astype(LOW).reshape(2, tok, width)
        copy = pltpu.make_async_copy(m.part.at[blocks], m.part_y.at[blocks], m.store.at[c])
        copy.start()
        stores.append(copy)

    def backward(blocks):
        rows = len(blocks) * tok
        dy = jnp.concatenate([m.dy_all[b] for b in blocks], 0)
        grad = matmul_nt(dy, m.wd[...].reshape(part, width))
        for k, b in enumerate(blocks):
            one = grad[k * tok : (k + 1) * tok]
            m.grads[b, :, :part] = (one * m.by_gate[b]).astype(LOW)
            m.grads[b, :, part:] = (one * m.by_up[b]).astype(LOW)
        both = jnp.concatenate([m.grads[b] for b in blocks], 0)
        for i in range(n_dp):
            cols = slice(i * rank, (i + 1) * rank)
            out = matmul_nt(both, m.wgu[i]).astype(LOW)
            for k, b in enumerate(blocks):
                m.part[b, :, cols] = out[k * tok : (k + 1) * tok]

    jobs = [functools.partial(forward, c) for c in range(n_seq // 2)]
    jobs.append(stored)
    jobs.append(lambda: backward([at.seq]))
    for t in range(1, ring_dy.steps):
        for _ in range(3 if t == 1 else 4):
            if jobs:
                jobs.pop(0)()
        ring_dy.step(t)
        if t < ring_dy.steps - 1:
            jobs.append(functools.partial(backward, [at.ring(-t), at.ring(t)]))
    for job in jobs:
        job()
    if ring_dy.steps > 1:
        ring_dy.rest(ring_dy.steps - 2)
        backward([at.ring(1 - ring_dy.steps), at.ring(ring_dy.steps - 1)])
    ring_h.early()
    ring_dy.finish()
    backward([at.ring(ring_dy.steps)])
    gu.finish()

    ring_h.step(0)

    def grad_gu(k):
        chip = lax.rem(at.chip + 1 + k, at.chips)
        for c in (1 - at.core, at.core):
            normed = m.second_all[:, :, rows_of(2 * chip + c, rank)].reshape(length, rank)
            m.wgu[2 * chip + c] = matmul_tn(normed, m.grads[...].reshape(length, wide)).astype(LOW)
            if c is not at.core:
                side.to_core(chip).start()

    def grad_down():
        step = width // n_dp
        for i in range(n_dp):
            cols = slice(i * step, (i + 1) * step)
            dy = m.dy_all[:, :, cols].reshape(length, step)
            m.wd[:, :, cols] = (
                matmul_tn(m.hidden[...].reshape(length, part), dy)
                .astype(LOW)
                .reshape(m.wd.shape[:2] + (step,))
            )
        store(m.wd, m.grad_d, 3)

    jobs = [functools.partial(grad_gu, k) for k in range(at.chips)]
    jobs += [side.across, grad_down]
    for t in range(1, ring_h.steps):
        for _ in range(2):
            if jobs:
                jobs.pop(0)()
        ring_h.step(t)
    for job in jobs:
        job()
    ring_h.finish(m.grad_h)
    store(m.grad_h, m.grad_h_to, 4)
    side.finish(m.fin)
    store(m.fin, m.fin_to, 5)
    stored()


def feed(n_dp, n_seq, second, dy, gu, wd):
    tok, width = second.shape
    deep, wide = gu.shape
    ff = wd.shape[1]
    part = wide // 2
    ins = dict(second=(second, ANY), dy=(dy, ANY), gu=(gu, ANY), wd_all=(wd, ANY))
    outs = dict(
        part_y=(shape_of((n_seq, tok, width), LOW), ANY),
        grad_h_to=(shape_of((tok, width), FULL), ANY),
        fin_to=(shape_of((deep, wide), LOW), ANY),
        grad_d=(shape_of(wd.shape, LOW), ANY),
    )
    scratch = dict(
        local=dma(6),
        grad_h=vm(FULL, tok, width),
        fin=vm(LOW, deep, wide),
        wd=vm(LOW, *wd.shape),
        store=dma(n_seq // 2),
        second_all=vm(LOW, n_seq, tok, width),
        dy_all=vm(LOW, n_seq, tok, width),
        wgu=vm(LOW, n_dp, deep, wide),
        by_gate=vm(FULL, n_seq, tok, part),
        by_up=vm(FULL, n_seq, tok, part),
        hidden=vm(LOW, n_seq, tok, part),
        grads=vm(LOW, n_seq, tok, wide),
        part=vm(LOW, n_seq, tok, width),
        gu_sem=DpGather.scratch(n_dp),
        ring_n=Ring.semaphores(n_seq),
        ring_dy=Ring.semaphores(n_seq),
        ring_h=RingScatter.scratch(n_seq, tok, width),
        side=DpScatter.scratch(n_dp, deep, wide),
    )
    return run(functools.partial(feed_kernel, n_dp, n_seq), "feed_forward", 2, ins, outs, scratch)


def back_kernel(n_dp, n_seq, own_ff, ff, kv_of, m):
    at = Where(n_dp, n_seq)
    tok, width = m.x.shape
    q_width = m.q.shape[1]
    groups = q_width // (2 * HEAD_DIM)
    rank = n_seq * m.wq.shape[2]
    length = n_seq * tok
    pair = 2 * HEAD_DIM
    greet(at.seq_ids() + at.dp_ids())
    swap_gu = [
        remote(m.fin.at[one[1]], m.got_gu.at[at.seq], m.swap_gu[0].at[k], m.swap_gu[1].at[k], one)
        for k, one in enumerate(at.seq_ids())
    ]
    ring_y = RingScatter(at, m.part_y, *m.ring_y, *m.staged)
    d_g = DpGather(at, m.d_own, m.d_all, *m.d_sem, m.local.at[0])
    ring_kv = RingScatter(at, m.part_kv, *m.ring_kv)
    ring_q = RingScatter(at, m.landed_q, *m.ring_q, axis=1)
    ring_o = RingScatter(at, m.part_o, *m.ring_o)
    down = DpScatter(at, m.part_d, *m.down)
    back = DpScatter(at, m.d_all, *m.back)
    swap_q = [
        remote(m.part_q.at[one[0]], m.landed_q.at[at.dp], m.swap_q[0].at[k], m.swap_q[1].at[k], one)
        for k, one in enumerate(at.dp_ids())
    ]
    ring_y.step(0)
    stores = []

    def store(key):
        copy = pltpu.make_async_copy(getattr(m, key), getattr(m, key + "_to"), m.store.at[len(stores)])
        copy.start()
        stores.append(copy)

    waiting = list(swap_gu)

    def pace(count=1):
        for copy in waiting[:count]:
            copy.start()
        del waiting[:count]

    loads = [
        pltpu.make_async_copy(getattr(m, key + "_in"), getattr(m, key), m.load.at[2 + k])
        for k, key in enumerate(LOADED)
    ]
    for copy in loads:
        copy.start()

    def load_kv(r):
        block = m.kv.at[:, pl.ds(r * tok, tok)]
        return pltpu.make_async_copy(block, m.kv_row.at[r % 2], m.load.at[r % 2])

    load_kv(0).start()
    own_gu = pltpu.make_async_copy(m.fin.at[at.seq], m.got_gu.at[at.seq], m.local.at[3])
    own_gu.start()

    def norm_back(grad, gain, value):
        grad = grad * gain
        scale = lax.rsqrt(jnp.mean(value * value, -1, keepdims=True) + EPS)
        normed = value * scale
        return scale * (grad - normed * jnp.mean(grad * normed, -1, keepdims=True))

    for copy in loads[:4]:
        copy.wait()
    m.dmid[...] = m.dy[...].astype(FULL) + norm_back(
        m.grad_h[...], m.gains[1:2], m.middle[...]
    )
    m.d_own[...] = m.dmid[...].astype(LOW)
    d_g.start()
    if ring_y.steps > 1:
        ring_y.step(1)
    d_g.hand()
    for copy in loads[4:]:
        copy.wait()
    d_g.arrived()
    down.start()
    m.do[...] = matmul_nt(
        m.d_all[...].reshape(n_dp * tok, width), m.wo[...].reshape(q_width, width)
    ).astype(LOW)
    later = list(range(2, ring_y.steps))
    down.across()
    if later:
        ring_y.step(later.pop(0))
    for r in range(n_dp):
        rows = slice(r * tok, (r + 1) * tok)
        load_kv(r).wait()
        if r + 1 < n_dp:
            load_kv(r + 1).start()
        k, v = spread_kv(m.kv_row[r % 2].reshape(length, pair))
        m.k2[...] = k
        m.v2[...] = v
        m.mask[...] = mask_of(own_positions(at, tok), m.starts[rows, :1], length)
        m.dk2[...] = jnp.zeros_like(m.dk2)
        m.dv2[...] = jnp.zeros_like(m.dv2)

        def group(g, carry):
            cols = rows_of(g, pair)
            q2 = split_heads(m.q[rows, cols])
            do2 = split_heads(m.do[rows, cols])
            raw = matmul_nt(q2, m.k2[...])
            raw = raw + jnp.concatenate([m.mask[...]] * 2, 0)
            here = lanes(2 * tok) == r * groups + g
            lse = jnp.sum(jnp.where(here, m.lse[...], 0.0), 1, keepdims=True)
            probs = jnp.exp(raw - lse)
            grad_probs = matmul_nt(do2, m.v2[...])
            delta = jnp.sum(probs * grad_probs, -1, keepdims=True)
            grad_raw = (probs * (grad_probs - delta)).astype(LOW)
            m.dq[rows, cols] = join_heads(matmul(grad_raw, m.k2[...]))
            m.dk2[...] += matmul_tn(grad_raw, q2)
            m.dv2[...] += matmul_tn(probs.astype(LOW), do2)
            return carry

        lax.fori_loop(0, groups, group, 0)
        dk = m.dk2[...]
        dv = m.dv2[...]
        dkv = jnp.where(
            low_head(length), dk + pltpu.roll(dk, HEAD_DIM, 1), dv + pltpu.roll(dv, HEAD_DIM, 1)
        )
        m.part_kv[:, rows] = dkv.astype(LOW).reshape(n_seq, tok, pair)
        if later and r % 2:
            ring_y.step(later.pop(0))
    for t in later:
        ring_y.step(t)
    ring_kv.step(0)
    m.part_o[...] = (
        matmul_tn(m.o[...], m.d_all[...].reshape(n_dp * tok, width))
        .astype(LOW)
        .reshape(m.part_o.shape)
    )
    d_g.finish()
    for t in range(1, ring_kv.steps):
        ring_kv.step(t)
        pace()
    ring_kv.finish(m.dkv)
    ring_o.step(0)
    factor = HEAD_DIM ** (-0.5)
    for g in range(groups + 1):
        cols = slice(g * pair, (g + 1) * pair)
        grad = m.dq[:, cols] * factor if g < groups else m.dkv[...]
        turned = grad * m.cos[...] - swapped(grad) * m.sin[...]
        if g == groups:
            turned = jnp.where(low_head(grad.shape[0]), turned, grad)
        m.dqkv[:, cols] = turned.astype(LOW)
    ring_y.finish(m.wide)
    n1 = m.ring_y[0].at[0, pl.ds(0, n_dp)]
    fetch = pltpu.make_async_copy(m.n1, n1, m.local.at[2])
    fetch.start()
    m.out[...] = (m.middle[...] + m.wide[...]).astype(m.out.dtype)
    store("out")
    pace()
    fetch.wait()
    for i in range(n_dp):
        cols = slice(i * rank, (i + 1) * rank)
        m.part_q[i] = (
            matmul_tn(n1[:, :, cols].reshape(n_dp * tok, rank), m.dqkv[...])
            .astype(LOW)
            .reshape(n_seq, rank // n_seq, q_width + pair)
        )
    for copy in swap_q:
        copy.start()
    m.landed_q[at.dp] = m.part_q[at.dp]
    pace()
    if ring_o.steps > 1:
        ring_o.step(1)
    pace()
    for i in range(n_dp):
        cols = slice(i * rank, (i + 1) * rank)
        weight = m.wq[:, i].reshape(rank, q_width + pair)
        m.d_all[:, :, cols] = (
            matmul_nt(m.dqkv[...], weight).astype(LOW).reshape(n_dp, tok, rank)
        )
    back.start()
    pace()
    pace(len(waiting))

    def unpack(grad, first):
        for s in range(n_seq):
            for i in range(n_dp):
                grad[:, (i * n_seq + s) * own_ff : (i * n_seq + s + 1) * own_ff] = m.got_gu[
                    s, :, first + i * ff : first + i * ff + own_ff
                ]

    def unpack_gate():
        for copy in swap_gu:
            copy.wait()
        own_gu.wait()
        unpack(m.grad_g, 0)
        store("grad_g")

    def unpack_up():
        unpack(m.grad_u, n_dp * ff)
        store("grad_u")

    def grad_inputs():
        back.finish(m.wide)
        m.grad_x[...] = m.dmid[...] + norm_back(
            m.wide[...], m.gains[:1], m.x[...].astype(FULL)
        )
        store("grad_x")

    def finish_down():
        down.finish(m.grad_d)
        store("grad_d")

    jobs = [finish_down, back.across]
    for t in range(2, ring_o.steps):
        ring_o.step(t)
        if jobs:
            jobs.pop(0)()
    jobs += [unpack_gate, unpack_up, grad_inputs]
    for copy in swap_q:
        copy.wait()
    ring_q.step(0)
    for t in range(1, ring_q.steps):
        ring_q.step(t)
        if jobs:
            jobs.pop(0)()
    for job in jobs:
        job()
    ring_o.finish(m.grad_o)
    store("grad_o")
    ring_q.finish(m.got_q)
    m.grad_kv[...] = jnp.zeros_like(m.grad_kv)
    for i, kv in enumerate(kv_of):
        m.grad_q[:, i * q_width : (i + 1) * q_width] = m.got_q[i, :, :q_width]
        for k in (0, 1):
            first = q_width + k * HEAD_DIM
            m.grad_kv[k, :, kv * HEAD_DIM : (kv + 1) * HEAD_DIM] += m.got_q[
                i, :, first : first + HEAD_DIM
            ].astype(FULL)
    store("grad_q")
    store("grad_kv")
    for copy in stores:
        copy.wait()


LOADED = ("grad_h", "dy", "middle", "gains", "wo", "q", "o", "lse", "cos", "sin", "starts", "wq", "part_d", "x")


def back(n_dp, n_seq, own_ff, ff, kv_of, dtype, ins, shapes):
    tok, width = ins["x"].shape
    every = n_dp * tok
    q_width = ins["q"].shape[1]
    pair = 2 * HEAD_DIM
    length = n_seq * tok
    rank, columns = ins["wq"].shape[2:]
    outs = dict(
        out=shape_of((tok, width), dtype),
        grad_x=shape_of((tok, width), FULL),
        grad_o=shape_of((rank, width), FULL),
        grad_d=shape_of((ff, width), FULL),
        grad_q=shape_of(shapes["q"], LOW),
        grad_kv=shape_of((2,) + shapes["k"], FULL),
        grad_g=shape_of(shapes["gate"], LOW),
        grad_u=shape_of(shapes["gate"], LOW),
    )
    placed = {
        key + "_in" if key in LOADED else key: (
            value,
            ANY,
        )
        for key, value in ins.items()
    }
    scratch = {key: pltpu.VMEM(ins[key].shape, ins[key].dtype) for key in LOADED}
    scratch |= {key: pltpu.VMEM(value.shape, value.dtype) for key, value in outs.items()}
    scratch |= dict(
        store=dma(len(outs)),
        local=dma(4),
        load=dma(2 + len(LOADED)),
        got_q=vm(LOW, n_dp, rank, columns),
        down=DpScatter.scratch(n_dp, ff, width),
        kv_row=vm(LOW, 2, n_seq, tok, pair),
        dmid=vm(FULL, tok, width),
        d_own=vm(LOW, tok, width),
        d_all=vm(LOW, n_dp, tok, width),
        d_sem=DpGather.scratch(n_dp),
        do=vm(LOW, every, q_width),
        k2=vm(LOW, length, pair),
        v2=vm(LOW, length, pair),
        mask=vm(FULL, tok, length),
        dk2=vm(FULL, length, pair),
        dv2=vm(FULL, length, pair),
        dq=vm(FULL, every, q_width),
        dkv=vm(FULL, every, pair),
        dqkv=vm(LOW, every, columns),
        wide=vm(FULL, tok, width),
        landed_q=vm(LOW, n_dp, n_seq, rank, columns),
        part_kv=vm(LOW, n_seq, every, pair),
        part_q=vm(LOW, n_dp, n_seq, rank, columns),
        part_o=vm(LOW, n_seq, rank, width),
        back=DpScatter.scratch(n_dp, tok, width),
        ring_y=RingScatter.scratch(n_seq, tok, width),
        staged=RingScatter.staging(tok, width),
        ring_kv=RingScatter.scratch(n_seq, every, pair),
        ring_q=RingScatter.scratch(n_seq, n_dp, rank, columns),
        ring_o=RingScatter.scratch(n_seq, rank, width),
        swap_q=Exchange.scratch(n_dp),
        swap_gu=Exchange.scratch(n_seq),
        got_gu=vm(LOW, *ins["fin"].shape),
    )
    return run(
        functools.partial(back_kernel, n_dp, n_seq, own_ff, ff, kv_of),
        "attention_backward",
        3,
        placed,
        {key + "_to": (value, ANY) for key, value in outs.items()},
        scratch,
    )


def body(
    n_dp,
    n_seq,
    tokens,
    segment_ids,
    gain_attn,
    w_query,
    w_key,
    w_value,
    w_output,
    gain_mlp,
    w_gate,
    w_up,
    w_down,
    cotangent,
):
    local, width = tokens.shape[1], tokens.shape[2]
    length = n_seq * local
    own_rows = w_query.shape[0]
    own_ff = w_down.shape[0]
    ff = -(-own_ff // 16) * 16
    heads = HEADS // n_dp
    q_width = heads * HEAD_DIM
    x_own = tokens.reshape(local, width)
    dy_own = cotangent.reshape(local, width)

    kv_of = [i * heads // GROUP for i in range(n_dp)]
    got = front(
        n_dp,
        n_seq,
        own_ff,
        kv_of,
        dict(
            x=x_own,
            wg_in=w_gate,
            wu_in=w_up,
            wo=w_output,
            wd=jnp.pad(w_down, ((0, ff - own_ff), (0, 0))),
        ),
        dict(
            wq=w_query,
            wk=w_key,
            wv=w_value,
            gain_one=gain_attn.reshape(1, own_rows),
            gain_two=gain_mlp.reshape(1, own_rows),
            ids=segment_ids.reshape(1, local),
        ),
    )
    fed = feed(
        n_dp,
        n_seq,
        got["second"],
        dy_own,
        got["gu"].reshape(n_seq * own_rows, 2 * n_dp * ff),
        got["wd_all"],
    )
    ins = dict(
        part_y=fed["part_y"],
        grad_h=fed["grad_h_to"],
        fin=fed["fin_to"].reshape(got["gu"].shape),
        part_d=fed["grad_d"],
        x=x_own,
        dy=dy_own,
        middle=got["middle"],
    )
    for name in ("n1", "q", "kv", "o", "lse", "cos", "sin", "starts", "gains", "wq", "wo"):
        ins[name] = got[name + "_out"]
    done = back(
        n_dp,
        n_seq,
        own_ff,
        ff,
        kv_of,
        tokens.dtype,
        ins,
        dict(q=w_query.shape, k=w_key.shape, gate=w_gate.shape),
    )
    return finish(
        {key[: -len("_to")]: value for key, value in done.items()}
        | dict(
            gain_one=gain_attn.reshape(1, own_rows),
            gain_two=gain_mlp.reshape(1, own_rows),
            wq=w_query,
            wk=w_key,
            wv=w_value,
            wg=w_gate,
            wu=w_up,
        ),
        tokens.shape,
        own_ff,
    )


def finish_kernel(m):
    names = ("wg", "grad_g", "grad_x", "grad_d", "out", "grad_o", "wu", "grad_u", "wq", "grad_q")
    loads = {
        name: pltpu.make_async_copy(getattr(m, name), getattr(m, name + "_v"), m.load.at[k])
        for k, name in enumerate(names)
    }
    for copy in loads.values():
        copy.start()
    stores = []

    def store(src, dst):
        copy = pltpu.make_async_copy(src, dst, m.store.at[len(stores)])
        copy.start()
        stores.append(copy)

    def one(weight, raw, into):
        raw = raw[...].astype(FULL)
        into[...] = raw
        return jnp.sum(weight[...].astype(FULL) * raw, 1, keepdims=True)

    def whole(weight, raw, into, target):
        loads[weight].wait()
        loads[raw].wait()
        part = one(getattr(m, weight + "_v"), getattr(m, raw + "_v"), into)
        store(into, target)
        return part

    by_g = whole("wg", "grad_g", m.into_g, m.to_g)
    for name, target in (("grad_x", m.to_x), ("grad_d", m.to_d), ("out", m.to_out), ("grad_o", m.to_o)):
        loads[name].wait()
        store(getattr(m, name + "_v"), target)
    by_u = whole("wu", "grad_u", m.into_u, m.to_u)
    by_q = whole("wq", "grad_q", m.into_q, m.to_q)
    by_k = one(m.wk, m.grad_kv.at[0], m.to_k)
    by_v = one(m.wv, m.grad_kv.at[1], m.to_v)
    m.to_gain_one[...] = to_row(by_q + by_k + by_v) / m.gain_one[...].astype(FULL)
    m.to_gain_two[...] = to_row(by_g + by_u) / m.gain_two[...].astype(FULL)
    for copy in stores:
        copy.wait()


def finish(ins, shape, own_ff):
    rows = ins["wq"].shape[0]
    held = ("gain_one", "gain_two", "wk", "wv", "grad_kv")
    placed = {key: (value, VMEM if key in held else ANY) for key, value in ins.items()}
    outs = dict(
        to_out=(shape_of(ins["out"].shape, ins["out"].dtype), ANY),
        to_x=(shape_of(ins["grad_x"].shape, FULL), ANY),
        to_gain_one=(shape_of((1, rows), FULL), VMEM),
        to_q=(shape_of(ins["wq"].shape, FULL), ANY),
        to_k=(shape_of(ins["wk"].shape, FULL), VMEM),
        to_v=(shape_of(ins["wv"].shape, FULL), VMEM),
        to_o=(shape_of(ins["grad_o"].shape, FULL), ANY),
        to_gain_two=(shape_of((1, rows), FULL), VMEM),
        to_g=(shape_of(ins["wg"].shape, FULL), ANY),
        to_u=(shape_of(ins["wu"].shape, FULL), ANY),
        to_d=(shape_of(ins["grad_d"].shape, FULL), ANY),
    )
    scratch = dict(load=dma(10), store=dma(7))
    for name in ("g", "u", "q"):
        scratch["into_" + name] = vm(FULL, *ins["w" + name].shape)
    for key, value in ins.items():
        if key not in held:
            scratch[key + "_v"] = pltpu.VMEM(value.shape, value.dtype)
    done = run(finish_kernel, "finish", None, placed, outs, scratch)
    done = list(done.values())
    for k in (0, 1):
        done[k] = done[k].reshape(shape)
    for k in (2, 7):
        done[k] = done[k].reshape(rows)
    done[10] = done[10][:own_ff]
    return tuple(done)


def solution(mesh):
    rows = P(("dp", "seq"), None)
    vector = P(("dp", "seq"))
    row = P("dp", "seq", None)
    return jax.shard_map(
        functools.partial(body, mesh.shape["dp"], mesh.shape["seq"]),
        mesh=mesh,
        in_specs=(row, P("dp", "seq"), vector, rows, rows, rows, rows, vector, rows, rows, rows, row),
        out_specs=(row, row, vector, rows, rows, rows, rows, vector, rows, rows, rows),
        check_vma=False,
    )
```
